128 devices in a mesh: fsdp: 8 (over z, x_lo), seq: 16 (over x_hi, y, core).
Axes of the slice: x: 4 (x_hi: 2, x_lo: 2; x = x_hi * 2 + x_lo), y: 4, z: 4, core: 2. Of those that a mesh axis runs over, the one named last changes fastest.
Arguments:
- layer_input: bfloat16 [8, 2560, 1152], P('fsdp', 'seq'), may hold values from -6 to 6
- segment: int32 [8, 2560], P('fsdp'), may hold values from 0 to 12, as said below
- position: int32 [8, 2560], P('fsdp'), may hold values from 0 to 1759, as said below
- loss_token_mask: int32 [8, 2560], P('fsdp', 'seq'), may hold values from 0 to 1
- teacher: bfloat16 [8, 2560, 1152], P('fsdp', 'seq'), may hold values from -6 to 6
- attention_norm_gain: bfloat16 [1152], P(('fsdp', 'seq')), may hold values from -0.5 to 0.5
- query_weight: bfloat16 [1152, 1024], P(('fsdp', 'seq')), may hold values from -0.1875 to 0.1875
- key_weight: bfloat16 [1152, 256], P(('fsdp', 'seq')), may hold values from -0.1875 to 0.1875
- value_weight: bfloat16 [1152, 256], P(('fsdp', 'seq')), may hold values from -0.1875 to 0.1875
- output_weight: bfloat16 [1024, 1152], P(('fsdp', 'seq')), may hold values from -1.5 to 1.5
- adapter_query_first: bfloat16 [1152, 256], P(('fsdp', 'seq')), may hold values from -0.1875 to 0.1875
- adapter_query_second: bfloat16 [256, 1024], P(('fsdp', 'seq')), may hold values from -0.1875 to 0.1875
- adapter_key_first: bfloat16 [1152, 256], P(('fsdp', 'seq')), may hold values from -0.1875 to 0.1875
- adapter_key_second: bfloat16 [256, 256], P(('fsdp', 'seq')), may hold values from -0.1875 to 0.1875
- adapter_value_first: bfloat16 [1152, 256], P(('fsdp', 'seq')), may hold values from -0.1875 to 0.1875
- adapter_value_second: bfloat16 [256, 256], P(('fsdp', 'seq')), may hold values from -0.1875 to 0.1875
- adapter_output_first: bfloat16 [1024, 256], P(('fsdp', 'seq')), may hold values from -0.1875 to 0.1875
- adapter_output_second: bfloat16 [256, 1152], P(('fsdp', 'seq')), may hold values from -1.5 to 1.5
- feedforward_norm_gain: bfloat16 [1152], P(('fsdp', 'seq')), may hold values from -0.5 to 0.5
- gate_weight: bfloat16 [1152, 6912], P(('fsdp', 'seq')), may hold values from -0.1875 to 0.1875
- up_weight: bfloat16 [1152, 6912], P(('fsdp', 'seq')), may hold values from -0.1875 to 0.1875
- down_weight: bfloat16 [6912, 1152], P(('fsdp', 'seq')), may hold values from -0.078125 to 0.078125
- adapter_gate_first: bfloat16 [1152, 256], P(('fsdp', 'seq')), may hold values from -0.1875 to 0.1875
- adapter_gate_second: bfloat16 [256, 6912], P(('fsdp', 'seq')), may hold values from -0.1875 to 0.1875
- adapter_up_first: bfloat16 [1152, 256], P(('fsdp', 'seq')), may hold values from -0.1875 to 0.1875
- adapter_up_second: bfloat16 [256, 6912], P(('fsdp', 'seq')), may hold values from -0.1875 to 0.1875
- adapter_down_first: bfloat16 [6912, 256], P(('fsdp', 'seq')), may hold values from -0.078125 to 0.078125
- adapter_down_second: bfloat16 [256, 1152], P(('fsdp', 'seq')), may hold values from -0.1875 to 0.1875
Outputs:
- hidden_out: bfloat16 [8, 2560, 1152], P('fsdp', 'seq')
- loss_value: float32 [], replicated
- grad_hidden: bfloat16 [8, 2560, 1152], P('fsdp', 'seq')
- grad_gain_attention: float32 [1152], P(('fsdp', 'seq'))
- grad_w_query: float32 [1152, 1024], P(('fsdp', 'seq'))
- grad_w_key: float32 [1152, 256], P(('fsdp', 'seq'))
- grad_w_value: float32 [1152, 256], P(('fsdp', 'seq'))
- grad_w_output: float32 [1024, 1152], P(('fsdp', 'seq'))
- grad_lora_query_in: float32 [1152, 256], P(('fsdp', 'seq'))
- grad_lora_query_out: float32 [256, 1024], P(('fsdp', 'seq'))
- grad_lora_key_in: float32 [1152, 256], P(('fsdp', 'seq'))
- grad_lora_key_out: float32 [256, 256], P(('fsdp', 'seq'))
- grad_lora_value_in: float32 [1152, 256], P(('fsdp', 'seq'))
- grad_lora_value_out: float32 [256, 256], P(('fsdp', 'seq'))
- grad_lora_output_in: float32 [1024, 256], P(('fsdp', 'seq'))
- grad_lora_output_out: float32 [256, 1152], P(('fsdp', 'seq'))
- grad_gain_feedforward: float32 [1152], P(('fsdp', 'seq'))
- grad_w_gate: float32 [1152, 6912], P(('fsdp', 'seq'))
- grad_w_up: float32 [1152, 6912], P(('fsdp', 'seq'))
- grad_w_down: float32 [6912, 1152], P(('fsdp', 'seq'))
- grad_lora_gate_in: float32 [1152, 256], P(('fsdp', 'seq'))
- grad_lora_gate_out: float32 [256, 6912], P(('fsdp', 'seq'))
- grad_lora_up_in: float32 [1152, 256], P(('fsdp', 'seq'))
- grad_lora_up_out: float32 [256, 6912], P(('fsdp', 'seq'))
- grad_lora_down_in: float32 [6912, 256], P(('fsdp', 'seq'))
- grad_lora_down_out: float32 [256, 1152], P(('fsdp', 'seq'))
The draws below stay inside these ranges and needn't reach their ends.
Inputs may be any that keep to these rules, and one draw needn't show every extreme that they name: Within each tree the tokens run, in order: the trunk (segment 0), then for each branch b from 1 to 4 the branch b followed by its two leaves 3 + 2 b and 4 + 2 b. Every segment is a whole number of blocks of 80 tokens; the trunk has 16 to 20 of them. A token's position is its distance from the tree's root along its root-to-leaf path; the longest path of every tree has 1760 tokens.
All inputs are finite; a program needn't handle non-finite values.
Results may differ from the reference program's by a relative error of at most 0.015.
Values may be sent and summed in bfloat16 or wider, within the bound.
No kernel may reach another device: no remote copies, remote signals or barrier semaphores. Data moves between devices by JAX's collectives and lax.ppermute only.
A program may use at most 512 MiB of HBM per device.

```python
import math
import jax
import jax.numpy as jnp
import numpy as np
from jax import lax

MODEL_DIM = 1152
HEADS = 4
HEAD_WIDTH = 256
HIDDEN_UNITS = 6912
ADAPTER_RANK = 256
TREE_TOK = 2560
QUERY_HEADS_WIDTH = 1024
TREES = 8
TOKENS = 20480


dfs_order = np.array([0, 1, 5, 6, 2, 7, 8, 3, 9, 10, 4, 11, 12], dtype=np.int32)


parent_table = np.array([0, 0, 0, 0, 0, 1, 1, 2, 2, 3, 3, 4, 4], dtype=np.int32)


def tree_layout(key):
    unit_len = TREE_TOK // 32
    trunk_units = 16 + jax.random.randint(jax.random.fold_in(key, 11), (TREES,), 0, 5)
    chosen = jax.random.randint(jax.random.fold_in(key, 12), (TREES,), 1, 13)
    extra_units = 32 - 12 - trunk_units
    segment_ids = jnp.arange(13, dtype=jnp.int32)
    seg_units = 1 + extra_units[:, None] * (segment_ids[None, :] == chosen[:, None]).astype(jnp.int32)
    seg_units = jnp.where(segment_ids[None, :] == 0, trunk_units[:, None], seg_units)
    lengths = seg_units * unit_len
    ordered = lengths[:, jnp.asarray(dfs_order)]
    seg_ends = jnp.cumsum(ordered, axis=1)
    seg_starts = seg_ends - ordered
    token_ids = jnp.arange(TREE_TOK, dtype=jnp.int32)
    slot_index = jnp.sum((token_ids[None, :, None] >= seg_ends[:, None, :]).astype(jnp.int32), axis=2)
    slot_onehot = (slot_index[:, :, None] == segment_ids[None, None, :]).astype(jnp.int32)
    segment_out = jnp.sum(slot_onehot * jnp.asarray(dfs_order)[None, None, :], axis=2)
    offset = token_ids[None, :] - jnp.sum(slot_onehot * seg_starts[:, None, :], axis=2)
    trunk_len = lengths[:, 0:1]
    depth_seg = jnp.where(segment_ids[None, :] == 0, 0, jnp.where(segment_ids[None, :] <= 4, trunk_len, trunk_len + lengths[:, jnp.asarray(parent_table)]))
    seg_onehot = (segment_out[:, :, None] == segment_ids[None, None, :]).astype(jnp.int32)
    position_out = offset + jnp.sum(seg_onehot * depth_seg[:, None, :], axis=2)
    return (segment_out.astype(jnp.int32), position_out.astype(jnp.int32))


def draw_segment(key, part):
    return tree_layout(key)[0]


def draw_position(key, part):
    return tree_layout(key)[1]


def draw_loss_token_mask(key, part):
    all_tokens = TREES * TREE_TOK
    token_index = jnp.arange(all_tokens, dtype=jnp.int32).reshape(TREES, TREE_TOK)
    threshold = 250 + 500 * token_index // all_tokens
    drawn = jax.random.randint(key, (TREES, TREE_TOK), 0, 1000)
    return (drawn < threshold).astype(jnp.int32)


def steps_of(rng, dims, cuts, smallest, high):
    def one(dim, blocks):
        heights = jax.random.uniform(jax.random.fold_in(jax.random.fold_in(rng, 6), dim), (blocks,), jnp.float32, smallest / len(cuts), high / len(cuts))
        return jnp.repeat(jnp.exp(heights), dims[dim] // blocks).reshape((-1,) + (1,) * (len(dims) - dim - 1))

    level = one(*cuts[0])
    for cut in cuts[1:]:
        level = level * one(*cut)
    return level


def bell_draw(key, dims, scale, limit, shards=(), kind=jnp.bfloat16):
    entries = scale * jax.random.normal(key, dims, jnp.float32)
    if shards:
        entries = entries * steps_of(key, dims, shards, -0.22, 0.18)
    return jnp.clip(entries, -limit, limit).astype(kind)


def setup_inputs(seed: int = 0) -> dict:
    arg_keys = jax.random.split(jax.random.key(seed), 29)
    return {
        "layer_input": bell_draw(arg_keys[0], (TREES, TREE_TOK, MODEL_DIM), 1.0, 6.0, ((0, 8), (1, 16))),
        "segment": draw_segment(jax.random.fold_in(arg_keys[28], 71), 0),
        "position": draw_position(jax.random.fold_in(arg_keys[28], 71), 0),
        "loss_token_mask": draw_loss_token_mask(jax.random.fold_in(arg_keys[28], 71), 0),
        "teacher": bell_draw(arg_keys[4], (TREES, TREE_TOK, MODEL_DIM), 1.0, 6.0, ((0, 8), (1, 16))),
        "attention_norm_gain": jnp.clip(jax.random.uniform(arg_keys[5], (MODEL_DIM,), jnp.float32, -0.5, 0.5) * steps_of(arg_keys[5], (MODEL_DIM,), ((0, 128),), -0.4, 0.0), -0.5, 0.5).astype(jnp.bfloat16),
        "query_weight": bell_draw(arg_keys[6], (MODEL_DIM, QUERY_HEADS_WIDTH), MODEL_DIM ** -0.5, 0.1875, ((0, 128),)),
        "key_weight": bell_draw(arg_keys[7], (MODEL_DIM, HEAD_WIDTH), MODEL_DIM ** -0.5, 0.1875, ((0, 128),)),
        "value_weight": bell_draw(arg_keys[8], (MODEL_DIM, HEAD_WIDTH), MODEL_DIM ** -0.5, 0.1875, ((0, 128),)),
        "output_weight": bell_draw(arg_keys[9], (QUERY_HEADS_WIDTH, MODEL_DIM), (QUERY_HEADS_WIDTH // 64) ** -0.5, 1.5, ((0, 128),)),
        "adapter_query_first": bell_draw(arg_keys[10], (MODEL_DIM, ADAPTER_RANK), MODEL_DIM ** -0.5, 0.1875, ((0, 128),)),
        "adapter_query_second": bell_draw(arg_keys[11], (ADAPTER_RANK, QUERY_HEADS_WIDTH), (4 * ADAPTER_RANK) ** -0.5, 0.1875, ((0, 128),)),
        "adapter_key_first": bell_draw(arg_keys[12], (MODEL_DIM, ADAPTER_RANK), MODEL_DIM ** -0.5, 0.1875, ((0, 128),)),
        "adapter_key_second": bell_draw(arg_keys[13], (ADAPTER_RANK, HEAD_WIDTH), (4 * ADAPTER_RANK) ** -0.5, 0.1875, ((0, 128),)),
        "adapter_value_first": bell_draw(arg_keys[14], (MODEL_DIM, ADAPTER_RANK), MODEL_DIM ** -0.5, 0.1875, ((0, 128),)),
        "adapter_value_second": bell_draw(arg_keys[15], (ADAPTER_RANK, HEAD_WIDTH), (4 * ADAPTER_RANK) ** -0.5, 0.1875, ((0, 128),)),
        "adapter_output_first": bell_draw(arg_keys[16], (QUERY_HEADS_WIDTH, ADAPTER_RANK), QUERY_HEADS_WIDTH ** -0.5, 0.1875, ((0, 128),)),
        "adapter_output_second": bell_draw(arg_keys[17], (ADAPTER_RANK, MODEL_DIM), (ADAPTER_RANK // 16) ** -0.5, 1.5, ((0, 128),)),
        "feedforward_norm_gain": jnp.clip(jax.random.uniform(arg_keys[18], (MODEL_DIM,), jnp.float32, -0.5, 0.5) * steps_of(arg_keys[18], (MODEL_DIM,), ((0, 128),), -0.4, 0.0), -0.5, 0.5).astype(jnp.bfloat16),
        "gate_weight": bell_draw(arg_keys[19], (MODEL_DIM, HIDDEN_UNITS), MODEL_DIM ** -0.5, 0.1875, ((0, 128),)),
        "up_weight": bell_draw(arg_keys[20], (MODEL_DIM, HIDDEN_UNITS), MODEL_DIM ** -0.5, 0.1875, ((0, 128),)),
        "down_weight": bell_draw(arg_keys[21], (HIDDEN_UNITS, MODEL_DIM), HIDDEN_UNITS ** -0.5, 0.078125, ((0, 128),)),
        "adapter_gate_first": bell_draw(arg_keys[22], (MODEL_DIM, ADAPTER_RANK), MODEL_DIM ** -0.5, 0.1875, ((0, 128),)),
        "adapter_gate_second": bell_draw(arg_keys[23], (ADAPTER_RANK, HIDDEN_UNITS), (4 * ADAPTER_RANK) ** -0.5, 0.1875, ((0, 128),)),
        "adapter_up_first": bell_draw(arg_keys[24], (MODEL_DIM, ADAPTER_RANK), MODEL_DIM ** -0.5, 0.1875, ((0, 128),)),
        "adapter_up_second": bell_draw(arg_keys[25], (ADAPTER_RANK, HIDDEN_UNITS), (4 * ADAPTER_RANK) ** -0.5, 0.1875, ((0, 128),)),
        "adapter_down_first": bell_draw(arg_keys[26], (HIDDEN_UNITS, ADAPTER_RANK), HIDDEN_UNITS ** -0.5, 0.078125, ((0, 128),)),
        "adapter_down_second": bell_draw(arg_keys[27], (ADAPTER_RANK, MODEL_DIM), (4 * ADAPTER_RANK) ** -0.5, 0.1875, ((0, 128),)),
    }


EPSILON = 1e-06
ROPE_BASE = 10000.0
MASKED_SCORE = -1e+30
HIGHEST = lax.Precision.HIGHEST

@jax.custom_vjp
def low(v):
    return lax.optimization_barrier(v.astype(jnp.bfloat16)).astype(jnp.float32)

@jax.custom_vjp
def rank_backward(v):
    return v

def low_keep(v):
    return (low(v), None)

def low_pass(kept, grad):
    return (grad,)

def back_keep(v):
    return (v, None)

def back_low(kept, grad):
    return (low(grad),)
low.defvjp(low_keep, low_pass)
rank_backward.defvjp(back_keep, back_low)

def rounded_result(values):
    return rank_backward(low(values))

def matrix_product(left_side, right_side):
    return jnp.dot(left_side, right_side, precision=HIGHEST)

def ancestor_mask(query_seg, key_seg, query_pos, key_pos):
    q_column = query_seg[:, None]
    k_row = key_seg[None, :]
    parent_branch = (k_row >= 1) & (k_row <= 4) & (q_column >= 5) & ((q_column - 5) // 2 + 1 == k_row)
    related = (k_row == q_column) | (k_row == 0) | parent_branch
    return related & (key_pos[None, :] <= query_pos[:, None])

def rope_tables(tree_pos, head_size):
    half_size = head_size // 2
    frequency = ROPE_BASE ** (-(jnp.arange(half_size, dtype=jnp.float32) * 2.0 / head_size))
    angles = tree_pos.astype(jnp.float32)[:, None] * frequency[None, :]
    return (jnp.cos(angles), jnp.sin(angles))

def rotate(values, cos_table, sin_table):
    half_size = values.shape[-1] // 2
    first_half = values[..., :half_size]
    second_half = values[..., half_size:]
    cos_part = cos_table[:, None, :]
    sin_part = sin_table[:, None, :]
    return jnp.concatenate([first_half * cos_part - second_half * sin_part, second_half * cos_part + first_half * sin_part], axis=-1)

def norm_scale(values, gain_vector):
    return values * lax.rsqrt(lax.optimization_barrier(jnp.mean(values * values, axis=-1, keepdims=True)) + EPSILON) * (1.0 + gain_vector)

def adapter_projection(input_rows, frozen_weight, adapter_first_factor, adapter_second_factor):
    rank_row_block = rounded_result(matrix_product(input_rows, adapter_first_factor))
    return matrix_product(input_rows, frozen_weight) + matrix_product(rank_row_block, adapter_second_factor)

def gated_gelu(gate_logits, up_logits):
    return jax.nn.gelu(gate_logits, approximate=True) * up_logits

def tree_forward(hidden, weights, tree_seg, tree_pos, cos_table, sin_table):
    gain_att, query_matrix, key_matrix, value_matrix, output_matrix, query_first_factor, query_second_factor, key_first_factor, key_second_factor, value_first_factor, value_second_factor, output_first_factor, output_second_factor, gain_ff, gate_matrix, up_matrix, down_matrix, gate_first_factor, gate_second_factor, up_first_factor, up_second_factor, down_first_factor, down_second_factor = weights
    tokens_n = hidden.shape[0]
    attention_normed = low(norm_scale(hidden, gain_att))
    unrotated_queries = rank_backward(adapter_projection(attention_normed, query_matrix, query_first_factor, query_second_factor))
    unrotated_keys = rank_backward(adapter_projection(attention_normed, key_matrix, key_first_factor, key_second_factor))
    every_value_row = rounded_result(adapter_projection(attention_normed, value_matrix, value_first_factor, value_second_factor))
    queries_rot = low(rotate(unrotated_queries.reshape(tokens_n, HEADS, HEAD_WIDTH), cos_table, sin_table))
    keys_rot = low(rotate(unrotated_keys[:, None, :], cos_table, sin_table)[:, 0, :])
    block_size = math.gcd(tokens_n, 128)
    score_scale = HEAD_WIDTH ** (-0.5)

    def attend(block_index):
        first_row = block_index * block_size
        query_rows = lax.dynamic_slice_in_dim(queries_rot, first_row, block_size, 0)
        query_seg = lax.dynamic_slice_in_dim(tree_seg, first_row, block_size, 0)
        query_pos = lax.dynamic_slice_in_dim(tree_pos, first_row, block_size, 0)
        scores = rank_backward(jnp.einsum('thd,kd->thk', query_rows, keys_rot, precision=HIGHEST) * score_scale)
        allowed = ancestor_mask(query_seg, tree_seg, query_pos, tree_pos)[:, None, :]
        weights_soft = jax.nn.softmax(jnp.where(allowed, scores, MASKED_SCORE), axis=-1)
        return jnp.einsum('thk,kd->thd', low(weights_soft), every_value_row, precision=HIGHEST)
    attention_mix = lax.map(jax.checkpoint(attend), jnp.arange(tokens_n // block_size, dtype=jnp.int32))
    attention_mix = rounded_result(attention_mix.reshape(tokens_n, HEADS * HEAD_WIDTH))
    attention_result = rank_backward(adapter_projection(attention_mix, output_matrix, output_first_factor, output_second_factor))
    after_attention = hidden + attention_result
    feedforward_normed = low(norm_scale(after_attention, gain_ff))
    gate_logits = rank_backward(adapter_projection(feedforward_normed, gate_matrix, gate_first_factor, gate_second_factor))
    up_logits = rank_backward(adapter_projection(feedforward_normed, up_matrix, up_first_factor, up_second_factor))
    gated_hidden = rounded_result(gated_gelu(gate_logits, up_logits))
    feedforward_result = rank_backward(adapter_projection(gated_hidden, down_matrix, down_first_factor, down_second_factor))
    return after_attention + feedforward_result

def reference(layer_input, segment, position, loss_token_mask, teacher, attention_norm_gain, query_weight, key_weight, value_weight, output_weight, adapter_query_first, adapter_query_second, adapter_key_first, adapter_key_second, adapter_value_first, adapter_value_second, adapter_output_first, adapter_output_second, feedforward_norm_gain, gate_weight, up_weight, down_weight, adapter_gate_first, adapter_gate_second, adapter_up_first, adapter_up_second, adapter_down_first, adapter_down_second):
    parameters = tuple((weight_matrix.astype(jnp.float32) for weight_matrix in (attention_norm_gain, query_weight, key_weight, value_weight, output_weight, adapter_query_first, adapter_query_second, adapter_key_first, adapter_key_second, adapter_value_first, adapter_value_second, adapter_output_first, adapter_output_second, feedforward_norm_gain, gate_weight, up_weight, down_weight, adapter_gate_first, adapter_gate_second, adapter_up_first, adapter_up_second, adapter_down_first, adapter_down_second)))
    valid_count = jnp.sum(loss_token_mask).astype(jnp.float32)
    grad_scale = TOKENS / valid_count

    def one_tree(running, input_rows):
        hidden, tree_seg, tree_pos, tree_valid, tree_teacher = input_rows
        cos_table, sin_table = rope_tables(tree_pos, HEAD_WIDTH)

        def objective(hidden_f, weights):
            result = tree_forward(hidden_f, weights, tree_seg, tree_pos, cos_table, sin_table)
            error_rows = result - tree_teacher.astype(jnp.float32)
            valid_rows = tree_valid.astype(jnp.float32)[:, None]
            return (jnp.sum(valid_rows * error_rows * error_rows), result)
        numerator, pullback, result = jax.vjp(objective, hidden.astype(jnp.float32), parameters, has_aux=True)
        grad_input, grad_params = pullback(grad_scale)
        grad_sums, loss_sum = running
        grad_sums = jax.tree.map(jnp.add, grad_sums, grad_params)
        return ((grad_sums, loss_sum + numerator), (result.astype(jnp.bfloat16), grad_input.astype(jnp.bfloat16)))
    initial = (jax.tree.map(jnp.zeros_like, parameters), jnp.zeros((), jnp.float32))
    (grad_sums, loss_sum), (outputs, gradient_input_rows) = lax.scan(one_tree, initial, (layer_input, segment, position, loss_token_mask, teacher))
    loss_value = loss_sum / (MODEL_DIM * valid_count)
    return (outputs, loss_value, gradient_input_rows, grad_sums[0], grad_sums[1], grad_sums[2], grad_sums[3], grad_sums[4], grad_sums[5], grad_sums[6], grad_sums[7], grad_sums[8], grad_sums[9], grad_sums[10], grad_sums[11], grad_sums[12], grad_sums[13], grad_sums[14], grad_sums[15], grad_sums[16], grad_sums[17], grad_sums[18], grad_sums[19], grad_sums[20], grad_sums[21], grad_sums[22])
```

```python
import jax
import jax.numpy as jnp
import numpy as np
from jax import lax
from jax.sharding import Mesh, PartitionSpec as P

EPSILON = 1e-06
ROPE_BASE = 10000.0
MASKED_SCORE = -1e30
BF = jnp.bfloat16
F32 = jnp.float32

OUTER = ("z", "xl", "xh")
CHIPS = ("z", "xl", "xh", "y")
EVERY = ("z", "xl", "xh", "y", "c")
SIZES = dict(z=4, xl=2, xh=2, y=4, c=2)


def dot(a, b):
    return jnp.dot(a, b, preferred_element_type=F32)


def dot_tl(a, b):
    return lax.dot_general(a, b, (((0,), (0,)), ((), ())), preferred_element_type=F32)


def dot_tr(a, b):
    return lax.dot_general(a, b, (((1,), (1,)), ((), ())), preferred_element_type=F32)


def count_of(axes):
    return int(np.prod([SIZES[a] for a in axes]))


def exchange(x, axes):
    return lax.all_to_all(x, axes, split_axis=0, concat_axis=0, tiled=True)


def gather(x, axes):
    return exchange(jnp.broadcast_to(x[None], (count_of(axes),) + x.shape), axes)


def scatter_sum(x, axes):
    return jnp.sum(exchange(x, axes).astype(F32), axis=0)


def other_core(x):
    return lax.ppermute(x, "c", [(0, 1), (1, 0)])


def ordered(core, mine, other):
    return jnp.where(core == 0, jnp.stack([mine, other]), jnp.stack([other, mine]))


def swap_halves(core, pieces):
    keep = jnp.where(core == 0, pieces[0], pieces[1])
    send = jnp.where(core == 0, pieces[1], pieces[0])
    return ordered(core, keep, other_core(send))


def down_route():
    pairs = []
    for o in range(16):
        for t in range(8):
            pairs.append((8 * o + t, 8 * (8 * (o % 2) + t) + o // 2))
    return pairs


def norm_parts(values, gain):
    scale = lax.rsqrt(jnp.mean(values * values, axis=-1, keepdims=True) + EPSILON)
    n = values * scale
    return scale, n, (n * (1.0 + gain)).astype(BF)


def norm_back(scale, n, gain, grad):
    m = grad * (1.0 + gain)
    back = scale * (m - n * jnp.mean(m * n, axis=-1, keepdims=True))
    return back, jnp.sum(grad * n, axis=0)


def turn(x, cos, sin):
    h = cos.shape[-1]
    a, b = x[:, :h], x[:, h:]
    return jnp.concatenate([a * cos - b * sin, b * cos + a * sin], axis=-1)


def turn_back(x, cos, sin):
    return turn(x, cos, -sin)


def gather_tokens(x):
    mine = gather(x, ("y",)).reshape(-1, x.shape[1])
    return jnp.concatenate([mine, other_core(mine)], axis=0)


def scatter_tokens(mine_part, other_part):
    summed = mine_part + other_core(other_part.astype(BF)).astype(F32)
    rows = summed.shape[0] // 4
    return scatter_sum(summed.astype(BF).reshape(4, rows, -1), ("y",))


def on_device(
    layer_input,
    segment,
    position,
    loss_token_mask,
    teacher,
    gain_one,
    wq,
    wk,
    wv,
    wo,
    aq,
    bq,
    ak,
    bk,
    av,
    bv,
    ao,
    bo,
    gain_two,
    wg,
    wu,
    wd,
    ag,
    bg,
    au,
    bu,
    ad,
    bd,
):
    core = lax.axis_index("c")
    tokens = 160
    heads = 4
    width = 256
    score_scale = width**-0.5
    hidden = layer_input[0].astype(F32)
    count_here = jnp.sum(loss_token_mask[0]).astype(BF)

    p9 = jnp.concatenate([wq, wk, wv, aq, ak, av], axis=1)
    p2 = jnp.concatenate([bq, bk, bv, bo], axis=1)

    def att_piece(k):
        rest = p2[:, 1344 * k + 1152 : 1344 * k + 1344].reshape(1, 384)
        last = jnp.concatenate(
            [rest, gain_one[None], gain_two[None], count_here.reshape(1, 1), jnp.zeros((1, 749), BF)],
            axis=1,
        )
        return jnp.concatenate(
            [p9[:, 1152 * k : 1152 * (k + 1)], p2[:, 1344 * k : 1344 * k + 1152], last], axis=0
        )

    att_own = swap_halves(core, [att_piece(0), att_piece(1)]).reshape(24, 1152)
    att_mine = gather(att_own, CHIPS)
    att_both = ordered(core, att_mine, other_core(att_mine)).reshape(2, 128, 12, 1152)
    w9 = att_both[:, :, :9].reshape(2, 1152, 1152)
    w2 = att_both[:, :, 9:11].reshape(2, 256, 1152)
    w2_rest = att_both[:, :, 11, :384].reshape(2, 256, 192)
    gain_one_full = att_both[0, :, 11, 384:393].reshape(1, 1152).astype(F32)
    gain_two_full = att_both[0, :, 11, 393:402].reshape(1, 1152).astype(F32)
    valid_count = jnp.sum(att_both[0, :, 11, 402].astype(F32))
    full9 = jnp.concatenate([w9[0], w9[1]], axis=1)
    full2 = jnp.concatenate([w2[0], w2_rest[0], w2[1], w2_rest[1]], axis=1)
    bq_full, bk_full, bv_full, bo_full = (
        full2[:, :1024],
        full2[:, 1024:1280],
        full2[:, 1280:1536],
        full2[:, 1536:],
    )
    aq_full, ak_full, av_full = full9[:, 1536:1792], full9[:, 1792:2048], full9[:, 2048:]
    w_qkv = jnp.concatenate(
        [
            full9[:, :1024].astype(F32) + dot(aq_full, bq_full),
            full9[:, 1024:1280].astype(F32) + dot(ak_full, bk_full),
            full9[:, 1280:1536].astype(F32) + dot(av_full, bv_full),
        ],
        axis=1,
    ).astype(BF)

    p8 = jnp.concatenate([wo, ao], axis=1)
    out_own = swap_halves(core, [p8[:, :768], p8[:, 640:]]).reshape(16, 768)
    out_mine = gather(out_own, CHIPS)
    out_both = ordered(core, out_mine, other_core(out_mine)).reshape(2, 1024, 768)
    full8 = jnp.concatenate([out_both[0], out_both[1][:, 128:]], axis=1)
    ao_full = full8[:, 1152:]
    w_out = (full8[:, :1152].astype(F32) + dot(ao_full, bo_full)).astype(BF)

    ff_piece = [
        jnp.concatenate([m, bd[:, 512 * k : 512 * k + 640].reshape(5, 256)], axis=0)
        for k, m in enumerate((ag, au))
    ]
    ff_own = swap_halves(core, ff_piece).reshape(28, 256)
    ff_mine = gather(ff_own, CHIPS)
    ff_both = ordered(core, ff_mine, other_core(ff_mine)).reshape(2, 128, 14, 256)
    ag_full, au_full = ff_both[0, :, :9].reshape(1152, 256), ff_both[1, :, :9].reshape(1152, 256)
    bd_halves = ff_both[:, :, 9:].reshape(2, 256, 640)
    bd_full = jnp.concatenate([bd_halves[0], bd_halves[1][:, 128:]], axis=1)

    rows22 = jnp.concatenate([wg, wu, bg, bu], axis=0)
    rows22 = exchange(rows22.reshape(22, 8, 864).transpose(1, 0, 2), ("y", "c"))
    gu_own = jnp.concatenate(
        [
            rows22[:, :9].reshape(72, 864),
            rows22[:, 9:18].reshape(72, 864),
            rows22[:, 18:20].reshape(16, 864),
            rows22[:, 20:].reshape(16, 864),
        ],
        axis=0,
    )
    gu = gather(gu_own, OUTER)
    bg_cols, bu_cols = gu[:, 144:160].reshape(256, 864), gu[:, 160:].reshape(256, 864)
    w_gate = (gu[:, :72].reshape(1152, 864).astype(F32) + dot(ag_full, bg_cols)).astype(BF)
    w_up = (gu[:, 72:144].reshape(1152, 864).astype(F32) + dot(au_full, bu_cols)).astype(BF)
    down_own = lax.ppermute(jnp.concatenate([wd, ad], axis=1), EVERY, down_route())
    down = gather(down_own, OUTER).reshape(864, 1408)
    ad_rows = down[:, 1152:]
    w_down = (down[:, :1152].astype(F32) + dot(ad_rows, bd_full)).astype(BF)

    seq = (lax.axis_index("xh") * 4 + lax.axis_index("y")) * 2 + core
    tree_seg = segment[0]
    tree_pos = position[0]
    own_seg = lax.dynamic_slice_in_dim(tree_seg, seq * tokens, tokens)
    own_pos = lax.dynamic_slice_in_dim(tree_pos, seq * tokens, tokens)
    freq = ROPE_BASE ** (-(jnp.arange(128, dtype=F32) * 2.0 / width))
    angles = own_pos.astype(F32)[:, None] * freq[None, :]
    cos, sin = jnp.cos(angles), jnp.sin(angles)

    def by_core(v):
        v = v.reshape(8, 2, tokens)
        first = jnp.where(core == 0, v[:, 0], v[:, 1]).reshape(-1)
        second = jnp.where(core == 0, v[:, 1], v[:, 0]).reshape(-1)
        return jnp.concatenate([first, second])

    key_seg, key_pos = by_core(tree_seg)[None, :], by_core(tree_pos)[None, :]
    q_seg, q_pos = own_seg[:, None], own_pos[:, None]
    parent = (key_seg >= 1) & (key_seg <= 4) & (q_seg >= 5) & ((q_seg - 5) // 2 + 1 == key_seg)
    allowed = ((key_seg == q_seg) | (key_seg == 0) | parent) & (key_pos <= q_pos)
    allowed = jnp.concatenate([allowed] * heads, axis=0)

    scale_one, n_one, u_one = norm_parts(hidden, gain_one_full)
    qkv = dot(u_one, w_qkv)
    kv_own = jnp.concatenate([turn(qkv[:, 1024:1280], cos, sin), qkv[:, 1280:]], axis=1).astype(BF)
    kv_mine = gather(kv_own, ("xh", "y")).reshape(8 * tokens, 512)
    kv = jnp.concatenate([kv_mine, other_core(kv_mine)], axis=0)
    keys, values = kv[:, :256], kv[:, 256:]
    q_rows = jnp.concatenate(
        [turn(qkv[:, width * h : width * (h + 1)], cos, sin) for h in range(heads)], axis=0
    ).astype(BF)
    scores = jnp.where(allowed, dot_tr(q_rows, keys) * score_scale, MASKED_SCORE)
    top = jnp.max(scores, axis=-1, keepdims=True)
    ex = jnp.exp(scores - top)
    total = jnp.sum(ex, axis=-1, keepdims=True)
    lse = top + jnp.log(total)
    mix_rows = dot((ex / total).astype(BF), values).astype(BF)
    mix = jnp.concatenate([mix_rows[tokens * h : tokens * (h + 1)] for h in range(heads)], axis=1)
    after = hidden + dot(mix, w_out)

    scale_two, n_two, u_two = norm_parts(after, gain_two_full)
    u_all = gather_tokens(u_two)
    gate = dot(u_all, w_gate)
    up = dot(u_all, w_up)
    act, act_pull = jax.vjp(lambda g, u: jax.nn.gelu(g, approximate=True) * u, gate, up)
    act = act.astype(BF)
    out_part = dot(act, w_down)
    half = 4 * tokens
    result = after + scatter_tokens(out_part[:half], out_part[half:])

    valid = loss_token_mask[0].astype(F32)[:, None]
    error = result - teacher[0].astype(F32)
    loss_here = jnp.sum(valid * error * error)
    loss_all = exchange(jnp.broadcast_to(loss_here, (128, 128)), EVERY)
    loss_value = jnp.sum(loss_all[:, 0]) / (1152.0 * valid_count)
    grad_result = 2.0 * 20480.0 / valid_count * valid * error

    g_all = gather_tokens(grad_result.astype(BF))
    gw_down = dot_tl(act, g_all).astype(BF)
    g_act = dot_tr(g_all, w_down).astype(BF)
    g_gate, g_up = act_pull(g_act.astype(F32))
    g_gate, g_up = g_gate.astype(BF), g_up.astype(BF)
    g_u_part = dot_tr(g_gate, w_gate) + dot_tr(g_up, w_up)
    g_u_two = scatter_tokens(g_u_part[:half], g_u_part[half:])
    gw_gate = dot_tl(u_all, g_gate).astype(BF)
    gw_up = dot_tl(u_all, g_up).astype(BF)
    gb_gate = dot_tl(ag_full, gw_gate).astype(BF)
    gb_up = dot_tl(au_full, gw_up).astype(BF)
    gb_down = dot_tl(ad_rows, gw_down).astype(BF)
    gu_sum = scatter_sum(
        jnp.concatenate(
            [
                gw_gate.reshape(16, 72, 864),
                gw_up.reshape(16, 72, 864),
                gb_gate.reshape(16, 16, 864),
                gb_up.reshape(16, 16, 864),
            ],
            axis=1,
        ),
        OUTER,
    ).astype(BF)
    down_sum = scatter_sum(gw_down.reshape(16, 54, 1152), OUTER)
    ga_part = jnp.concatenate(
        [dot_tr(gu_sum[:72], bg_cols), dot_tr(gu_sum[72:144], bu_cols), jnp.zeros((72, 352), F32)],
        axis=1,
    ).astype(BF)
    back_t = exchange(
        jnp.concatenate(
            [
                gu_sum[:72].reshape(8, 9, 864),
                gu_sum[72:144].reshape(8, 9, 864),
                gu_sum[144:160].reshape(8, 2, 864),
                gu_sum[160:].reshape(8, 2, 864),
                ga_part.reshape(8, 9, 864),
            ],
            axis=1,
        ),
        ("y", "c"),
    )
    wide = back_t[:, :22].transpose(1, 0, 2).reshape(22, 6912).astype(F32)
    ga = jnp.sum(back_t[:, 22:, :512].astype(F32), axis=0)
    gw_down_own = lax.ppermute(down_sum.astype(BF), EVERY, [(b, a) for a, b in down_route()])
    ga_down_own = dot_tr(gw_down_own, bd_full)

    norm_two_back, g_gain_two = norm_back(scale_two, n_two, gain_two_full, g_u_two)
    g_after = grad_result + norm_two_back
    g_after_b = g_after.astype(BF)
    gw_out = dot_tl(mix, g_after_b).astype(BF)
    gb_out = dot_tl(ao_full, gw_out).astype(BF)

    def to_owners(parts, columns, starts):
        stacked = jnp.concatenate([p.reshape(64, p.shape[0] // 64, p.shape[1]) for p in parts], axis=1)
        first = stacked[:, :, starts[0] : starts[0] + columns]
        second = stacked[:, :, starts[1] : starts[1] + columns]
        keep = jnp.where(core == 0, first, second)
        send = jnp.where(core == 0, second, first)
        summed = (keep.astype(F32) + other_core(send).astype(F32)).astype(BF)
        total_rows = scatter_sum(summed, CHIPS).astype(BF)
        mine, away, at = [], [], 0
        for p in parts:
            r = p.shape[0] // 128
            block = total_rows[at : at + 2 * r]
            mine.append(jnp.where(core == 0, block[:r], block[r:]))
            away.append(jnp.where(core == 0, block[r:], block[:r]))
            at += 2 * r
        mine, away = jnp.concatenate(mine, axis=0), jnp.concatenate(away, axis=0)
        both = ordered(core, mine, other_core(away))
        skip = starts[0] + columns - starts[1]
        joined = jnp.concatenate([both[0], both[1][:, skip:]], axis=1)
        outs, at = [], 0
        for p in parts:
            r = p.shape[0] // 128
            outs.append(joined[at : at + r])
            at += r
        return outs

    gw_out_own, gb_out_own, gb_down_own = to_owners([gw_out, gb_out, gb_down], 640, (0, 512))
    ga_out_own = dot_tr(gw_out_own, bo_full)

    g_mix = dot_tr(g_after_b, w_out).astype(BF)
    g_rows = jnp.concatenate([g_mix[:, width * h : width * (h + 1)] for h in range(heads)], axis=0)
    scores_again = jnp.where(allowed, dot_tr(q_rows, keys) * score_scale, MASKED_SCORE)
    probs = jnp.where(allowed, jnp.exp(scores_again - lse), 0.0)
    g_probs = dot_tr(g_rows, values)
    g_scores = (probs * (g_probs - jnp.sum(probs * g_probs, axis=-1, keepdims=True))).astype(BF)
    g_q_rows = dot(g_scores, keys) * score_scale
    g_keys = dot_tl(g_scores, q_rows) * score_scale
    g_values = dot_tl(probs.astype(BF), g_rows)
    g_kv = jnp.concatenate([g_keys, g_values], axis=1)
    n_mine = 8 * tokens
    g_kv_sum = g_kv[:n_mine] + other_core(g_kv[n_mine:].astype(BF)).astype(F32)
    g_kv_own = scatter_sum(g_kv_sum.astype(BF).reshape(8, tokens, 512), ("xh", "y"))
    g_qkv = jnp.concatenate(
        [turn_back(g_q_rows[tokens * h : tokens * (h + 1)], cos, sin) for h in range(heads)]
        + [turn_back(g_kv_own[:, :256], cos, sin), g_kv_own[:, 256:]],
        axis=1,
    ).astype(BF)
    g_u_one = dot_tr(g_qkv, w_qkv)
    norm_one_back, g_gain_one = norm_back(scale_one, n_one, gain_one_full, g_u_one)
    grad_hidden = (g_after + norm_one_back).astype(BF)

    gw_qkv = dot_tl(u_one, g_qkv).astype(BF)
    gb_qkv = jnp.concatenate(
        [
            dot_tl(aq_full, gw_qkv[:, :1024]),
            dot_tl(ak_full, gw_qkv[:, 1024:1280]),
            dot_tl(av_full, gw_qkv[:, 1280:]),
        ],
        axis=1,
    ).astype(BF)
    gains = jnp.concatenate([g_gain_one.reshape(128, 1, 9), g_gain_two.reshape(128, 1, 9)], axis=2)
    gains = gains.reshape(64, 1, 36).astype(BF)
    gains_row = jnp.concatenate([gains, jnp.zeros((64, 1, 768 - 36), BF)], axis=2)
    gains_rows = jnp.concatenate([gains_row, gains_row], axis=2)

    stacked = jnp.concatenate(
        [gw_qkv.reshape(64, 18, 1536), gb_qkv.reshape(64, 4, 1536), gains_rows], axis=1
    )
    keep = jnp.where(core == 0, stacked[:, :, :768], stacked[:, :, 768:])
    send = jnp.where(core == 0, stacked[:, :, 768:], stacked[:, :, :768])
    summed = (keep.astype(F32) + other_core(send).astype(F32)).astype(BF)
    owned = scatter_sum(summed, CHIPS)
    mine = jnp.where(
        core == 0,
        jnp.concatenate([owned[:9], owned[18:20]], axis=0),
        jnp.concatenate([owned[9:18], owned[20:22]], axis=0),
    )
    away = jnp.where(
        core == 0,
        jnp.concatenate([owned[9:18], owned[20:22]], axis=0),
        jnp.concatenate([owned[:9], owned[18:20]], axis=0),
    )
    both = ordered(core, mine, other_core(away))
    gw_own = jnp.concatenate([both[0], both[1]], axis=1)
    gain_pair = jnp.where(core == 0, owned[22, :18], owned[22, 18:36])
    gw_own_b = gw_own[:9].astype(BF)

    return (
        result.astype(BF)[None],
        loss_value,
        grad_hidden[None],
        gain_pair[:9],
        gw_own[:9, :1024],
        gw_own[:9, 1024:1280],
        gw_own[:9, 1280:],
        gw_out_own.astype(F32),
        dot_tr(gw_own_b[:, :1024], bq_full),
        gw_own[9:, :1024],
        dot_tr(gw_own_b[:, 1024:1280], bk_full),
        gw_own[9:, 1024:1280],
        dot_tr(gw_own_b[:, 1280:], bv_full),
        gw_own[9:, 1280:],
        ga_out_own,
        gb_out_own.astype(F32),
        gain_pair[9:],
        wide[:9],
        wide[9:18],
        gw_down_own.astype(F32),
        ga[:, :256],
        wide[18:20],
        ga[:, 256:],
        wide[20:],
        ga_down_own,
        gb_down_own.astype(F32),
    )


def solution(mesh):
    mesh = Mesh(mesh.devices.reshape([SIZES[a] for a in EVERY]), EVERY)
    tree, seq = ("z", "xl"), ("xh", "y", "c")
    rows = P(EVERY, None)
    vector = P(EVERY)
    return jax.shard_map(
        on_device,
        mesh=mesh,
        in_specs=(
            P(tree, seq, None),
            P(tree, None),
            P(tree, None),
            P(tree, seq),
            P(tree, seq, None),
            vector,
        )
        + (rows,) * 12
        + (vector,)
        + (rows,) * 9,
        out_specs=(P(tree, seq, None), P(), P(tree, seq, None), vector)
        + (rows,) * 12
        + (vector,)
        + (rows,) * 9,
        check_vma=False,
    )
```

```python
import jax
import jax.numpy as jnp
from jax import lax
from jax.sharding import Mesh, PartitionSpec as P

EPSILON = 1e-06
ROPE_BASE = 10000.0
MASKED_SCORE = -1e30
BF = jnp.bfloat16
F32 = jnp.float32

CHIPS = ("z", "xl", "xh", "y")
EVERY = ("z", "xl", "xh", "y", "c")
SIZES = dict(z=4, xl=2, xh=2, y=4, c=2)
RING = dict(z="z", x=("xl", "xh"), y="y")
TOKENS = 160
HEADS = 4
WIDTH = 256


def dot(a, b):
    return jnp.dot(a, b, preferred_element_type=F32)


def dot_tl(a, b):
    return lax.dot_general(a, b, (((0,), (0,)), ((), ())), preferred_element_type=F32)


def dot_tr(a, b):
    return lax.dot_general(a, b, (((1,), (1,)), ((), ())), preferred_element_type=F32)


def exchange(x, axes):
    return lax.all_to_all(x, axes, split_axis=0, concat_axis=0, tiled=True)


def gather_chips(x):
    return exchange(jnp.broadcast_to(x[None], (64,) + x.shape), CHIPS)


def other_core(x):
    return lax.ppermute(x, "c", [(0, 1), (1, 0)])


def shift(x, axis, k):
    number = [0, 2, 1, 3] if axis == "x" else [0, 1, 2, 3]
    return lax.ppermute(x, RING[axis], [(number[i], number[(i + k) % 4]) for i in range(4)])


def pick(cond, a, b):
    return jnp.where(cond, a, b), jnp.where(cond, b, a)


def split_in_two(x):
    high = x.astype(BF)
    return high, (x - high.astype(F32)).astype(BF)


def select_back(x, table):
    high, low = split_in_two(x)
    return dot_tr(high, table) + dot_tr(low, table)


def down_route():
    pairs = []
    for o in range(16):
        for t in range(8):
            pairs.append((8 * o + t, 8 * (8 * (o % 2) + t) + o // 2))
    return pairs


def gather_zx(x, first):
    second = "z" if first == "x" else "x"
    line = jnp.stack([x] + [shift(x, first, k) for k in (1, 2, 3)])
    lines = [line] + [shift(line, second, k) for k in (1, 2, 3)]
    return jnp.stack(lines, axis=0 if first == "x" else 1)


def scatter_zx(x, first):
    second = "z" if first == "x" else "x"
    x = [x[k] if first == "z" else x[:, k] for k in range(4)]
    line = x[0].astype(F32)
    for k in (1, 2, 3):
        line = line + shift(x[k], first, 4 - k).astype(F32)
    line = line.astype(BF)
    out = line[0].astype(F32)
    for k in (1, 2, 3):
        out = out + shift(line[k], second, 4 - k).astype(F32)
    return out


def norm_parts(values, gain):
    scale = lax.rsqrt(jnp.mean(values * values, axis=-1, keepdims=True) + EPSILON)
    n = values * scale
    return scale, n, (n * (1.0 + gain)).astype(BF)


def norm_back(scale, n, gain, grad):
    m = grad * (1.0 + gain)
    back = scale * (m - n * jnp.mean(m * n, axis=-1, keepdims=True))
    return back, jnp.sum(grad * n, axis=0, keepdims=True)


def turn(x, cos, sin):
    h = cos.shape[-1]
    a, b = x[:, :h], x[:, h:]
    return jnp.concatenate([a * cos - b * sin, b * cos + a * sin], axis=-1)


def turn_back(x, cos, sin):
    return turn(x, cos, -sin)


def gather_tokens(x):
    mine = [x] + [shift(x, "y", k) for k in (1, 2, 3)]
    return jnp.concatenate(mine + [other_core(p) for p in mine], axis=0)


def scatter_tokens(part):
    blocks = part.reshape(2, 4, TOKENS, -1)
    total = None
    for k in (2, 1, 3, 0):
        piece = blocks[0, k] + other_core(blocks[1, k].astype(BF)).astype(F32)
        if k:
            piece = shift(piece.astype(BF), "y", 4 - k).astype(F32)
        total = piece if total is None else total + piece
    return total


def table(rows, columns):
    return (rows[:, None] == columns[None, :]).astype(BF)


def on_device(
    layer_input,
    segment,
    position,
    loss_token_mask,
    teacher,
    gain_one,
    wq,
    wk,
    wv,
    wo,
    aq,
    bq,
    ak,
    bk,
    av,
    bv,
    ao,
    bo,
    gain_two,
    wg,
    wu,
    wd,
    ag,
    bg,
    au,
    bu,
    ad,
    bd,
):
    core = lax.axis_index("c")
    at_z, at_y = lax.axis_index("z"), lax.axis_index("y")
    at_xl, at_xh = lax.axis_index("xl"), lax.axis_index("xh")
    at_x = 2 * at_xh + at_xl
    is_first = core == 0
    score_scale = WIDTH**-0.5
    hidden = layer_input[0].astype(F32)
    count_here = jnp.sum(loss_token_mask[0]).astype(BF)

    extra = jnp.concatenate([gain_one[None], gain_two[None], count_here.reshape(1, 1)], axis=1)
    extra = jnp.pad(extra, ((0, 1), (0, 384 - 19)))

    def attention_half(k):
        top = jnp.concatenate(
            [m[:, m.shape[1] // 2 * k : m.shape[1] // 2 * (k + 1)] for m in (wq, wk, wv, aq, ak, av)],
            axis=1,
        )
        low = jnp.concatenate(
            [m[:, m.shape[1] // 2 * k : m.shape[1] // 2 * (k + 1)] for m in (bq, bk, bv)] + [extra],
            axis=1,
        )
        return jnp.concatenate([top, low, jnp.zeros((1, 1152), BF)], axis=0)

    keep, send = pick(is_first, attention_half(0), attention_half(1))
    lower, upper = pick(is_first, keep, other_core(send))
    raw_one = gather_chips(jnp.concatenate([lower, upper], axis=0))
    raw_two = other_core(raw_one)
    marks = raw_one.reshape(128, 12, 1152)[:, 9, 768:896]
    gain_one_full = marks[:, :9].reshape(1, 1152).astype(F32)
    gain_two_full = marks[:, 9:18].reshape(1, 1152).astype(F32)
    valid_count = jnp.sum(marks[:, 18].astype(F32))
    raw = [raw_one.reshape(1536, 1152), raw_two.reshape(1536, 1152)]

    def output_half(k):
        zero = jnp.zeros((2, 128), BF)
        return jnp.concatenate(
            [
                jnp.concatenate([wo[:, 512 * k : 512 * k + 640], ao[:, 128 * k : 128 * k + 128]], axis=1),
                jnp.concatenate([bo[:, 512 * k : 512 * k + 640], zero], axis=1),
                jnp.concatenate([bd[:, 512 * k : 512 * k + 640], zero], axis=1),
            ],
            axis=0,
        )

    keep, send = pick(is_first, output_half(0), output_half(1))
    lower, upper = pick(is_first, keep, other_core(send))
    out_own = lax.optimization_barrier((jnp.concatenate([lower, upper], axis=0), raw_one))[0]
    out_one = gather_chips(out_own)
    out_two = other_core(out_one)
    raw_out = [out_one.reshape(1536, 768), out_two.reshape(1536, 768)]

    rows31 = jnp.concatenate(
        [
            wg,
            wu,
            bg,
            bu,
        ],
        axis=0,
    )
    rows31 = rows31.reshape(22, 8, 864).transpose(1, 0, 2)
    inner_rows = jnp.concatenate([ag, au, jnp.zeros((9, 352), BF)], axis=1)
    rows31 = jnp.concatenate([rows31, jnp.broadcast_to(inner_rows[None], (8, 9, 864))], axis=1)
    slab = jnp.zeros((8, 31, 864), BF)
    for ky in range(4):
        for kc in range(2):
            to = 2 * ((at_y + ky) % 4) + (core + kc) % 2
            source = 2 * ((at_y - ky) % 4) + (core - kc) % 2
            piece = lax.dynamic_index_in_dim(rows31, to, 0, keepdims=False)
            if ky or kc:
                route = []
                for y in range(4):
                    for c in range(2):
                        route.append((2 * y + c, 2 * ((y + ky) % 4) + (c + kc) % 2))
                piece = lax.ppermute(piece, ("y", "c"), route)
            slab = lax.dynamic_update_index_in_dim(slab, piece, source, 0)
    gate_own = jnp.concatenate([slab[:, :9].reshape(72, 864), slab[:, 18:20].reshape(16, 864)], axis=0)
    up_own = jnp.concatenate([slab[:, 9:18].reshape(72, 864), slab[:, 20:22].reshape(16, 864)], axis=0)
    inner_own = slab[:, 22:, :512].reshape(72, 512)
    down_own = lax.ppermute(
        jnp.pad(jnp.concatenate([wd, ad], axis=1), ((0, 2), (0, 0))), EVERY, down_route()
    )
    gate_own, up_own, inner_own, down_own, _ = lax.optimization_barrier(
        (gate_own, up_own, inner_own, down_own, raw_one)
    )
    gate_raw = gather_zx(gate_own, "x")
    up_raw = gather_zx(up_own, "z")
    inner_raw = gather_zx(inner_own, "x").reshape(1152, 512)
    down_raw = gather_zx(down_own, "z").reshape(896, 1408)

    ids = jnp.arange(1536, dtype=jnp.int32)
    dev, j = 2 * (ids // 24) + (ids % 24) // 12, ids % 12
    halves = jnp.arange(256, dtype=jnp.int32)
    inner_ids = jnp.where(halves < 128, 128 * core + halves, 128 * (1 - core) + halves - 128)
    heads_at = jnp.arange(1024, dtype=jnp.int32)
    head_ids = jnp.where(heads_at < 512, 512 * core + heads_at, 512 * (1 - core) + heads_at - 512)
    features = jnp.arange(1152, dtype=jnp.int32)
    put_rows = table(features, jnp.where(j < 9, 9 * dev + j, -1))
    put_inner = table(inner_ids, jnp.where((j >= 9) & (j < 11), 2 * dev + j - 9, -1))
    put_marks = table(features // 9, jnp.where(j == 11, dev, -1))
    put_mix = table(head_ids, jnp.where(j < 8, 8 * dev + j, -1))
    put_inner_out = table(inner_ids, jnp.where((j >= 8) & (j < 10), 2 * dev + j - 8, -1))
    put_inner_down = table(halves, jnp.where(j >= 10, 2 * dev + j - 10, -1))

    def plane(block):
        kz, kx = block // 4, block % 4
        x = (at_x - kx) % 4
        return (((at_z - kz) % 4) * 2 + x % 2) * 2 + x // 2

    put_feature = table(features, 72 * plane(features // 72) + features % 72)
    put_b = table(halves, 16 * plane(halves // 16) + halves % 16)
    hidden_ids = jnp.arange(864, dtype=jnp.int32)
    down_ids = jnp.arange(896, dtype=jnp.int32)
    put_down = table(
        hidden_ids, jnp.where(down_ids % 56 < 54, 54 * plane(down_ids // 56) + down_ids % 56, -1)
    )

    seq = (at_xh * 4 + at_y) * 2 + core
    tree_seg = segment[0]
    tree_pos = position[0]
    own_seg = lax.dynamic_slice_in_dim(tree_seg, seq * TOKENS, TOKENS)
    own_pos = lax.dynamic_slice_in_dim(tree_pos, seq * TOKENS, TOKENS)
    freq = ROPE_BASE ** (-(jnp.arange(128, dtype=F32) * 2.0 / WIDTH))
    angles = own_pos.astype(F32)[:, None] * freq[None, :]
    cos, sin = jnp.cos(angles), jnp.sin(angles)
    back = jnp.arange(16, dtype=jnp.int32)
    block_at = (((at_xh - (back % 8) // 4) % 2) * 4 + (at_y - back % 4) % 4) * 2 + jnp.where(
        back < 8, core, 1 - core
    )
    chosen = (block_at[:, None] == back[None, :]).astype(jnp.int32)[:, :, None]
    key_seg = jnp.sum(chosen * tree_seg.reshape(1, 16, TOKENS), axis=1).reshape(1, 2560)
    key_pos = jnp.sum(chosen * tree_pos.reshape(1, 16, TOKENS), axis=1).reshape(1, 2560)
    q_seg, q_pos = own_seg[:, None], own_pos[:, None]
    parent = (key_seg >= 1) & (key_seg <= 4) & (q_seg >= 5) & ((q_seg - 5) // 2 + 1 == key_seg)
    allowed = ((key_seg == q_seg) | (key_seg == 0) | parent) & (key_pos <= q_pos)
    allowed = jnp.concatenate([allowed] * HEADS, axis=0)

    scale_one, n_one, u_one = norm_parts(hidden, gain_one_full)
    u_rows = dot(u_one, put_rows).astype(BF)
    inner = [dot(u_rows, raw[i][:, 768:]).astype(BF) for i in (0, 1)]
    sides = []
    for i in range(3):
        part = jnp.concatenate([inner[0][:, 128 * i : 128 * i + 128], inner[1][:, 128 * i : 128 * i + 128]], axis=1)
        sides.append(u_rows + dot(part, put_inner).astype(BF))
    kk = pick(is_first, *[dot(sides[1], raw[i][:, 512:640]) for i in (0, 1)])
    vv = pick(is_first, *[dot(sides[2], raw[i][:, 640:768]) for i in (0, 1)])
    kv_own = jnp.concatenate([turn(jnp.concatenate(kk, axis=1), cos, sin), vv[0], vv[1]], axis=1).astype(BF)

    def tree_shift(x, kh, ky):
        route = []
        for h in range(2):
            for y in range(4):
                route.append((4 * h + y, 4 * ((h + kh) % 2) + (y + ky) % 4))
        return lax.ppermute(x, ("xh", "y"), route)

    kv_mine = [kv_own] + [tree_shift(kv_own, k // 4, k % 4) for k in range(1, 8)]
    kv_mine = jnp.concatenate(kv_mine, axis=0)
    kv = jnp.concatenate([kv_mine, other_core(kv_mine)], axis=0)
    keys, values = kv[:, :256], kv[:, 256:]
    queries = [dot(sides[0], raw[i][:, :512]) for i in (0, 1)]
    q_rows = jnp.concatenate(
        [turn(queries[h // 2][:, WIDTH * (h % 2) : WIDTH * (h % 2 + 1)], cos, sin) for h in range(HEADS)],
        axis=0,
    ).astype(BF)
    scores = jnp.where(allowed, dot_tr(q_rows, keys) * score_scale, MASKED_SCORE)
    top = jnp.max(scores, axis=-1, keepdims=True)
    ex = jnp.exp(scores - top)
    total = jnp.sum(ex, axis=-1, keepdims=True)
    lse = top + jnp.log(total)
    mix_rows = dot((ex / total).astype(BF), values).astype(BF)
    mix = jnp.concatenate([mix_rows[TOKENS * h : TOKENS * (h + 1)] for h in range(HEADS)], axis=1)
    mix_placed = dot(mix, put_mix).astype(BF)
    inner_out = jnp.concatenate([dot(mix_placed, raw_out[i][:, 640:]) for i in (0, 1)], axis=1).astype(BF)
    side_out = mix_placed + dot(inner_out, put_inner_out).astype(BF)
    left, right = pick(is_first, *[dot(side_out, raw_out[i][:, :640]) for i in (0, 1)])
    after = hidden + jnp.concatenate([left, right[:, 128:]], axis=1)

    a_gate = dot(inner_raw[:, :256], put_b).astype(BF)
    a_up = dot(inner_raw[:, 256:], put_b).astype(BF)
    b_gate = gate_raw[:, :, 72:].reshape(256, 864)
    b_up = up_raw[:, :, 72:].reshape(256, 864)
    w_gate = (gate_raw[:, :, :72].reshape(1152, 864).astype(F32) + dot(a_gate, b_gate)).astype(BF)
    w_up = (up_raw[:, :, :72].reshape(1152, 864).astype(F32) + dot(a_up, b_up)).astype(BF)
    left, right = pick(is_first, *[dot(put_inner_down, raw_out[i][:, :640]).astype(BF) for i in (0, 1)])
    b_down = jnp.concatenate([left, right[:, 128:]], axis=1)
    a_down = dot(put_down, down_raw[:, 1152:]).astype(BF)
    w_down = (dot(put_down, down_raw[:, :1152]) + dot(a_down, b_down)).astype(BF)

    scale_two, n_two, u_two = norm_parts(after, gain_two_full)
    u_all = gather_tokens(dot(u_two, put_feature).astype(BF))
    gate = dot(u_all, w_gate)
    up = dot(u_all, w_up)
    act, act_pull = jax.vjp(lambda g, u: jax.nn.gelu(g, approximate=True) * u, gate, up)
    act = act.astype(BF)
    result = after + scatter_tokens(dot(act, w_down))

    valid = loss_token_mask[0].astype(F32)[:, None]
    error = result - teacher[0].astype(F32)
    loss_here = jnp.sum(valid * error * error)
    grad_result = 2.0 * 20480.0 / valid_count * valid * error

    g_all = gather_tokens(grad_result.astype(BF))
    g_act = dot_tr(g_all, w_down).astype(BF)
    g_gate, g_up = act_pull(g_act.astype(F32))
    g_gate, g_up = g_gate.astype(BF), g_up.astype(BF)
    g_u_two = select_back(scatter_tokens(dot_tr(g_gate, w_gate) + dot_tr(g_up, w_up)), put_feature)
    gw_gate = dot_tl(u_all, g_gate).astype(BF)
    gw_up = dot_tl(u_all, g_up).astype(BF)
    gw_down = dot_tl(act, g_all).astype(BF)
    gb_gate = dot_tl(a_gate, gw_gate).astype(BF)
    gb_up = dot_tl(a_up, gw_up).astype(BF)
    gb_down = dot_tl(a_down, gw_down).astype(BF)
    gw_down = dot_tl(put_down, gw_down).astype(BF)
    gate_sum = scatter_zx(
        jnp.concatenate([gw_gate.reshape(4, 4, 72, 864), gb_gate.reshape(4, 4, 16, 864)], axis=2), "z"
    ).astype(BF)
    up_sum = scatter_zx(
        jnp.concatenate([gw_up.reshape(4, 4, 72, 864), gb_up.reshape(4, 4, 16, 864)], axis=2), "x"
    ).astype(BF)
    down_sum = scatter_zx(gw_down.reshape(4, 4, 56, 1152), "x").astype(BF)
    ga_gate = dot_tr(dot_tr(gate_sum[:72], b_gate).astype(BF), put_b)
    ga_up = dot_tr(dot_tr(up_sum[:72], b_up).astype(BF), put_b)
    ga_part = jnp.concatenate([ga_gate, ga_up, jnp.zeros((72, 352), F32)], axis=1).astype(BF)
    leaving = jnp.concatenate(
        [
            gate_sum[:72].reshape(8, 9, 864),
            up_sum[:72].reshape(8, 9, 864),
            gate_sum[72:].reshape(8, 2, 864),
            up_sum[72:].reshape(8, 2, 864),
            ga_part.reshape(8, 9, 864),
        ],
        axis=1,
    )
    slab = jnp.zeros((8, 31, 864), BF)
    for ky in range(4):
        for kc in range(2):
            to = 2 * ((at_y + ky) % 4) + (core + kc) % 2
            source = 2 * ((at_y - ky) % 4) + (core - kc) % 2
            piece = lax.dynamic_index_in_dim(leaving, to, 0, keepdims=False)
            if ky or kc:
                route = []
                for y in range(4):
                    for c in range(2):
                        route.append((2 * y + c, 2 * ((y + ky) % 4) + (c + kc) % 2))
                piece = lax.ppermute(piece, ("y", "c"), route)
            slab = lax.dynamic_update_index_in_dim(slab, piece, source, 0)
    wide = slab[:, :22].transpose(1, 0, 2).reshape(22, 6912).astype(F32)
    ga = jnp.sum(slab[:, 22:, :512].astype(F32), axis=0)
    gw_down_own = lax.ppermute(down_sum, EVERY, [(b, a) for a, b in down_route()])[:54]
    ga_down_own = dot_tr(gw_down_own, b_down)

    norm_two_back, g_gain_two = norm_back(scale_two, n_two, gain_two_full, g_u_two)
    g_after = grad_result + norm_two_back
    g_after_b = g_after.astype(BF)
    once = jnp.where(jnp.arange(640) < 128, 0, 1).astype(BF)[None]
    g_half = pick(is_first, g_after_b[:, :640], g_after_b[:, 512:])
    g_once = pick(is_first, g_after_b[:, :640], g_after_b[:, 512:] * once)
    d_out = dot_tr(g_once[0], raw_out[0][:, :640]) + dot_tr(g_once[1], raw_out[1][:, :640])
    gi_out = dot_tr(d_out.astype(BF), put_inner_out).astype(BF)
    d_out = (
        d_out
        + dot_tr(gi_out[:, :128], raw_out[0][:, 640:])
        + dot_tr(gi_out[:, 128:], raw_out[1][:, 640:])
    )
    g_mix = dot_tr(d_out.astype(BF), put_mix).astype(BF)
    g_rows = jnp.concatenate([g_mix[:, WIDTH * h : WIDTH * (h + 1)] for h in range(HEADS)], axis=0)
    scores_again = jnp.where(allowed, dot_tr(q_rows, keys) * score_scale, MASKED_SCORE)
    probs = jnp.where(allowed, jnp.exp(scores_again - lse), 0.0)
    g_probs = dot_tr(g_rows, values)
    g_scores = (probs * (g_probs - jnp.sum(probs * g_probs, axis=-1, keepdims=True))).astype(BF)
    g_keys = dot_tl(g_scores, q_rows) * score_scale
    g_values = dot_tl(probs.astype(BF), g_rows)
    g_kv = jnp.concatenate([g_keys, g_values], axis=1)
    n_mine = 8 * TOKENS
    g_kv_sum = g_kv[:n_mine] + other_core(g_kv[n_mine:].astype(BF)).astype(F32)
    g_kv_b = g_kv_sum.astype(BF)
    g_kv_own = g_kv_sum[:TOKENS]
    for k in range(1, 8):
        away = g_kv_b[TOKENS * k : TOKENS * (k + 1)]
        g_kv_own = g_kv_own + tree_shift(away, k // 4, (4 - k % 4) % 4).astype(F32)
    g_q_rows = dot(g_scores, keys) * score_scale
    g_q = [
        jnp.concatenate(
            [turn_back(g_q_rows[TOKENS * h : TOKENS * (h + 1)], cos, sin) for h in (2 * i, 2 * i + 1)],
            axis=1,
        ).astype(BF)
        for i in (0, 1)
    ]
    g_k = turn_back(g_kv_own[:, :256], cos, sin).astype(BF)
    g_v = g_kv_own[:, 256:].astype(BF)
    g_k = pick(is_first, g_k[:, :128], g_k[:, 128:])
    g_v = pick(is_first, g_v[:, :128], g_v[:, 128:])
    d_one = None
    for i, (g, first, last) in enumerate(((g_q, 0, 512), (g_k, 512, 640), (g_v, 640, 768))):
        d = dot_tr(g[0], raw[0][:, first:last]) + dot_tr(g[1], raw[1][:, first:last])
        gi = dot_tr(d.astype(BF), put_inner).astype(BF)
        inner_at = 768 + 128 * i
        d = d + dot_tr(gi[:, :128], raw[0][:, inner_at : inner_at + 128])
        d = d + dot_tr(gi[:, 128:], raw[1][:, inner_at : inner_at + 128])
        d_one = d if d_one is None else d_one + d
    g_u_one = select_back(d_one, put_rows)
    norm_one_back, g_gain_one = norm_back(scale_one, n_one, gain_one_full, g_u_one)
    grad_hidden = (g_after + norm_one_back).astype(BF)

    def to_owners(own, away):
        summed = (own + other_core(away.astype(BF)).astype(F32)).astype(BF)
        return jnp.sum(exchange(summed.reshape(64, 24, -1), CHIPS).astype(F32), axis=0)

    def both_halves(owned):
        mine, away = pick(is_first, owned[:12], owned[12:])
        return pick(is_first, mine, other_core(away.astype(BF)).astype(F32))

    left, right = pick(is_first, gb_down[:, :640], gb_down[:, 512:])
    owned_out = to_owners(
        dot_tl(side_out, g_half[0]) + dot_tl(put_inner_down, left),
        dot_tl(side_out, g_half[1]) + dot_tl(put_inner_down, right),
    )
    left, right = both_halves(owned_out)
    own_out = jnp.concatenate([left, right[:, 128:]], axis=1)
    d = dot_tr(own_out[:8, :640].astype(BF), pick(is_first, *raw_out)[0][:, :640]) + dot_tr(
        own_out[:8, 640:].astype(BF), pick(is_first, *raw_out)[1][:, 128:640]
    )
    ga_out_own = dot_tr(d.astype(BF), put_inner_out)
    ga_out_own = jnp.concatenate(pick(is_first, ga_out_own[:, :128], ga_out_own[:, 128:]), axis=1)

    nines = jnp.arange(9, dtype=jnp.int32)[:, None] == features[None, :] % 9
    loss_high, loss_rest = split_in_two(loss_here)
    loss_mid, loss_low = split_in_two(loss_here - loss_high.astype(F32))
    at_marks = (j == 11).astype(BF)[None, :]
    more_side = jnp.concatenate(
        [
            dot(jnp.where(nines, g_gain_one, 0.0).astype(BF), put_marks).astype(BF),
            dot(jnp.where(nines, g_gain_two, 0.0).astype(BF), put_marks).astype(BF),
            loss_high * at_marks,
            loss_mid * at_marks,
            loss_low * at_marks,
            jnp.zeros((11, 1536), BF),
        ],
        axis=0,
    )
    lines = jnp.arange(32, dtype=jnp.int32)
    line_at = jnp.where(lines < 18, lines, jnp.where(lines < 21, lines + 3 * core, -1))
    more_grad = table(line_at, jnp.arange(512, dtype=jnp.int32))
    side_q = jnp.concatenate([sides[0], more_side], axis=0)
    sums = [
        jnp.concatenate(
            [
                dot_tl(side_q, jnp.concatenate([g_q[i], more_grad], axis=0)),
                dot_tl(sides[1], g_k[i]),
                dot_tl(sides[2], g_v[i]),
            ],
            axis=1,
        )
        for i in (0, 1)
    ]
    owned = to_owners(sums[0], sums[1])
    loss_value = jnp.sum(owned[11, 18:24]) / (1152.0 * valid_count)
    left, right = both_halves(owned)
    gains = left[11]
    left_b, right_b = left.astype(BF), right.astype(BF)
    mine_b, other_b = pick(is_first, left_b, right_b)
    ga_own = []
    for first, last in ((0, 512), (512, 640), (640, 768)):
        d = dot_tr(mine_b[:, first:last], raw[0][:, first:last]) + dot_tr(
            other_b[:, first:last], raw[1][:, first:last]
        )
        g = dot_tr(d.astype(BF), put_inner)[:9]
        ga_own.append(jnp.concatenate(pick(is_first, g[:, :128], g[:, 128:]), axis=1))

    def columns(first, last, rows):
        return jnp.concatenate([left[rows, first:last], right[rows, first:last]], axis=1)

    top_rows, low_rows = slice(0, 9), slice(9, 11)

    return (
        result.astype(BF)[None],
        loss_value,
        grad_hidden[None],
        gains[:9],
        columns(0, 512, top_rows),
        columns(512, 640, top_rows),
        columns(640, 768, top_rows),
        own_out[:8],
        ga_own[0],
        columns(0, 512, low_rows),
        ga_own[1],
        columns(512, 640, low_rows),
        ga_own[2],
        columns(640, 768, low_rows),
        ga_out_own,
        own_out[8:10],
        gains[9:18],
        wide[:9],
        wide[9:18],
        gw_down_own.astype(F32),
        ga[:, :256],
        wide[18:20],
        ga[:, 256:],
        wide[20:],
        ga_down_own,
        own_out[10:],
    )


def solution(mesh):
    mesh = Mesh(mesh.devices.reshape([SIZES[a] for a in EVERY]), EVERY)
    tree, seq = ("z", "xl"), ("xh", "y", "c")
    rows = P(EVERY, None)
    vector = P(EVERY)
    return jax.shard_map(
        on_device,
        mesh=mesh,
        in_specs=(
            P(tree, seq, None),
            P(tree, None),
            P(tree, None),
            P(tree, seq),
            P(tree, seq, None),
            vector,
        )
        + (rows,) * 12
        + (vector,)
        + (rows,) * 9,
        out_specs=(P(tree, seq, None), P(), P(tree, seq, None), vector)
        + (rows,) * 12
        + (vector,)
        + (rows,) * 9,
        check_vma=False,
    )
```

```python
import jax
import jax.numpy as jnp
from jax import lax
from jax.sharding import Mesh, PartitionSpec as P

EPSILON = 1e-06
ROPE_BASE = 10000.0
MASKED_SCORE = -1e30
BF = jnp.bfloat16
F32 = jnp.float32

CHIPS = ("z", "xl", "xh", "y")
EVERY = ("z", "xl", "xh", "y", "c")
SIZES = dict(z=4, xl=2, xh=2, y=4, c=2)
RING = dict(z="z", x=("xl", "xh"), y="y")
TOKENS = 160
HEADS = 4
WIDTH = 256


def dot(a, b):
    return jnp.dot(a, b, preferred_element_type=F32)


def dot_tl(a, b):
    return lax.dot_general(a, b, (((0,), (0,)), ((), ())), preferred_element_type=F32)


def dot_tr(a, b):
    return lax.dot_general(a, b, (((1,), (1,)), ((), ())), preferred_element_type=F32)


def exchange(x, axes):
    return lax.all_to_all(x, axes, split_axis=0, concat_axis=0, tiled=True)


def gather_chips(x):
    return exchange(jnp.broadcast_to(x[None], (64,) + x.shape), CHIPS)


def other_core(x):
    return lax.ppermute(x, "c", [(0, 1), (1, 0)])


def shift(x, axis, k):
    number = [0, 2, 1, 3] if axis == "x" else [0, 1, 2, 3]
    return lax.ppermute(x, RING[axis], [(number[i], number[(i + k) % 4]) for i in range(4)])


def pick(cond, a, b):
    return jnp.where(cond, a, b), jnp.where(cond, b, a)


def split_in_two(x):
    high = x.astype(BF)
    return high, (x - high.astype(F32)).astype(BF)


def select_back(x, table):
    high, low = split_in_two(x)
    return dot_tr(high, table) + dot_tr(low, table)


def down_route():
    pairs = []
    for o in range(16):
        for t in range(8):
            pairs.append((8 * o + t, 8 * (8 * (o % 2) + t) + o // 2))
    return pairs


def gather_line(x, axis):
    return jnp.stack([x] + [shift(x, axis, k) for k in (1, 2, 3)])


def scatter_zx(x, first):
    second = "z" if first == "x" else "x"
    x = [x[k] if first == "z" else x[:, k] for k in range(4)]
    line = x[0].astype(F32)
    for k in (1, 2, 3):
        line = line + shift(x[k], first, 4 - k).astype(F32)
    line = line.astype(BF)
    out = line[0].astype(F32)
    for k in (1, 2, 3):
        out = out + shift(line[k], second, 4 - k).astype(F32)
    return out


def norm_parts(values, gain):
    scale = lax.rsqrt(jnp.mean(values * values, axis=-1, keepdims=True) + EPSILON)
    n = values * scale
    return scale, n, (n * (1.0 + gain)).astype(BF)


def norm_back(scale, n, gain, grad):
    m = grad * (1.0 + gain)
    back = scale * (m - n * jnp.mean(m * n, axis=-1, keepdims=True))
    return back, jnp.sum(grad * n, axis=0, keepdims=True)


def turn(x, cos, sin):
    h = cos.shape[-1]
    a, b = x[:, :h], x[:, h:]
    return jnp.concatenate([a * cos - b * sin, b * cos + a * sin], axis=-1)


def turn_back(x, cos, sin):
    return turn(x, cos, -sin)


def gather_tokens(x):
    mine = [x] + [shift(x, "y", k) for k in (1, 2, 3)]
    return jnp.concatenate(mine + [other_core(p) for p in mine], axis=0)


def scatter_tokens(part):
    blocks = part.reshape(2, 4, TOKENS, -1)
    total = None
    for k in (2, 1, 3, 0):
        piece = blocks[0, k] + other_core(blocks[1, k].astype(BF)).astype(F32)
        if k:
            piece = shift(piece.astype(BF), "y", 4 - k).astype(F32)
        total = piece if total is None else total + piece
    return total


def after(done, *values):
    return lax.optimization_barrier(values + (done,))


def table(rows, columns):
    return (rows[:, None] == columns[None, :]).astype(BF)


def swap_columns(pieces, core, at_y):
    slab = jnp.zeros(pieces.shape, pieces.dtype)
    for ky in range(4):
        for kc in range(2):
            to = 2 * ((at_y + ky) % 4) + (core + kc) % 2
            source = 2 * ((at_y - ky) % 4) + (core - kc) % 2
            piece = lax.dynamic_index_in_dim(pieces, to, 0, keepdims=False)
            if ky or kc:
                route = []
                for y in range(4):
                    for c in range(2):
                        route.append((2 * y + c, 2 * ((y + ky) % 4) + (c + kc) % 2))
                piece = lax.ppermute(piece, ("y", "c"), route)
            slab = lax.dynamic_update_index_in_dim(slab, piece, source, 0)
    return slab


def on_device(
    layer_input,
    segment,
    position,
    loss_token_mask,
    teacher,
    gain_one,
    wq,
    wk,
    wv,
    wo,
    aq,
    bq,
    ak,
    bk,
    av,
    bv,
    ao,
    bo,
    gain_two,
    wg,
    wu,
    wd,
    ag,
    bg,
    au,
    bu,
    ad,
    bd,
):
    core = lax.axis_index("c")
    at_z, at_y = lax.axis_index("z"), lax.axis_index("y")
    at_xl, at_xh = lax.axis_index("xl"), lax.axis_index("xh")
    at_x = 2 * at_xh + at_xl
    is_first = core == 0
    score_scale = WIDTH**-0.5
    count_here = jnp.sum(loss_token_mask[0]).astype(BF)

    extra = jnp.concatenate([gain_one[None], gain_two[None], count_here.reshape(1, 1)], axis=1)
    extra = jnp.pad(extra, ((0, 1), (0, 384 - 19)))

    def attention_half(k):
        top = jnp.concatenate(
            [m[:, m.shape[1] // 2 * k : m.shape[1] // 2 * (k + 1)] for m in (wq, wk, wv, aq, ak, av)],
            axis=1,
        )
        low = jnp.concatenate(
            [m[:, m.shape[1] // 2 * k : m.shape[1] // 2 * (k + 1)] for m in (bq, bk, bv)] + [extra],
            axis=1,
        )
        return jnp.concatenate([top, low, jnp.zeros((1, 1152), BF)], axis=0)

    keep, send = pick(is_first, attention_half(0), attention_half(1))
    lower, upper = pick(is_first, keep, other_core(send))
    att_own = jnp.concatenate([lower, upper], axis=0)
    raw_one = gather_chips(att_own)
    raw_two = other_core(raw_one)
    (layer_input, wg, wu, bg, bu, wd, ad, ag, au, wo, ao, bo, bd, segment, position, core, at_z, _) = after(
        att_own,
        layer_input, wg, wu, bg, bu, wd, ad, ag, au, wo, ao, bo, bd, segment, position, core, at_z,
    )
    is_first = core == 0
    hidden = layer_input[0].astype(F32)
    marks = raw_one.reshape(128, 12, 1152)[:, 9, 768:896]
    gain_one_full = marks[:, :9].reshape(1, 1152).astype(F32)
    gain_two_full = marks[:, 9:18].reshape(1, 1152).astype(F32)
    valid_count = jnp.sum(marks[:, 18].astype(F32))
    raw = [raw_one.reshape(1536, 1152), raw_two.reshape(1536, 1152)]

    def output_half(k):
        wide = jnp.concatenate([m[:, 512 * k : 512 * k + 640] for m in (wo, bo, bd)], axis=0)
        narrow = jnp.pad(ao[:, 128 * k : 128 * k + 128], ((0, 4), (0, 0)))
        return jnp.concatenate([wide, narrow, jnp.pad((ag, au)[k], ((0, 3), (0, 0)))], axis=1)

    keep, send = pick(is_first, output_half(0), output_half(1))
    lower, upper = pick(is_first, keep, other_core(send))
    out_own, _ = after(raw_one, jnp.concatenate([lower, upper], axis=0))
    out_one = gather_chips(out_own)
    out_two = other_core(out_one)
    raw_out = [out_one.reshape(1536, 1024), out_two.reshape(1536, 1024)]

    rows22 = jnp.concatenate([wg, wu, bg, bu], axis=0).reshape(22, 128, 54)
    rows22 = jnp.pad(rows22, ((0, 0), (0, 0), (0, 2))).reshape(22, 8, 896).transpose(1, 0, 2)
    slab = swap_columns(rows22, core, at_y)
    ff_own = jnp.concatenate(
        [
            slab[:, :9].reshape(72, 896),
            slab[:, 9:18].reshape(72, 896),
            slab[:, 18:20].reshape(16, 896),
            slab[:, 20:22].reshape(16, 896),
        ],
        axis=0,
    )
    down_own = lax.ppermute(
        jnp.pad(jnp.concatenate([wd, ad], axis=1), ((0, 2), (0, 0))), EVERY, down_route()
    )
    down_own, _ = after(raw_one, down_own)

    ids = jnp.arange(1536, dtype=jnp.int32)
    dev, j = 2 * (ids // 24) + (ids % 24) // 12, ids % 12
    halves = jnp.arange(256, dtype=jnp.int32)
    inner_ids = jnp.where(halves < 128, 128 * core + halves, 128 * (1 - core) + halves - 128)
    heads_at = jnp.arange(1024, dtype=jnp.int32)
    head_ids = jnp.where(heads_at < 512, 512 * core + heads_at, 512 * (1 - core) + heads_at - 512)
    features = jnp.arange(1152, dtype=jnp.int32)
    put_rows = table(features, jnp.where(j < 9, 9 * dev + j, -1))
    put_inner = table(inner_ids, jnp.where((j >= 9) & (j < 11), 2 * dev + j - 9, -1))
    put_marks = table(features // 9, jnp.where(j == 11, dev, -1))
    put_mix = table(head_ids, jnp.where(j < 8, 8 * dev + j, -1))
    put_inner_out = table(inner_ids, jnp.where((j >= 8) & (j < 10), 2 * dev + j - 8, -1))
    put_inner_down = table(halves, jnp.where(j >= 10, 2 * dev + j - 10, -1))

    def plane(block):
        kz, kx = block // 4, block % 4
        x = (at_x - kx) % 4
        return (((at_z - kz) % 4) * 2 + x % 2) * 2 + x // 2

    hidden_ids = jnp.arange(896, dtype=jnp.int32)
    put_down = table(hidden_ids, 56 * plane(hidden_ids // 56) + hidden_ids % 56)

    seq = (at_xh * 4 + at_y) * 2 + core
    tree_seg = segment[0]
    tree_pos = position[0]
    own_seg = lax.dynamic_slice_in_dim(tree_seg, seq * TOKENS, TOKENS)
    own_pos = lax.dynamic_slice_in_dim(tree_pos, seq * TOKENS, TOKENS)
    freq = ROPE_BASE ** (-(jnp.arange(128, dtype=F32) * 2.0 / WIDTH))
    angles = own_pos.astype(F32)[:, None] * freq[None, :]
    cos, sin = jnp.cos(angles), jnp.sin(angles)
    back = jnp.arange(16, dtype=jnp.int32)
    block_at = (((at_xh - (back % 8) // 4) % 2) * 4 + (at_y - back % 4) % 4) * 2 + jnp.where(
        back < 8, core, 1 - core
    )
    chosen = (block_at[:, None] == back[None, :]).astype(jnp.int32)[:, :, None]
    key_seg = jnp.sum(chosen * tree_seg.reshape(1, 16, TOKENS), axis=1).reshape(1, 2560)
    key_pos = jnp.sum(chosen * tree_pos.reshape(1, 16, TOKENS), axis=1).reshape(1, 2560)
    q_seg, q_pos = own_seg[:, None], own_pos[:, None]
    parent = (key_seg >= 1) & (key_seg <= 4) & (q_seg >= 5) & ((q_seg - 5) // 2 + 1 == key_seg)
    allowed = ((key_seg == q_seg) | (key_seg == 0) | parent) & (key_pos <= q_pos)
    allowed = jnp.concatenate([allowed] * HEADS, axis=0)

    scale_one, n_one, u_one = norm_parts(hidden, gain_one_full)
    u_rows = dot(u_one, put_rows).astype(BF)
    inner = [dot(u_rows, raw[i][:, 768:]).astype(BF) for i in (0, 1)]
    sides = []
    for i in range(3):
        part = jnp.concatenate([inner[0][:, 128 * i : 128 * i + 128], inner[1][:, 128 * i : 128 * i + 128]], axis=1)
        sides.append(u_rows + dot(part, put_inner).astype(BF))
    kk = pick(is_first, *[dot(sides[1], raw[i][:, 512:640]) for i in (0, 1)])
    vv = pick(is_first, *[dot(sides[2], raw[i][:, 640:768]) for i in (0, 1)])
    kv_own = jnp.concatenate([turn(jnp.concatenate(kk, axis=1), cos, sin), vv[0], vv[1]], axis=1).astype(BF)

    down_line = gather_line(down_own, "z")
    ff_own, _ = after(kv_own, ff_own)
    ff_all = exchange(jnp.broadcast_to(ff_own[None], (16, 176, 896)), ("z", "xl", "xh"))

    def tree_shift(x, kh, ky):
        route = []
        for h in range(2):
            for y in range(4):
                route.append((4 * h + y, 4 * ((h + kh) % 2) + (y + ky) % 4))
        return lax.ppermute(x, ("xh", "y"), route)

    kv_mine = [kv_own] + [tree_shift(kv_own, k // 4, k % 4) for k in range(1, 8)]
    kv_mine = jnp.concatenate(kv_mine, axis=0)
    kv = jnp.concatenate([kv_mine, other_core(kv_mine)], axis=0)
    keys, values = kv[:, :256], kv[:, 256:]
    down_line, _ = after(kv, down_line)
    down_raw = jnp.stack([down_line] + [shift(down_line, "x", k) for k in (1, 2, 3)], axis=1)
    down_raw = down_raw.reshape(896, 1408)
    queries = [dot(sides[0], raw[i][:, :512]) for i in (0, 1)]
    q_rows = jnp.concatenate(
        [turn(queries[h // 2][:, WIDTH * (h % 2) : WIDTH * (h % 2 + 1)], cos, sin) for h in range(HEADS)],
        axis=0,
    ).astype(BF)
    scores = jnp.where(allowed, dot_tr(q_rows, keys) * score_scale, MASKED_SCORE)
    top = jnp.max(scores, axis=-1, keepdims=True)
    ex = jnp.exp(scores - top)
    total = jnp.sum(ex, axis=-1, keepdims=True)
    lse = top + jnp.log(total)
    mix_rows = dot((ex / total).astype(BF), values).astype(BF)
    mix = jnp.concatenate([mix_rows[TOKENS * h : TOKENS * (h + 1)] for h in range(HEADS)], axis=1)
    mix_placed = dot(mix, put_mix).astype(BF)
    inner_out = jnp.concatenate([dot(mix_placed, raw_out[i][:, 640:768]) for i in (0, 1)], axis=1).astype(BF)
    side_out = mix_placed + dot(inner_out, put_inner_out).astype(BF)
    left, right = pick(is_first, *[dot(side_out, raw_out[i][:, :640]) for i in (0, 1)])
    after_att = hidden + jnp.concatenate([left, right[:, 128:]], axis=1)

    a_gate, a_up = pick(is_first, *[dot(put_rows, raw_out[i][:, 768:]).astype(BF) for i in (0, 1)])
    b_gate = ff_all[:, 144:160].reshape(256, 896)
    b_up = ff_all[:, 160:].reshape(256, 896)
    w_gate = (ff_all[:, :72].reshape(1152, 896).astype(F32) + dot(a_gate, b_gate)).astype(BF)
    w_up = (ff_all[:, 72:144].reshape(1152, 896).astype(F32) + dot(a_up, b_up)).astype(BF)
    left, right = pick(is_first, *[dot(put_inner_down, raw_out[i][:, :640]).astype(BF) for i in (0, 1)])
    b_down = jnp.concatenate([left, right[:, 128:]], axis=1)
    a_down = dot(put_down, down_raw[:, 1152:]).astype(BF)
    w_down = (dot(put_down, down_raw[:, :1152]) + dot(a_down, b_down)).astype(BF)

    scale_two, n_two, u_two = norm_parts(after_att, gain_two_full)
    u_all = gather_tokens(u_two)
    gate = dot(u_all, w_gate)
    up = dot(u_all, w_up)
    act, act_pull = jax.vjp(lambda g, u: jax.nn.gelu(g, approximate=True) * u, gate, up)
    act = act.astype(BF)
    result = after_att + scatter_tokens(dot(act, w_down))

    valid = loss_token_mask[0].astype(F32)[:, None]
    error = result - teacher[0].astype(F32)
    loss_here = jnp.sum(valid * error * error)
    grad_result = 2.0 * 20480.0 / valid_count * valid * error

    g_all = gather_tokens(grad_result.astype(BF))
    g_act = dot_tr(g_all, w_down).astype(BF)
    g_gate, g_up = act_pull(g_act.astype(F32))
    g_gate, g_up = g_gate.astype(BF), g_up.astype(BF)
    g_u_part = dot_tr(g_gate, w_gate) + dot_tr(g_up, w_up)
    g_u_two = scatter_tokens(g_u_part)
    u_all, act, g_all, g_gate, g_up, _ = after(g_u_part, u_all, act, g_all, g_gate, g_up)
    gw_gate = dot_tl(u_all, g_gate).astype(BF)
    gw_up = dot_tl(u_all, g_up).astype(BF)
    gb_gate = dot_tl(a_gate, gw_gate).astype(BF)
    gb_up = dot_tl(a_up, gw_up).astype(BF)
    ff_grads = jnp.concatenate(
        [
            gw_gate.reshape(16, 72, 896),
            gw_up.reshape(16, 72, 896),
            gb_gate.reshape(16, 16, 896),
            gb_up.reshape(16, 16, 896),
        ],
        axis=1,
    )
    ff_sum = jnp.sum(exchange(ff_grads, ("z", "xl", "xh")).astype(F32), axis=0).astype(BF)
    gw_down = dot_tl(act, g_all).astype(BF)
    gb_down = dot_tl(a_down, gw_down).astype(BF)
    gw_down = dot_tl(put_down, gw_down).astype(BF)
    down_sum = scatter_zx(gw_down.reshape(4, 4, 56, 1152), "x").astype(BF)
    ga_part = jnp.concatenate(
        [dot_tr(ff_sum[:72], b_gate), dot_tr(ff_sum[72:144], b_up), jnp.zeros((72, 384), F32)], axis=1
    ).astype(BF)
    leaving = jnp.concatenate(
        [
            ff_sum[:72].reshape(8, 9, 896),
            ff_sum[72:144].reshape(8, 9, 896),
            ff_sum[144:160].reshape(8, 2, 896),
            ff_sum[160:].reshape(8, 2, 896),
            ga_part.reshape(8, 9, 896),
        ],
        axis=1,
    )
    slab = swap_columns(leaving, core, at_y)
    wide = slab[:, :22].transpose(1, 0, 2).reshape(22, 128, 56)[:, :, :54].reshape(22, 6912).astype(F32)
    ga = jnp.sum(slab[:, 22:, :512].astype(F32), axis=0)
    gw_down_own = lax.ppermute(down_sum, EVERY, [(b, a) for a, b in down_route()])[:54]
    ga_down_own = dot_tr(gw_down_own, b_down)

    norm_two_back, g_gain_two = norm_back(scale_two, n_two, gain_two_full, g_u_two)
    g_after = grad_result + norm_two_back
    g_after_b = g_after.astype(BF)
    once = jnp.where(jnp.arange(640) < 128, 0, 1).astype(BF)[None]
    g_half = pick(is_first, g_after_b[:, :640], g_after_b[:, 512:])
    g_once = pick(is_first, g_after_b[:, :640], g_after_b[:, 512:] * once)
    d_out = dot_tr(g_once[0], raw_out[0][:, :640]) + dot_tr(g_once[1], raw_out[1][:, :640])
    gi_out = dot_tr(d_out.astype(BF), put_inner_out).astype(BF)
    d_out = (
        d_out
        + dot_tr(gi_out[:, :128], raw_out[0][:, 640:768])
        + dot_tr(gi_out[:, 128:], raw_out[1][:, 640:768])
    )
    g_mix = dot_tr(d_out.astype(BF), put_mix).astype(BF)
    g_rows = jnp.concatenate([g_mix[:, WIDTH * h : WIDTH * (h + 1)] for h in range(HEADS)], axis=0)
    scores_again = jnp.where(allowed, dot_tr(q_rows, keys) * score_scale, MASKED_SCORE)
    probs = jnp.where(allowed, jnp.exp(scores_again - lse), 0.0)
    g_probs = dot_tr(g_rows, values)
    g_scores = (probs * (g_probs - jnp.sum(probs * g_probs, axis=-1, keepdims=True))).astype(BF)
    g_keys = dot_tl(g_scores, q_rows) * score_scale
    g_values = dot_tl(probs.astype(BF), g_rows)
    g_kv = jnp.concatenate([g_keys, g_values], axis=1)
    n_mine = 8 * TOKENS
    g_kv_sum = g_kv[:n_mine] + other_core(g_kv[n_mine:].astype(BF)).astype(F32)
    g_kv_b = g_kv_sum.astype(BF)
    g_kv_own = g_kv_sum[:TOKENS]
    for k in range(1, 8):
        away = g_kv_b[TOKENS * k : TOKENS * (k + 1)]
        g_kv_own = g_kv_own + tree_shift(away, k // 4, (4 - k % 4) % 4).astype(F32)
    g_scores, side_out, _ = after(g_kv_b, g_scores, side_out)
    g_q_rows = dot(g_scores, keys) * score_scale
    g_q = [
        jnp.concatenate(
            [turn_back(g_q_rows[TOKENS * h : TOKENS * (h + 1)], cos, sin) for h in (2 * i, 2 * i + 1)],
            axis=1,
        ).astype(BF)
        for i in (0, 1)
    ]
    g_k = turn_back(g_kv_own[:, :256], cos, sin).astype(BF)
    g_v = g_kv_own[:, 256:].astype(BF)
    g_k = pick(is_first, g_k[:, :128], g_k[:, 128:])
    g_v = pick(is_first, g_v[:, :128], g_v[:, 128:])
    d_one = None
    for i, (g, first, last) in enumerate(((g_q, 0, 512), (g_k, 512, 640), (g_v, 640, 768))):
        d = dot_tr(g[0], raw[0][:, first:last]) + dot_tr(g[1], raw[1][:, first:last])
        gi = dot_tr(d.astype(BF), put_inner).astype(BF)
        inner_at = 768 + 128 * i
        d = d + dot_tr(gi[:, :128], raw[0][:, inner_at : inner_at + 128])
        d = d + dot_tr(gi[:, 128:], raw[1][:, inner_at : inner_at + 128])
        d_one = d if d_one is None else d_one + d
    g_u_one = select_back(d_one, put_rows)
    norm_one_back, g_gain_one = norm_back(scale_one, n_one, gain_one_full, g_u_one)
    grad_hidden = (g_after + norm_one_back).astype(BF)

    def to_owners(own, away):
        summed = (own + other_core(away.astype(BF)).astype(F32)).astype(BF)
        return jnp.sum(exchange(summed.reshape(64, 24, -1), CHIPS).astype(F32), axis=0)

    def both_halves(owned):
        mine, away = pick(is_first, owned[:12], owned[12:])
        return pick(is_first, mine, other_core(away.astype(BF)).astype(F32))

    left, right = pick(is_first, gb_down[:, :640], gb_down[:, 512:])
    owned_out = to_owners(
        dot_tl(side_out, g_half[0]) + dot_tl(put_inner_down, left),
        dot_tl(side_out, g_half[1]) + dot_tl(put_inner_down, right),
    )
    left, right = both_halves(owned_out)
    own_out = jnp.concatenate([left, right[:, 128:]], axis=1)
    d = dot_tr(own_out[:8, :640].astype(BF), pick(is_first, *raw_out)[0][:, :640]) + dot_tr(
        own_out[:8, 640:].astype(BF), pick(is_first, *raw_out)[1][:, 128:640]
    )
    ga_out_own = dot_tr(d.astype(BF), put_inner_out)
    ga_out_own = jnp.concatenate(pick(is_first, ga_out_own[:, :128], ga_out_own[:, 128:]), axis=1)

    nines = jnp.arange(9, dtype=jnp.int32)[:, None] == features[None, :] % 9
    loss_high, loss_rest = split_in_two(loss_here)
    loss_mid, loss_low = split_in_two(loss_here - loss_high.astype(F32))
    at_marks = (j == 11).astype(BF)[None, :]
    more_side = jnp.concatenate(
        [
            dot(jnp.where(nines, g_gain_one, 0.0).astype(BF), put_marks).astype(BF),
            dot(jnp.where(nines, g_gain_two, 0.0).astype(BF), put_marks).astype(BF),
            loss_high * at_marks,
            loss_mid * at_marks,
            loss_low * at_marks,
            jnp.zeros((11, 1536), BF),
        ],
        axis=0,
    )
    lines = jnp.arange(32, dtype=jnp.int32)
    line_at = jnp.where(lines < 18, lines, jnp.where(lines < 21, lines + 3 * core, -1))
    more_grad = table(line_at, jnp.arange(512, dtype=jnp.int32))
    side_q = jnp.concatenate([sides[0], more_side], axis=0)
    sums = [
        jnp.concatenate(
            [
                dot_tl(side_q, jnp.concatenate([g_q[i], more_grad], axis=0)),
                dot_tl(sides[1], g_k[i]),
                dot_tl(sides[2], g_v[i]),
            ],
            axis=1,
        )
        for i in (0, 1)
    ]
    owned = to_owners(sums[0], sums[1])
    loss_value = jnp.sum(owned[11, 18:24]) / (1152.0 * valid_count)
    left, right = both_halves(owned)
    gains = left[11]
    left_b, right_b = left.astype(BF), right.astype(BF)
    mine_b, other_b = pick(is_first, left_b, right_b)
    ga_own = []
    for first, last in ((0, 512), (512, 640), (640, 768)):
        d = dot_tr(mine_b[:, first:last], raw[0][:, first:last]) + dot_tr(
            other_b[:, first:last], raw[1][:, first:last]
        )
        g = dot_tr(d.astype(BF), put_inner)[:9]
        ga_own.append(jnp.concatenate(pick(is_first, g[:, :128], g[:, 128:]), axis=1))

    def columns(first, last, rows):
        return jnp.concatenate([left[rows, first:last], right[rows, first:last]], axis=1)

    top_rows, low_rows = slice(0, 9), slice(9, 11)

    return (
        result.astype(BF)[None],
        loss_value,
        grad_hidden[None],
        gains[:9],
        columns(0, 512, top_rows),
        columns(512, 640, top_rows),
        columns(640, 768, top_rows),
        own_out[:8],
        ga_own[0],
        columns(0, 512, low_rows),
        ga_own[1],
        columns(512, 640, low_rows),
        ga_own[2],
        columns(640, 768, low_rows),
        ga_out_own,
        own_out[8:10],
        gains[9:18],
        wide[:9],
        wide[9:18],
        gw_down_own.astype(F32),
        ga[:, :256],
        wide[18:20],
        ga[:, 256:],
        wide[20:],
        ga_down_own,
        own_out[10:],
    )


def solution(mesh):
    mesh = Mesh(mesh.devices.reshape([SIZES[a] for a in EVERY]), EVERY)
    tree, seq = ("z", "xl"), ("xh", "y", "c")
    rows = P(EVERY, None)
    vector = P(EVERY)
    return jax.shard_map(
        on_device,
        mesh=mesh,
        in_specs=(
            P(tree, seq, None),
            P(tree, None),
            P(tree, None),
            P(tree, seq),
            P(tree, seq, None),
            vector,
        )
        + (rows,) * 12
        + (vector,)
        + (rows,) * 9,
        out_specs=(P(tree, seq, None), P(), P(tree, seq, None), vector)
        + (rows,) * 12
        + (vector,)
        + (rows,) * 9,
        check_vma=False,
    )
```

```python
import jax
import jax.numpy as jnp
from jax import lax
from jax.sharding import Mesh, PartitionSpec as P

EPSILON = 1e-06
ROPE_BASE = 10000.0
MASKED_SCORE = -1e30
BF = jnp.bfloat16
F32 = jnp.float32

CHIPS = ("z", "xl", "xh", "y")
EVERY = ("z", "xl", "xh", "y", "c")
SIZES = dict(z=4, xl=2, xh=2, y=4, c=2)
RING = dict(z="z", x=("xl", "xh"), y="y")
TOKENS = 160
HEADS = 4
WIDTH = 256


def dot(a, b):
    return jnp.dot(a, b, preferred_element_type=F32)


def dot_tl(a, b):
    return lax.dot_general(a, b, (((0,), (0,)), ((), ())), preferred_element_type=F32)


def dot_tr(a, b):
    return lax.dot_general(a, b, (((1,), (1,)), ((), ())), preferred_element_type=F32)


def exchange(x, axes):
    return lax.all_to_all(x, axes, split_axis=0, concat_axis=0, tiled=True)


def gather_chips(x):
    return exchange(jnp.broadcast_to(x[None], (64,) + x.shape), CHIPS)


def other_core(x):
    return lax.ppermute(x, "c", [(0, 1), (1, 0)])


def shift(x, axis, k):
    number = [0, 2, 1, 3] if axis == "x" else [0, 1, 2, 3]
    return lax.ppermute(x, RING[axis], [(number[i], number[(i + k) % 4]) for i in range(4)])


def pick(cond, a, b):
    return jnp.where(cond, a, b), jnp.where(cond, b, a)


def split_in_two(x):
    high = x.astype(BF)
    return high, (x - high.astype(F32)).astype(BF)


def select_back(x, table):
    high, low = split_in_two(x)
    return dot_tr(high, table) + dot_tr(low, table)


def down_route():
    pairs = []
    for o in range(16):
        for t in range(8):
            pairs.append((8 * o + t, 8 * (8 * (o % 2) + t) + o // 2))
    return pairs


def gather_line(x, axis):
    return jnp.stack([x] + [shift(x, axis, k) for k in (1, 2, 3)])


def norm_parts(values, gain):
    scale = lax.rsqrt(jnp.mean(values * values, axis=-1, keepdims=True) + EPSILON)
    n = values * scale
    return scale, n, (n * (1.0 + gain)).astype(BF)


def norm_back(scale, n, gain, grad):
    m = grad * (1.0 + gain)
    back = scale * (m - n * jnp.mean(m * n, axis=-1, keepdims=True))
    return back, jnp.sum(grad * n, axis=0, keepdims=True)


def turn(x, cos, sin):
    h = cos.shape[-1]
    a, b = x[:, :h], x[:, h:]
    return jnp.concatenate([a * cos - b * sin, b * cos + a * sin], axis=-1)


def turn_back(x, cos, sin):
    return turn(x, cos, -sin)


def gather_tokens(x):
    mine = [x] + [shift(x, "y", k) for k in (1, 2, 3)]
    return jnp.concatenate(mine + [other_core(p) for p in mine], axis=0)


def scatter_tokens(part):
    blocks = part.reshape(2, 4, TOKENS, -1)
    total = None
    for k in (2, 1, 3, 0):
        piece = blocks[0, k] + other_core(blocks[1, k].astype(BF)).astype(F32)
        if k:
            piece = shift(piece.astype(BF), "y", 4 - k).astype(F32)
        total = piece if total is None else total + piece
    return total


def after(done, *values):
    return lax.optimization_barrier(values + (done,))


def table(rows, columns):
    return (rows[:, None] == columns[None, :]).astype(BF)


def on_device(
    layer_input,
    segment,
    position,
    loss_token_mask,
    teacher,
    gain_one,
    wq,
    wk,
    wv,
    wo,
    aq,
    bq,
    ak,
    bk,
    av,
    bv,
    ao,
    bo,
    gain_two,
    wg,
    wu,
    wd,
    ag,
    bg,
    au,
    bu,
    ad,
    bd,
):
    core = lax.axis_index("c")
    at_z, at_y = lax.axis_index("z"), lax.axis_index("y")
    at_xl, at_xh = lax.axis_index("xl"), lax.axis_index("xh")
    at_x = 2 * at_xh + at_xl
    is_first = core == 0
    score_scale = WIDTH**-0.5
    count_here = jnp.sum(loss_token_mask[0]).astype(BF)

    extra = jnp.concatenate([gain_one[None], gain_two[None], count_here.reshape(1, 1)], axis=1)
    extra = jnp.pad(extra, ((0, 1), (0, 384 - 19)))

    def attention_half(k):
        top = jnp.concatenate(
            [m[:, m.shape[1] // 2 * k : m.shape[1] // 2 * (k + 1)] for m in (wq, wk, wv, aq, ak, av)],
            axis=1,
        )
        low = jnp.concatenate(
            [m[:, m.shape[1] // 2 * k : m.shape[1] // 2 * (k + 1)] for m in (bq, bk, bv)] + [extra],
            axis=1,
        )
        return jnp.concatenate([top, low, jnp.zeros((1, 1152), BF)], axis=0)

    keep, send = pick(is_first, attention_half(0), attention_half(1))
    lower, upper = pick(is_first, keep, other_core(send))
    att_own = jnp.concatenate([lower, upper], axis=0)
    raw_one = gather_chips(att_own)
    raw_two = other_core(raw_one)
    (layer_input, wg, wu, bg, bu, wd, ad, ag, au, wo, ao, bo, bd, segment, position, core, at_z, _) = after(
        att_own,
        layer_input, wg, wu, bg, bu, wd, ad, ag, au, wo, ao, bo, bd, segment, position, core, at_z,
    )
    is_first = core == 0
    hidden = layer_input[0].astype(F32)
    marks = raw_one.reshape(128, 12, 1152)[:, 9, 768:896]
    gain_one_full = marks[:, :9].reshape(1, 1152).astype(F32)
    gain_two_full = marks[:, 9:18].reshape(1, 1152).astype(F32)
    valid_count = jnp.sum(marks[:, 18].astype(F32))
    raw = [raw_one.reshape(1536, 1152), raw_two.reshape(1536, 1152)]

    def output_half(k):
        wide = jnp.concatenate([m[:, 512 * k : 512 * k + 640] for m in (wo, bo, bd)], axis=0)
        narrow = jnp.pad(ao[:, 128 * k : 128 * k + 128], ((0, 4), (0, 0)))
        return jnp.concatenate([wide, narrow, jnp.pad((ag, au)[k], ((0, 3), (0, 0)))], axis=1)

    keep, send = pick(is_first, output_half(0), output_half(1))
    lower, upper = pick(is_first, keep, other_core(send))
    out_own = jnp.concatenate([lower, upper], axis=0)

    rows22 = jnp.pad(jnp.concatenate([wg, wu, bg, bu], axis=0), ((0, 2), (0, 0)))
    rows22 = jnp.concatenate([rows22[:, 864 * t : 864 * (t + 1)] for t in range(8)], axis=0)
    wider = jnp.arange(896, dtype=jnp.int32)
    wider = table(jnp.arange(864, dtype=jnp.int32), jnp.where(wider % 56 < 54, wider // 56 * 54 + wider % 56, -1))
    slab = exchange(dot(rows22, wider).astype(BF).reshape(8, 24, 896), ("y", "c"))
    row = jnp.arange(176, dtype=jnp.int32)
    low = row - 144
    at_row = jnp.where(
        row < 72,
        row // 9 * 24 + row % 9,
        jnp.where(
            row < 144,
            (row - 72) // 9 * 24 + 9 + (row - 72) % 9,
            low % 16 // 2 * 24 + 18 + low // 16 * 2 + low % 2,
        ),
    )
    ff_own = dot(table(at_row, jnp.arange(192, dtype=jnp.int32)), slab.reshape(192, 896)).astype(BF)
    down_own = lax.ppermute(
        jnp.pad(jnp.concatenate([wd, ad], axis=1), ((0, 2), (0, 0))), EVERY, down_route()
    )
    down_line = gather_line(down_own, "z")
    down_line, _ = after(raw_one, down_line)
    down_lines = [down_line] + [shift(down_line, "x", k) for k in (1, 2, 3)]

    ids = jnp.arange(1536, dtype=jnp.int32)
    dev, j = 2 * (ids // 24) + (ids % 24) // 12, ids % 12
    halves = jnp.arange(256, dtype=jnp.int32)
    inner_ids = jnp.where(halves < 128, 128 * core + halves, 128 * (1 - core) + halves - 128)
    heads_at = jnp.arange(1024, dtype=jnp.int32)
    head_ids = jnp.where(heads_at < 512, 512 * core + heads_at, 512 * (1 - core) + heads_at - 512)
    features = jnp.arange(1152, dtype=jnp.int32)
    put_rows = table(features, jnp.where(j < 9, 9 * dev + j, -1))
    put_inner = table(inner_ids, jnp.where((j >= 9) & (j < 11), 2 * dev + j - 9, -1))
    put_marks = table(features // 9, jnp.where(j == 11, dev, -1))
    put_mix = table(head_ids, jnp.where(j < 8, 8 * dev + j, -1))
    put_inner_out = table(inner_ids, jnp.where((j >= 8) & (j < 10), 2 * dev + j - 8, -1))
    put_inner_down = table(halves, jnp.where(j >= 10, 2 * dev + j - 10, -1))

    def plane(block):
        kx, kz = block // 4, block % 4
        x = (at_x - kx) % 4
        return (((at_z - kz) % 4) * 2 + x % 2) * 2 + x // 2

    hidden_ids = jnp.arange(896, dtype=jnp.int32)
    put_down = table(hidden_ids, 56 * plane(hidden_ids // 56) + hidden_ids % 56)

    seq = (at_xh * 4 + at_y) * 2 + core
    tree_seg = segment[0]
    tree_pos = position[0]
    own_seg = lax.dynamic_slice_in_dim(tree_seg, seq * TOKENS, TOKENS)
    own_pos = lax.dynamic_slice_in_dim(tree_pos, seq * TOKENS, TOKENS)
    freq = ROPE_BASE ** (-(jnp.arange(128, dtype=F32) * 2.0 / WIDTH))
    angles = own_pos.astype(F32)[:, None] * freq[None, :]
    cos, sin = jnp.cos(angles), jnp.sin(angles)
    back = jnp.arange(16, dtype=jnp.int32)
    block_at = (((at_xh - (back % 8) // 4) % 2) * 4 + (at_y - back % 4) % 4) * 2 + jnp.where(
        back < 8, core, 1 - core
    )
    chosen = (block_at[:, None] == back[None, :]).astype(jnp.int32)[:, :, None]
    key_seg = jnp.sum(chosen * tree_seg.reshape(1, 16, TOKENS), axis=1).reshape(1, 2560)
    key_pos = jnp.sum(chosen * tree_pos.reshape(1, 16, TOKENS), axis=1).reshape(1, 2560)
    q_seg, q_pos = own_seg[:, None], own_pos[:, None]
    parent = (key_seg >= 1) & (key_seg <= 4) & (q_seg >= 5) & ((q_seg - 5) // 2 + 1 == key_seg)
    allowed = ((key_seg == q_seg) | (key_seg == 0) | parent) & (key_pos <= q_pos)
    allowed = jnp.concatenate([allowed] * HEADS, axis=0)

    scale_one, n_one, u_one = norm_parts(hidden, gain_one_full)
    u_rows = dot(u_one, put_rows).astype(BF)
    inner = [dot(u_rows, raw[i][:, 768:]).astype(BF) for i in (0, 1)]
    sides = []
    for i in range(3):
        part = jnp.concatenate([inner[0][:, 128 * i : 128 * i + 128], inner[1][:, 128 * i : 128 * i + 128]], axis=1)
        sides.append(u_rows + dot(part, put_inner).astype(BF))
    kk = pick(is_first, *[dot(sides[1], raw[i][:, 512:640]) for i in (0, 1)])
    vv = pick(is_first, *[dot(sides[2], raw[i][:, 640:768]) for i in (0, 1)])
    kv_own = jnp.concatenate([turn(jnp.concatenate(kk, axis=1), cos, sin), vv[0], vv[1]], axis=1).astype(BF)

    def tree_shift(x, kh, ky):
        route = []
        for h in range(2):
            for y in range(4):
                route.append((4 * h + y, 4 * ((h + kh) % 2) + (y + ky) % 4))
        return lax.ppermute(x, ("xh", "y"), route)

    out_own, _ = after(kv_own, out_own)
    out_one = gather_chips(out_own)
    out_two = other_core(out_one)
    raw_out = [out_one.reshape(1536, 1024), out_two.reshape(1536, 1024)]
    kv_mine = [kv_own] + [tree_shift(kv_own, k // 4, k % 4) for k in range(1, 8)]
    kv_mine = jnp.concatenate(kv_mine, axis=0)
    kv = jnp.concatenate([kv_mine, other_core(kv_mine)], axis=0)
    keys, values = kv[:, :256], kv[:, 256:]
    ff_own, _ = after(kv, ff_own)
    ff_all = exchange(jnp.broadcast_to(ff_own[None], (16, 176, 896)), ("z", "xl", "xh"))
    queries = [dot(sides[0], raw[i][:, :512]) for i in (0, 1)]
    q_rows = jnp.concatenate(
        [turn(queries[h // 2][:, WIDTH * (h % 2) : WIDTH * (h % 2 + 1)], cos, sin) for h in range(HEADS)],
        axis=0,
    ).astype(BF)
    scores = jnp.where(allowed, dot_tr(q_rows, keys) * score_scale, MASKED_SCORE)
    top = jnp.max(scores, axis=-1, keepdims=True)
    ex = jnp.exp(scores - top)
    total = jnp.sum(ex, axis=-1, keepdims=True)
    lse = top + jnp.log(total)
    mix_rows = dot((ex / total).astype(BF), values).astype(BF)
    mix = jnp.concatenate([mix_rows[TOKENS * h : TOKENS * (h + 1)] for h in range(HEADS)], axis=1)
    mix_placed = dot(mix, put_mix).astype(BF)
    inner_out = jnp.concatenate([dot(mix_placed, raw_out[i][:, 640:768]) for i in (0, 1)], axis=1).astype(BF)
    side_out = mix_placed + dot(inner_out, put_inner_out).astype(BF)
    left, right = pick(is_first, *[dot(side_out, raw_out[i][:, :640]) for i in (0, 1)])
    after_att = hidden + jnp.concatenate([left, right[:, 128:]], axis=1)

    scale_two, n_two, u_two = norm_parts(after_att, gain_two_full)
    u_all = gather_tokens(u_two)

    ff_all, down_lines, _ = after(u_two, ff_all, down_lines)
    down_raw = jnp.concatenate(down_lines, axis=0).reshape(896, 1408)
    a_gate, a_up = pick(is_first, *[dot(put_rows, raw_out[i][:, 768:]).astype(BF) for i in (0, 1)])
    b_gate = ff_all[:, 144:160].reshape(256, 896)
    b_up = ff_all[:, 160:].reshape(256, 896)
    w_gate = (ff_all[:, :72].reshape(1152, 896).astype(F32) + dot(a_gate, b_gate)).astype(BF)
    w_up = (ff_all[:, 72:144].reshape(1152, 896).astype(F32) + dot(a_up, b_up)).astype(BF)
    left, right = pick(is_first, *[dot(put_inner_down, raw_out[i][:, :640]).astype(BF) for i in (0, 1)])
    b_down = jnp.concatenate([left, right[:, 128:]], axis=1)
    a_down = dot(put_down, down_raw[:, 1152:]).astype(BF)
    w_down = (dot(put_down, down_raw[:, :1152]) + dot(a_down, b_down)).astype(BF)

    gate = dot(u_all, w_gate)
    up = dot(u_all, w_up)
    act, act_pull = jax.vjp(lambda g, u: jax.nn.gelu(g, approximate=True) * u, gate, up)
    act = act.astype(BF)
    result = after_att + scatter_tokens(dot(act, w_down))

    valid = loss_token_mask[0].astype(F32)[:, None]
    error = result - teacher[0].astype(F32)
    loss_here = jnp.sum(valid * error * error)
    grad_result = 2.0 * 20480.0 / valid_count * valid * error

    g_all = gather_tokens(grad_result.astype(BF))
    g_act = dot_tr(g_all, w_down).astype(BF)
    g_gate, g_up = act_pull(g_act.astype(F32))
    g_gate, g_up = g_gate.astype(BF), g_up.astype(BF)
    g_u_part = dot_tr(g_gate, w_gate) + dot_tr(g_up, w_up)
    g_u_two = scatter_tokens(g_u_part)
    u_all, act, g_all, g_gate, g_up, _ = after(g_u_part, u_all, act, g_all, g_gate, g_up)
    gw_gate = dot_tl(u_all, g_gate).astype(BF)
    gw_up = dot_tl(u_all, g_up).astype(BF)
    gb_gate = dot_tl(a_gate, gw_gate).astype(BF)
    gb_up = dot_tl(a_up, gw_up).astype(BF)
    ff_grads = jnp.concatenate(
        [
            gw_gate.reshape(16, 72, 896),
            gw_up.reshape(16, 72, 896),
            gb_gate.reshape(16, 16, 896),
            gb_up.reshape(16, 16, 896),
        ],
        axis=1,
    )
    ff_parts = exchange(ff_grads, ("z", "xl", "xh"))
    gw_down = dot_tl(act, g_all).astype(BF)
    gb_down = dot_tl(a_down, gw_down).astype(BF)
    gw_down = dot_tl(put_down, gw_down).astype(BF)
    down_pieces = gw_down.reshape(4, 4, 56, 1152)
    down_first = [down_pieces[0]] + [shift(down_pieces[k], "x", 4 - k) for k in (1, 2, 3)]

    norm_two_back, g_gain_two = norm_back(scale_two, n_two, gain_two_full, g_u_two)
    g_after = grad_result + norm_two_back
    g_after_b = g_after.astype(BF)
    once = jnp.where(jnp.arange(640) < 128, 0, 1).astype(BF)[None]
    g_half = pick(is_first, g_after_b[:, :640], g_after_b[:, 512:])
    g_once = pick(is_first, g_after_b[:, :640], g_after_b[:, 512:] * once)
    d_out = dot_tr(g_once[0], raw_out[0][:, :640]) + dot_tr(g_once[1], raw_out[1][:, :640])
    gi_out = dot_tr(d_out.astype(BF), put_inner_out).astype(BF)
    d_out = (
        d_out
        + dot_tr(gi_out[:, :128], raw_out[0][:, 640:768])
        + dot_tr(gi_out[:, 128:], raw_out[1][:, 640:768])
    )
    g_mix = dot_tr(d_out.astype(BF), put_mix).astype(BF)
    g_rows = jnp.concatenate([g_mix[:, WIDTH * h : WIDTH * (h + 1)] for h in range(HEADS)], axis=0)
    scores_again = jnp.where(allowed, dot_tr(q_rows, keys) * score_scale, MASKED_SCORE)
    probs = jnp.where(allowed, jnp.exp(scores_again - lse), 0.0)
    g_probs = dot_tr(g_rows, values)
    g_scores = (probs * (g_probs - jnp.sum(probs * g_probs, axis=-1, keepdims=True))).astype(BF)
    g_keys = dot_tl(g_scores, q_rows) * score_scale
    g_values = dot_tl(probs.astype(BF), g_rows)
    g_kv = jnp.concatenate([g_keys, g_values], axis=1)
    n_mine = 8 * TOKENS
    g_kv_sum = g_kv[:n_mine] + other_core(g_kv[n_mine:].astype(BF)).astype(F32)
    g_kv_b = g_kv_sum.astype(BF)
    g_kv_own = g_kv_sum[:TOKENS]
    for k in range(1, 8):
        away = g_kv_b[TOKENS * k : TOKENS * (k + 1)]
        g_kv_own = g_kv_own + tree_shift(away, k // 4, (4 - k % 4) % 4).astype(F32)
    g_scores, side_out, ff_parts, down_first, gb_down, _ = after(
        g_kv_b, g_scores, side_out, ff_parts, down_first, gb_down
    )
    g_q_rows = dot(g_scores, keys) * score_scale
    g_q = [
        jnp.concatenate(
            [turn_back(g_q_rows[TOKENS * h : TOKENS * (h + 1)], cos, sin) for h in (2 * i, 2 * i + 1)],
            axis=1,
        ).astype(BF)
        for i in (0, 1)
    ]
    down_line = sum(m.astype(F32) for m in down_first).astype(BF)
    down_second = [down_line[0]] + [shift(down_line[k], "z", 4 - k) for k in (1, 2, 3)]
    ff_sum = jnp.sum(ff_parts.astype(F32), axis=0).astype(BF)
    ga_part = jnp.concatenate(
        [dot_tr(ff_sum[:72], b_gate), dot_tr(ff_sum[72:144], b_up), jnp.zeros((72, 384), F32)], axis=1
    ).astype(BF)
    back_row = jnp.arange(256, dtype=jnp.int32)
    group, line = back_row // 32, back_row % 32
    take = jnp.where(
        line < 9,
        9 * group + line,
        jnp.where(
            line < 18,
            72 + 9 * group + line - 9,
            jnp.where(
                line < 22,
                144 + 16 * ((line - 18) // 2) + 2 * group + line % 2,
                jnp.where(line < 31, 176 + 9 * group + line - 22, -1),
            ),
        ),
    )
    leaving = dot(
        table(take, jnp.arange(248, dtype=jnp.int32)), jnp.concatenate([ff_sum, ga_part], axis=0)
    ).astype(BF)
    slab = exchange(leaving.reshape(8, 32, 896), ("y", "c"))
    g_k = turn_back(g_kv_own[:, :256], cos, sin).astype(BF)
    g_v = g_kv_own[:, 256:].astype(BF)
    g_k = pick(is_first, g_k[:, :128], g_k[:, 128:])
    g_v = pick(is_first, g_v[:, :128], g_v[:, 128:])
    d_one = None
    for i, (g, first, last) in enumerate(((g_q, 0, 512), (g_k, 512, 640), (g_v, 640, 768))):
        d = dot_tr(g[0], raw[0][:, first:last]) + dot_tr(g[1], raw[1][:, first:last])
        gi = dot_tr(d.astype(BF), put_inner).astype(BF)
        inner_at = 768 + 128 * i
        d = d + dot_tr(gi[:, :128], raw[0][:, inner_at : inner_at + 128])
        d = d + dot_tr(gi[:, 128:], raw[1][:, inner_at : inner_at + 128])
        d_one = d if d_one is None else d_one + d
    g_u_one = select_back(d_one, put_rows)
    norm_one_back, g_gain_one = norm_back(scale_one, n_one, gain_one_full, g_u_one)
    grad_hidden = (g_after + norm_one_back).astype(BF)

    def of_chip(own, away):
        return (own.astype(F32) + other_core(away.astype(BF)).astype(F32)).astype(BF).reshape(64, 24, -1)

    def both_halves(owned):
        mine, away = pick(is_first, owned[:12], owned[12:])
        return pick(is_first, mine, other_core(away.astype(BF)).astype(F32))

    left, right = pick(is_first, gb_down[:, :640], gb_down[:, 512:])
    chip_out = of_chip(
        dot_tl(side_out, g_half[0]) + dot_tl(put_inner_down, left),
        dot_tl(side_out, g_half[1]) + dot_tl(put_inner_down, right),
    )
    nines = jnp.arange(9, dtype=jnp.int32)[:, None] == features[None, :] % 9
    loss_high, loss_rest = split_in_two(loss_here)
    loss_mid, loss_low = split_in_two(loss_here - loss_high.astype(F32))
    at_marks = (j == 11).astype(BF)[None, :]
    more_side = jnp.concatenate(
        [
            dot(jnp.where(nines, g_gain_one, 0.0).astype(BF), put_marks).astype(BF),
            dot(jnp.where(nines, g_gain_two, 0.0).astype(BF), put_marks).astype(BF),
            loss_high * at_marks,
            loss_mid * at_marks,
            loss_low * at_marks,
            jnp.zeros((11, 1536), BF),
        ],
        axis=0,
    )
    lines = jnp.arange(32, dtype=jnp.int32)
    line_at = jnp.where(lines < 18, lines, jnp.where(lines < 21, lines + 3 * core, -1))
    more_grad = table(line_at, jnp.arange(512, dtype=jnp.int32))
    side_q = jnp.concatenate([sides[0], more_side], axis=0)
    sums = [
        jnp.concatenate(
            [
                dot_tl(side_q, jnp.concatenate([g_q[i], more_grad], axis=0)).astype(BF),
                dot_tl(sides[1], g_k[i]).astype(BF),
                dot_tl(sides[2], g_v[i]).astype(BF),
            ],
            axis=1,
        )
        for i in (0, 1)
    ]
    chip_sums = jnp.concatenate([of_chip(sums[0], sums[1]), chip_out], axis=2)
    parts = exchange(chip_sums, CHIPS)
    slab, down_second, _ = after(chip_sums, slab, down_second)

    narrow = dot_tr(slab.reshape(256, 896), wider).reshape(8, 32, 864)
    wide = jnp.concatenate([narrow[t] for t in range(8)], axis=1)
    ga = jnp.sum(slab[:, 22:31, :512].astype(F32), axis=0)
    down_sum = sum(m.astype(F32) for m in down_second).astype(BF)
    gw_down_own = lax.ppermute(down_sum, EVERY, [(b, a) for a, b in down_route()])[:54]
    ga_down_own = dot_tr(gw_down_own, b_down)
    all_owned = jnp.sum(parts.astype(F32), axis=0)
    owned, owned_out = all_owned[:, :768], all_owned[:, 768:]
    left, right = both_halves(owned_out)
    own_out = jnp.concatenate([left, right[:, 128:]], axis=1)
    d = dot_tr(own_out[:8, :640].astype(BF), pick(is_first, *raw_out)[0][:, :640]) + dot_tr(
        own_out[:8, 640:].astype(BF), pick(is_first, *raw_out)[1][:, 128:640]
    )
    ga_out_own = dot_tr(d.astype(BF), put_inner_out)
    ga_out_own = jnp.concatenate(pick(is_first, ga_out_own[:, :128], ga_out_own[:, 128:]), axis=1)
    loss_value = jnp.sum(owned[11, 18:24]) / (1152.0 * valid_count)
    left, right = both_halves(owned)
    gains = left[11]
    left_b, right_b = left.astype(BF), right.astype(BF)
    mine_b, other_b = pick(is_first, left_b, right_b)
    ga_own = []
    for first, last in ((0, 512), (512, 640), (640, 768)):
        d = dot_tr(mine_b[:, first:last], raw[0][:, first:last]) + dot_tr(
            other_b[:, first:last], raw[1][:, first:last]
        )
        g = dot_tr(d.astype(BF), put_inner)[:9]
        ga_own.append(jnp.concatenate(pick(is_first, g[:, :128], g[:, 128:]), axis=1))

    def columns(first, last, rows):
        return jnp.concatenate([left[rows, first:last], right[rows, first:last]], axis=1)

    top_rows, low_rows = slice(0, 9), slice(9, 11)

    return (
        result.astype(BF)[None],
        loss_value,
        grad_hidden[None],
        gains[:9],
        columns(0, 512, top_rows),
        columns(512, 640, top_rows),
        columns(640, 768, top_rows),
        own_out[:8],
        ga_own[0],
        columns(0, 512, low_rows),
        ga_own[1],
        columns(512, 640, low_rows),
        ga_own[2],
        columns(640, 768, low_rows),
        ga_out_own,
        own_out[8:10],
        gains[9:18],
        wide[:9],
        wide[9:18],
        gw_down_own.astype(F32),
        ga[:, :256],
        wide[18:20],
        ga[:, 256:],
        wide[20:22],
        ga_down_own,
        own_out[10:],
    )


def solution(mesh):
    mesh = Mesh(mesh.devices.reshape([SIZES[a] for a in EVERY]), EVERY)
    tree, seq = ("z", "xl"), ("xh", "y", "c")
    rows = P(EVERY, None)
    vector = P(EVERY)
    return jax.shard_map(
        on_device,
        mesh=mesh,
        in_specs=(
            P(tree, seq, None),
            P(tree, None),
            P(tree, None),
            P(tree, seq),
            P(tree, seq, None),
            vector,
        )
        + (rows,) * 12
        + (vector,)
        + (rows,) * 9,
        out_specs=(P(tree, seq, None), P(), P(tree, seq, None), vector)
        + (rows,) * 12
        + (vector,)
        + (rows,) * 9,
        check_vma=False,
    )
```

```python
import jax
import jax.numpy as jnp
from jax import lax
from jax.sharding import Mesh, PartitionSpec as P

EPSILON = 1e-06
ROPE_BASE = 10000.0
MASKED_SCORE = -1e30
BF = jnp.bfloat16
F32 = jnp.float32

CHIPS = ("z", "xl", "xh", "y")
EVERY = ("z", "xl", "xh", "y", "c")
SIZES = dict(z=4, xl=2, xh=2, y=4, c=2)
RING = dict(z="z", x=("xl", "xh"), y="y")
TOKENS = 160
HEADS = 4
WIDTH = 256


def dot(a, b):
    return jnp.dot(a, b, preferred_element_type=F32)


def dot_tl(a, b):
    return lax.dot_general(a, b, (((0,), (0,)), ((), ())), preferred_element_type=F32)


def dot_tr(a, b):
    return lax.dot_general(a, b, (((1,), (1,)), ((), ())), preferred_element_type=F32)


def exchange(x, axes):
    return lax.all_to_all(x, axes, split_axis=0, concat_axis=0, tiled=True)


def gather_chips(x):
    return exchange(jnp.broadcast_to(x[None], (64,) + x.shape), CHIPS)


def other_core(x):
    return lax.ppermute(x, "c", [(0, 1), (1, 0)])


def other_half(x):
    return lax.ppermute(x, "xh", [(0, 1), (1, 0)])


def shift(x, axis, k):
    number = [0, 2, 1, 3] if axis == "x" else [0, 1, 2, 3]
    return lax.ppermute(x, RING[axis], [(number[i], number[(i + k) % 4]) for i in range(4)])


def pick(cond, a, b):
    return jnp.where(cond, a, b), jnp.where(cond, b, a)


def split_in_two(x):
    high = x.astype(BF)
    return high, x - high.astype(F32)


def select_back(x, table):
    high, low = split_in_two(x)
    return dot_tr(high, table) + dot_tr(low.astype(BF), table)


def down_route():
    pairs = []
    for o in range(16):
        for t in range(8):
            pairs.append((8 * o + t, 8 * (8 * (o % 2) + t) + o // 2))
    return pairs


def gather_line(x, axis):
    return jnp.stack([x] + [shift(x, axis, k) for k in (1, 2, 3)])


def norm_parts(values, gain):
    scale = lax.rsqrt(jnp.mean(values * values, axis=-1, keepdims=True) + EPSILON)
    n = values * scale
    return scale, n, (n * (1.0 + gain)).astype(BF)


def norm_back(scale, n, gain, grad):
    m = grad * (1.0 + gain)
    back = scale * (m - n * jnp.mean(m * n, axis=-1, keepdims=True))
    return back, jnp.sum(grad * n, axis=0, keepdims=True)


def turn(x, cos, sin):
    h = cos.shape[-1]
    a, b = x[:, :h], x[:, h:]
    return jnp.concatenate([a * cos - b * sin, b * cos + a * sin], axis=-1)


def turn_back(x, cos, sin):
    return turn(x, cos, -sin)


def gather_tokens(x):
    mine = [x] + [shift(x, "y", k) for k in (1, 2, 3)]
    return jnp.concatenate(mine + [other_core(p) for p in mine], axis=0)


def scatter_tokens(part):
    blocks = part.reshape(2, 4, TOKENS, -1)
    total = None
    for k in (2, 1, 3, 0):
        piece = blocks[0, k] + other_core(blocks[1, k].astype(BF)).astype(F32)
        if k:
            piece = shift(piece.astype(BF), "y", 4 - k).astype(F32)
        total = piece if total is None else total + piece
    return total


def after(done, *values):
    return lax.optimization_barrier(values + (done,))


def table(rows, columns):
    return (rows[:, None] == columns[None, :]).astype(BF)


def on_device(
    layer_input,
    segment,
    position,
    loss_token_mask,
    teacher,
    gain_one,
    wq,
    wk,
    wv,
    wo,
    aq,
    bq,
    ak,
    bk,
    av,
    bv,
    ao,
    bo,
    gain_two,
    wg,
    wu,
    wd,
    ag,
    bg,
    au,
    bu,
    ad,
    bd,
):
    core = lax.axis_index("c")
    at_z, at_y = lax.axis_index("z"), lax.axis_index("y")
    at_xl, at_xh = lax.axis_index("xl"), lax.axis_index("xh")
    at_x = 2 * at_xh + at_xl
    is_first = core == 0
    score_scale = WIDTH**-0.5
    count_here = jnp.sum(loss_token_mask[0]).astype(BF)

    extra = jnp.concatenate([gain_one[None], gain_two[None], count_here.reshape(1, 1)], axis=1)
    extra = jnp.pad(extra, ((0, 1), (0, 384 - 19)))

    def attention_half(k):
        top = jnp.concatenate(
            [m[:, m.shape[1] // 2 * k : m.shape[1] // 2 * (k + 1)] for m in (wq, wk, wv, aq, ak, av)],
            axis=1,
        )
        low = jnp.concatenate(
            [m[:, m.shape[1] // 2 * k : m.shape[1] // 2 * (k + 1)] for m in (bq, bk, bv)] + [extra],
            axis=1,
        )
        return jnp.concatenate([top, low, jnp.zeros((1, 1152), BF)], axis=0)

    keep, send = pick(is_first, attention_half(0), attention_half(1))
    lower, upper = pick(is_first, keep, other_core(send))
    att_own = jnp.concatenate([lower, upper], axis=0)
    raw_one = gather_chips(att_own)
    raw_two = other_core(raw_one)
    (layer_input, wg, wu, bg, bu, wd, ad, ag, au, wo, ao, bo, bd, segment, position, core, at_z, _) = after(
        att_own,
        layer_input, wg, wu, bg, bu, wd, ad, ag, au, wo, ao, bo, bd, segment, position, core, at_z,
    )
    is_first = core == 0
    hidden = layer_input[0].astype(F32)
    marks = raw_one.reshape(128, 12, 1152)[:, 9, 768:896]
    gain_one_full = marks[:, :9].reshape(1, 1152).astype(F32)
    gain_two_full = marks[:, 9:18].reshape(1, 1152).astype(F32)
    valid_count = jnp.sum(marks[:, 18].astype(F32))
    raw = [raw_one.reshape(1536, 1152), raw_two.reshape(1536, 1152)]

    def output_half(k):
        wide = jnp.concatenate([m[:, 512 * k : 512 * k + 640] for m in (wo, bo, bd)], axis=0)
        narrow = jnp.pad(ao[:, 128 * k : 128 * k + 128], ((0, 4), (0, 0)))
        return jnp.concatenate([wide, narrow, jnp.pad((ag, au)[k], ((0, 3), (0, 0)))], axis=1)

    keep, send = pick(is_first, output_half(0), output_half(1))
    lower, upper = pick(is_first, keep, other_core(send))
    out_own = jnp.concatenate([lower, upper], axis=0)

    def column_of(k):
        return 2 * ((at_y + k // 2) % 4) + (core + k) % 2

    def column_shift(x, k):
        route = []
        for y in range(4):
            for c in range(2):
                route.append((2 * y + c, 2 * ((y + k // 2) % 4) + (c + k) % 2))
        return lax.ppermute(x, ("y", "c"), route)

    rows22 = jnp.pad(jnp.concatenate([wg, wu, bg, bu], axis=0), ((0, 2), (0, 0)))
    rows22 = jnp.concatenate([rows22[:, 864 * t : 864 * (t + 1)] for t in range(8)], axis=0)
    wider = jnp.arange(896, dtype=jnp.int32)
    wider = table(jnp.arange(864, dtype=jnp.int32), jnp.where(wider % 56 < 54, wider // 56 * 54 + wider % 56, -1))
    rows22 = dot(rows22, wider).astype(BF).reshape(8, 24, 896)
    slab = []
    for k in range(8):
        piece = lax.dynamic_index_in_dim(rows22, column_of(k), 0, keepdims=False)
        slab.append(column_shift(piece, k) if k else piece)
    slab = jnp.concatenate(slab, axis=0)
    back = jnp.arange(8, dtype=jnp.int32)
    sources = 2 * ((at_y - back // 2) % 4) + (core - back) % 2
    row = jnp.arange(176, dtype=jnp.int32)
    low = row - 144
    at_row = jnp.where(
        row < 72,
        row // 9 * 24 + row % 9,
        jnp.where(
            row < 144,
            (row - 72) // 9 * 24 + 9 + (row - 72) % 9,
            low % 16 // 2 * 24 + 18 + low // 16 * 2 + low % 2,
        ),
    )
    in_slab = jnp.arange(192, dtype=jnp.int32)
    in_slab = jnp.repeat(sources, 24) * 24 + in_slab % 24
    ff_own = dot(table(at_row, in_slab), slab).astype(BF)
    down_own = lax.ppermute(
        jnp.pad(jnp.concatenate([wd, ad], axis=1), ((0, 2), (0, 0))), EVERY, down_route()
    )
    down_line = gather_line(down_own, "z")
    down_line, _ = after(raw_one, down_line)
    down_lines = [down_line] + [shift(down_line, "x", k) for k in (1, 2, 3)]

    out_own, _ = after(raw_one, out_own)
    out_one = gather_chips(out_own)
    out_two = other_core(out_one)
    raw_out = [out_one.reshape(1536, 1024), out_two.reshape(1536, 1024)]
    ff_own, _ = after(out_one, ff_own)
    ff_all = exchange(jnp.broadcast_to(ff_own[None], (16, 176, 896)), ("z", "xl", "xh"))

    ids = jnp.arange(1536, dtype=jnp.int32)
    dev, j = 2 * (ids // 24) + (ids % 24) // 12, ids % 12
    halves = jnp.arange(256, dtype=jnp.int32)
    inner_ids = jnp.where(halves < 128, 128 * core + halves, 128 * (1 - core) + halves - 128)
    heads_at = jnp.arange(1024, dtype=jnp.int32)
    head_ids = jnp.where(heads_at < 512, 512 * core + heads_at, 512 * (1 - core) + heads_at - 512)
    features = jnp.arange(1152, dtype=jnp.int32)
    put_rows = table(features, jnp.where(j < 9, 9 * dev + j, -1))
    put_inner = table(inner_ids, jnp.where((j >= 9) & (j < 11), 2 * dev + j - 9, -1))
    put_marks = table(features // 9, jnp.where(j == 11, dev, -1))
    put_mix = table(head_ids, jnp.where(j < 8, 8 * dev + j, -1))
    put_inner_out = table(inner_ids, jnp.where((j >= 8) & (j < 10), 2 * dev + j - 8, -1))
    put_inner_down = table(halves, jnp.where(j >= 10, 2 * dev + j - 10, -1))

    def plane(block):
        kx, kz = block // 4, block % 4
        x = (at_x - kx) % 4
        return (((at_z - kz) % 4) * 2 + x % 2) * 2 + x // 2

    hidden_ids = jnp.arange(896, dtype=jnp.int32)
    put_down = table(hidden_ids, 56 * plane(hidden_ids // 56) + hidden_ids % 56)

    seq = (at_xh * 4 + at_y) * 2 + core
    tree_seg = segment[0]
    tree_pos = position[0]
    own_seg = lax.dynamic_slice_in_dim(tree_seg, seq * TOKENS, TOKENS)
    own_pos = lax.dynamic_slice_in_dim(tree_pos, seq * TOKENS, TOKENS)
    freq = ROPE_BASE ** (-(jnp.arange(128, dtype=F32) * 2.0 / WIDTH))
    angles = own_pos.astype(F32)[:, None] * freq[None, :]
    cos, sin = jnp.cos(angles), jnp.sin(angles)
    back = jnp.arange(16, dtype=jnp.int32)
    block_at = (((at_xh - (back % 8) // 4) % 2) * 4 + (at_y - back % 4) % 4) * 2 + jnp.where(
        back < 8, core, 1 - core
    )
    chosen = (block_at[:, None] == back[None, :]).astype(jnp.int32)[:, :, None]
    key_seg = jnp.sum(chosen * tree_seg.reshape(1, 16, TOKENS), axis=1).reshape(1, 2560)
    key_pos = jnp.sum(chosen * tree_pos.reshape(1, 16, TOKENS), axis=1).reshape(1, 2560)
    q_seg, q_pos = own_seg[:, None], own_pos[:, None]
    parent = (key_seg >= 1) & (key_seg <= 4) & (q_seg >= 5) & ((q_seg - 5) // 2 + 1 == key_seg)
    allowed = ((key_seg == q_seg) | (key_seg == 0) | parent) & (key_pos <= q_pos)
    allowed = jnp.concatenate([allowed] * HEADS, axis=0)

    scale_one, n_one, u_one = norm_parts(hidden, gain_one_full)
    u_rows = dot(u_one, put_rows).astype(BF)
    inner = [dot(u_rows, raw[i][:, 768:]).astype(BF) for i in (0, 1)]
    sides = []
    for i in range(3):
        part = jnp.concatenate([inner[0][:, 128 * i : 128 * i + 128], inner[1][:, 128 * i : 128 * i + 128]], axis=1)
        sides.append(u_rows + dot(part, put_inner).astype(BF))
    kk = pick(is_first, *[dot(sides[1], raw[i][:, 512:640]) for i in (0, 1)])
    vv = pick(is_first, *[dot(sides[2], raw[i][:, 640:768]) for i in (0, 1)])
    kv_own = jnp.concatenate([turn(jnp.concatenate(kk, axis=1), cos, sin), vv[0], vv[1]], axis=1).astype(BF)

    kv_line = gather_line(kv_own, "y").reshape(640, 512)
    kv_mine = jnp.concatenate([kv_line, other_half(kv_line)], axis=0)
    kv = jnp.concatenate([kv_mine, other_core(kv_mine)], axis=0)
    keys, values = kv[:, :256], kv[:, 256:]
    queries = [dot(sides[0], raw[i][:, :512]) for i in (0, 1)]
    q_rows = jnp.concatenate(
        [turn(queries[h // 2][:, WIDTH * (h % 2) : WIDTH * (h % 2 + 1)], cos, sin) for h in range(HEADS)],
        axis=0,
    ).astype(BF)
    scores = jnp.where(allowed, dot_tr(q_rows, keys) * score_scale, MASKED_SCORE)
    top = jnp.max(scores, axis=-1, keepdims=True)
    ex = jnp.exp(scores - top)
    total = jnp.sum(ex, axis=-1, keepdims=True)
    lse = top + jnp.log(total)
    mix_rows = dot((ex / total).astype(BF), values).astype(BF)
    mix = jnp.concatenate([mix_rows[TOKENS * h : TOKENS * (h + 1)] for h in range(HEADS)], axis=1)
    mix_placed = dot(mix, put_mix).astype(BF)
    inner_out = jnp.concatenate([dot(mix_placed, raw_out[i][:, 640:768]) for i in (0, 1)], axis=1).astype(BF)
    side_out = mix_placed + dot(inner_out, put_inner_out).astype(BF)
    left, right = pick(is_first, *[dot(side_out, raw_out[i][:, :640]) for i in (0, 1)])
    after_att = hidden + jnp.concatenate([left, right[:, 128:]], axis=1)

    scale_two, n_two, u_two = norm_parts(after_att, gain_two_full)
    u_all = gather_tokens(u_two)

    down_lines, _ = after(u_two, down_lines)
    down_raw = jnp.concatenate(down_lines, axis=0).reshape(896, 1408)
    left, right = pick(is_first, *[dot(put_inner_down, raw_out[i][:, :640]).astype(BF) for i in (0, 1)])
    b_down = jnp.concatenate([left, right[:, 128:]], axis=1)
    a_down = dot(put_down, down_raw[:, 1152:]).astype(BF)
    w_down = (dot(put_down, down_raw[:, :1152]) + dot(a_down, b_down)).astype(BF)
    a_gate, a_up = pick(is_first, *[dot(put_rows, raw_out[i][:, 768:]).astype(BF) for i in (0, 1)])
    ff_all, _ = after(w_down, ff_all)
    b_gate = ff_all[:, 144:160].reshape(256, 896)
    b_up = ff_all[:, 160:].reshape(256, 896)
    w_gate = (ff_all[:, :72].reshape(1152, 896).astype(F32) + dot(a_gate, b_gate)).astype(BF)
    w_up = (ff_all[:, 72:144].reshape(1152, 896).astype(F32) + dot(a_up, b_up)).astype(BF)

    gate = dot(u_all, w_gate)
    up = dot(u_all, w_up)
    act, act_pull = jax.vjp(lambda g, u: jax.nn.gelu(g, approximate=True) * u, gate, up)
    act = act.astype(BF)
    result = after_att + scatter_tokens(dot(act, w_down))

    valid = loss_token_mask[0].astype(F32)[:, None]
    error = result - teacher[0].astype(F32)
    loss_here = jnp.sum(valid * error * error)
    grad_result = 2.0 * 20480.0 / valid_count * valid * error

    g_all = gather_tokens(grad_result.astype(BF))
    g_act = dot_tr(g_all, w_down).astype(BF)
    g_gate, g_up = act_pull(g_act.astype(F32))
    g_gate, g_up = g_gate.astype(BF), g_up.astype(BF)
    g_u_part = dot_tr(g_gate, w_gate) + dot_tr(g_up, w_up)
    g_u_two = scatter_tokens(g_u_part)
    u_all, act, g_all, g_gate, g_up, _ = after(g_u_part, u_all, act, g_all, g_gate, g_up)
    gw_gate = dot_tl(u_all, g_gate).astype(BF)
    gw_up = dot_tl(u_all, g_up).astype(BF)
    gb_gate = dot_tl(a_gate, gw_gate).astype(BF)
    gb_up = dot_tl(a_up, gw_up).astype(BF)
    ff_grads = jnp.concatenate(
        [
            gw_gate.reshape(16, 72, 896),
            gw_up.reshape(16, 72, 896),
            gb_gate.reshape(16, 16, 896),
            gb_up.reshape(16, 16, 896),
        ],
        axis=1,
    )
    ff_parts = exchange(ff_grads, ("z", "xl", "xh"))
    gw_down = dot_tl(act, g_all).astype(BF)
    gb_down = dot_tl(a_down, gw_down).astype(BF)
    gw_down = dot_tl(put_down, gw_down).astype(BF)
    down_pieces = gw_down.reshape(4, 4, 56, 1152)
    down_first = [down_pieces[0]] + [shift(down_pieces[k], "x", 4 - k) for k in (1, 2, 3)]

    norm_two_back, g_gain_two = norm_back(scale_two, n_two, gain_two_full, g_u_two)
    g_after = grad_result + norm_two_back
    g_after_b = g_after.astype(BF)
    once = jnp.where(jnp.arange(640) < 128, 0, 1).astype(BF)[None]
    g_half = pick(is_first, g_after_b[:, :640], g_after_b[:, 512:])
    g_once = pick(is_first, g_after_b[:, :640], g_after_b[:, 512:] * once)
    d_out = dot_tr(g_once[0], raw_out[0][:, :640]) + dot_tr(g_once[1], raw_out[1][:, :640])
    gi_out = dot_tr(d_out.astype(BF), put_inner_out).astype(BF)
    d_out = (
        d_out
        + dot_tr(gi_out[:, :128], raw_out[0][:, 640:768])
        + dot_tr(gi_out[:, 128:], raw_out[1][:, 640:768])
    )
    g_mix = dot_tr(d_out.astype(BF), put_mix).astype(BF)
    g_rows = jnp.concatenate([g_mix[:, WIDTH * h : WIDTH * (h + 1)] for h in range(HEADS)], axis=0)
    scores_again = jnp.where(allowed, dot_tr(q_rows, keys) * score_scale, MASKED_SCORE)
    probs = jnp.where(allowed, jnp.exp(scores_again - lse), 0.0)
    g_probs = dot_tr(g_rows, values)
    g_scores = (probs * (g_probs - jnp.sum(probs * g_probs, axis=-1, keepdims=True))).astype(BF)
    g_keys = dot_tl(g_scores, q_rows) * score_scale
    g_values = dot_tl(probs.astype(BF), g_rows)
    g_kv = jnp.concatenate([g_keys, g_values], axis=1)
    n_mine = 8 * TOKENS
    g_kv_sum = g_kv[:n_mine] + other_core(g_kv[n_mine:].astype(BF)).astype(F32)
    g_kv_b = g_kv_sum.astype(BF)
    g_line = g_kv_sum[:640] + other_half(g_kv_b[640:]).astype(F32)
    g_kv_own = g_line[:TOKENS]
    g_line = g_line.astype(BF)
    for k in (1, 2, 3):
        g_kv_own = g_kv_own + shift(g_line[TOKENS * k : TOKENS * (k + 1)], "y", 4 - k).astype(F32)
    g_scores, side_out, ff_parts, down_first, gb_down, _ = after(
        g_kv_b, g_scores, side_out, ff_parts, down_first, gb_down
    )
    g_q_rows = dot(g_scores, keys) * score_scale
    g_q = [
        jnp.concatenate(
            [turn_back(g_q_rows[TOKENS * h : TOKENS * (h + 1)], cos, sin) for h in (2 * i, 2 * i + 1)],
            axis=1,
        ).astype(BF)
        for i in (0, 1)
    ]
    down_line = sum(m.astype(F32) for m in down_first).astype(BF)
    down_second = [down_line[0]] + [shift(down_line[k], "z", 4 - k) for k in (1, 2, 3)]
    ff_sum = jnp.sum(ff_parts.astype(F32), axis=0).astype(BF)
    ga_part = jnp.concatenate(
        [dot_tr(ff_sum[:72], b_gate), dot_tr(ff_sum[72:144], b_up), jnp.zeros((72, 384), F32)], axis=1
    ).astype(BF)
    back_row = jnp.arange(256, dtype=jnp.int32)
    group, line = back_row // 32, back_row % 32
    take = jnp.where(
        line < 9,
        9 * group + line,
        jnp.where(
            line < 18,
            72 + 9 * group + line - 9,
            jnp.where(
                line < 22,
                144 + 16 * ((line - 18) // 2) + 2 * group + line % 2,
                jnp.where(line < 31, 176 + 9 * group + line - 22, -1),
            ),
        ),
    )
    leaving = dot(
        table(take, jnp.arange(248, dtype=jnp.int32)), jnp.concatenate([ff_sum, ga_part], axis=0)
    ).astype(BF)
    slab = exchange(leaving.reshape(8, 32, 896), ("y", "c"))
    g_k = turn_back(g_kv_own[:, :256], cos, sin).astype(BF)
    g_v = g_kv_own[:, 256:].astype(BF)
    g_k = pick(is_first, g_k[:, :128], g_k[:, 128:])
    g_v = pick(is_first, g_v[:, :128], g_v[:, 128:])
    d_one = None
    for i, (g, first, last) in enumerate(((g_q, 0, 512), (g_k, 512, 640), (g_v, 640, 768))):
        d = dot_tr(g[0], raw[0][:, first:last]) + dot_tr(g[1], raw[1][:, first:last])
        gi = dot_tr(d.astype(BF), put_inner).astype(BF)
        inner_at = 768 + 128 * i
        d = d + dot_tr(gi[:, :128], raw[0][:, inner_at : inner_at + 128])
        d = d + dot_tr(gi[:, 128:], raw[1][:, inner_at : inner_at + 128])
        d_one = d if d_one is None else d_one + d
    g_u_one = select_back(d_one, put_rows)
    norm_one_back, g_gain_one = norm_back(scale_one, n_one, gain_one_full, g_u_one)
    grad_hidden = (g_after + norm_one_back).astype(BF)

    def of_chip(own, away):
        return (own.astype(F32) + other_core(away.astype(BF)).astype(F32)).astype(BF).reshape(64, 24, -1)

    def both_halves(owned):
        mine, away = pick(is_first, owned[:12], owned[12:])
        return pick(is_first, mine, other_core(away.astype(BF)).astype(F32))

    left, right = pick(is_first, gb_down[:, :640], gb_down[:, 512:])
    chip_out = of_chip(
        dot_tl(side_out, g_half[0]) + dot_tl(put_inner_down, left),
        dot_tl(side_out, g_half[1]) + dot_tl(put_inner_down, right),
    )
    loss_high, loss_rest = split_in_two(loss_here)
    loss_mid, loss_low = split_in_two(loss_rest)
    loss_low = loss_low.astype(BF)
    at_row = jnp.arange(32, dtype=jnp.int32)[:, None]
    nines = (features[None, :] % 9 == at_row % 9) & (at_row < 18)
    gain_rows = jnp.where(nines, jnp.where(at_row < 9, g_gain_one, g_gain_two), 0.0).astype(BF)
    loss_rows = jnp.where(
        at_row == 18, loss_high, jnp.where(at_row == 19, loss_mid, jnp.where(at_row == 20, loss_low, 0))
    ).astype(F32)
    more_side = (dot(gain_rows, put_marks) + loss_rows * (j == 11)[None, :]).astype(BF)
    lines = jnp.arange(32, dtype=jnp.int32)
    line_at = jnp.where(lines < 18, lines, jnp.where(lines < 21, lines + 3 * core, -1))
    more_grad = table(line_at, jnp.arange(512, dtype=jnp.int32))
    sums = [
        jnp.concatenate(
            [
                (dot_tl(sides[0], g_q[i]) + dot_tl(more_side, more_grad)).astype(BF),
                dot_tl(sides[1], g_k[i]).astype(BF),
                dot_tl(sides[2], g_v[i]).astype(BF),
            ],
            axis=1,
        )
        for i in (0, 1)
    ]
    chip_sums = jnp.concatenate([of_chip(sums[0], sums[1]), chip_out], axis=2)
    parts = exchange(chip_sums, CHIPS)
    slab, down_second, _ = after(chip_sums, slab, down_second)

    narrow = dot_tr(slab.reshape(256, 896), wider).reshape(8, 32, 864)
    wide = jnp.concatenate([narrow[t] for t in range(8)], axis=1)
    ga = jnp.sum(slab[:, 22:31, :512].astype(F32), axis=0)
    down_sum = sum(m.astype(F32) for m in down_second).astype(BF)
    gw_down_own = lax.ppermute(down_sum, EVERY, [(b, a) for a, b in down_route()])[:54]
    ga_down_own = dot_tr(gw_down_own, b_down)
    all_owned = jnp.sum(parts.astype(F32), axis=0)
    owned, owned_out = all_owned[:, :768], all_owned[:, 768:]
    left, right = both_halves(owned_out)
    own_out = jnp.concatenate([left, right[:, 128:]], axis=1)
    d = dot_tr(own_out[:8, :640].astype(BF), pick(is_first, *raw_out)[0][:, :640]) + dot_tr(
        own_out[:8, 640:].astype(BF), pick(is_first, *raw_out)[1][:, 128:640]
    )
    ga_out_own = dot_tr(d.astype(BF), put_inner_out)
    ga_out_own = jnp.concatenate(pick(is_first, ga_out_own[:, :128], ga_out_own[:, 128:]), axis=1)
    loss_value = jnp.sum(owned[11, 18:24]) / (1152.0 * valid_count)
    left, right = both_halves(owned)
    gains = left[11]
    left_b, right_b = left.astype(BF), right.astype(BF)
    mine_b, other_b = pick(is_first, left_b, right_b)
    ga_own = []
    for first, last in ((0, 512), (512, 640), (640, 768)):
        d = dot_tr(mine_b[:, first:last], raw[0][:, first:last]) + dot_tr(
            other_b[:, first:last], raw[1][:, first:last]
        )
        g = dot_tr(d.astype(BF), put_inner)[:9]
        ga_own.append(jnp.concatenate(pick(is_first, g[:, :128], g[:, 128:]), axis=1))

    def columns(first, last, rows):
        return jnp.concatenate([left[rows, first:last], right[rows, first:last]], axis=1)

    top_rows, low_rows = slice(0, 9), slice(9, 11)

    return (
        result.astype(BF)[None],
        loss_value,
        grad_hidden[None],
        gains[:9],
        columns(0, 512, top_rows),
        columns(512, 640, top_rows),
        columns(640, 768, top_rows),
        own_out[:8],
        ga_own[0],
        columns(0, 512, low_rows),
        ga_own[1],
        columns(512, 640, low_rows),
        ga_own[2],
        columns(640, 768, low_rows),
        ga_out_own,
        own_out[8:10],
        gains[9:18],
        wide[:9],
        wide[9:18],
        gw_down_own.astype(F32),
        ga[:, :256],
        wide[18:20],
        ga[:, 256:],
        wide[20:22],
        ga_down_own,
        own_out[10:],
    )


def solution(mesh):
    mesh = Mesh(mesh.devices.reshape([SIZES[a] for a in EVERY]), EVERY)
    tree, seq = ("z", "xl"), ("xh", "y", "c")
    rows = P(EVERY, None)
    vector = P(EVERY)
    return jax.shard_map(
        on_device,
        mesh=mesh,
        in_specs=(
            P(tree, seq, None),
            P(tree, None),
            P(tree, None),
            P(tree, seq),
            P(tree, seq, None),
            vector,
        )
        + (rows,) * 12
        + (vector,)
        + (rows,) * 9,
        out_specs=(P(tree, seq, None), P(), P(tree, seq, None), vector)
        + (rows,) * 12
        + (vector,)
        + (rows,) * 9,
        check_vma=False,
    )
```

```python
import jax
import jax.numpy as jnp
from jax import lax
from jax.sharding import Mesh, PartitionSpec as P

EPSILON = 1e-06
ROPE_BASE = 10000.0
MASKED_SCORE = -1e30
BF = jnp.bfloat16
F32 = jnp.float32

PLANE = ("z", "xl", "xh")
CHIPS = ("z", "xl", "xh", "y")
EVERY = ("z", "xl", "xh", "y", "c")
SIZES = dict(z=4, xl=2, xh=2, y=4, c=2)
RING = dict(z="z", x=("xl", "xh"), y="y")
TOKENS = 160
HEADS = 4
WIDTH = 256


def dot(a, b):
    return jnp.dot(a, b, preferred_element_type=F32)


def dot_tl(a, b):
    return lax.dot_general(a, b, (((0,), (0,)), ((), ())), preferred_element_type=F32)


def dot_tr(a, b):
    return lax.dot_general(a, b, (((1,), (1,)), ((), ())), preferred_element_type=F32)


def exchange(x, axes):
    return lax.all_to_all(x, axes, split_axis=0, concat_axis=0, tiled=True)


def gather_chips(x):
    return exchange(jnp.broadcast_to(x[None], (64,) + x.shape), CHIPS)


def other_core(x):
    return lax.ppermute(x, "c", [(0, 1), (1, 0)])


def other_half(x):
    return lax.ppermute(x, "xh", [(0, 1), (1, 0)])


def shift(x, axis, k):
    number = [0, 2, 1, 3] if axis == "x" else [0, 1, 2, 3]
    return lax.ppermute(x, RING[axis], [(number[i], number[(i + k) % 4]) for i in range(4)])


def pick(cond, a, b):
    return jnp.where(cond, a, b), jnp.where(cond, b, a)


def split_in_two(x):
    high = x.astype(BF)
    return high, x - high.astype(F32)


def select_back(x, table):
    high, low = split_in_two(x)
    return dot_tr(high, table) + dot_tr(low.astype(BF), table)


def down_route():
    pairs = []
    for o in range(16):
        for t in range(8):
            pairs.append((8 * o + t, 8 * (8 * (o % 2) + t) + o // 2))
    return pairs


def gather_line(x, axis):
    return jnp.stack([x] + [shift(x, axis, k) for k in (1, 2, 3)])


def leave(x, axis, dim, at_z, at_x):
    parts = []
    for k in range(4):
        place = (at_z - k) % 4 if axis == "z" else (at_x - k) % 4 % 2 * 2 + (at_x - k) % 4 // 2
        block = lax.dynamic_index_in_dim(x, place, dim, keepdims=False)
        parts.append(shift(block, axis, 4 - k) if k else block)
    return parts


def add(parts):
    total = parts[0].astype(F32)
    for p in parts[1:]:
        total = total + p.astype(F32)
    return total


def norm_parts(values, gain):
    scale = lax.rsqrt(jnp.mean(values * values, axis=-1, keepdims=True) + EPSILON)
    n = values * scale
    return scale, n, (n * (1.0 + gain)).astype(BF)


def norm_back(scale, n, gain, grad):
    m = grad * (1.0 + gain)
    back = scale * (m - n * jnp.mean(m * n, axis=-1, keepdims=True))
    return back


def turn(x, cos, sin):
    h = cos.shape[-1]
    a, b = x[:, :h], x[:, h:]
    return jnp.concatenate([a * cos - b * sin, b * cos + a * sin], axis=-1)


def turn_back(x, cos, sin):
    return turn(x, cos, -sin)


def gather_tokens(x):
    mine = [x] + [shift(x, "y", k) for k in (1, 2, 3)]
    return jnp.concatenate(mine + [other_core(p) for p in mine], axis=0)


def scatter_tokens(part):
    blocks = part.reshape(2, 4, TOKENS, -1)
    total = None
    for k in (2, 1, 3, 0):
        piece = blocks[0, k] + other_core(blocks[1, k].astype(BF)).astype(F32)
        if k:
            piece = shift(piece.astype(BF), "y", 4 - k).astype(F32)
        total = piece if total is None else total + piece
    return total


def after(done, *values):
    return tuple(lax.optimization_barrier((v, done))[0] for v in values) + (done,)


def table(rows, columns):
    return (rows[:, None] == columns[None, :]).astype(BF)


def on_device(
    layer_input,
    segment,
    position,
    loss_token_mask,
    teacher,
    gain_one,
    wq,
    wk,
    wv,
    wo,
    aq,
    bq,
    ak,
    bk,
    av,
    bv,
    ao,
    bo,
    gain_two,
    wg,
    wu,
    wd,
    ag,
    bg,
    au,
    bu,
    ad,
    bd,
):
    core = lax.axis_index("c")
    at_z, at_y = lax.axis_index("z"), lax.axis_index("y")
    at_xl, at_xh = lax.axis_index("xl"), lax.axis_index("xh")
    at_x = 2 * at_xh + at_xl
    is_first = core == 0
    score_scale = WIDTH**-0.5
    count_here = jnp.sum(loss_token_mask[0]).astype(BF)

    extra = jnp.concatenate([gain_one[None], gain_two[None], count_here.reshape(1, 1)], axis=1)
    extra = jnp.pad(extra, ((0, 1), (0, 384 - 19)))

    def attention_half(k):
        top = jnp.concatenate(
            [m[:, m.shape[1] // 2 * k : m.shape[1] // 2 * (k + 1)] for m in (wq, wk, wv, aq, ak, av)],
            axis=1,
        )
        low = jnp.concatenate(
            [m[:, m.shape[1] // 2 * k : m.shape[1] // 2 * (k + 1)] for m in (bq, bk, bv)] + [extra],
            axis=1,
        )
        return jnp.concatenate([top, low, jnp.zeros((1, 1152), BF)], axis=0)

    keep, send = pick(is_first, attention_half(0), attention_half(1))
    lower, upper = pick(is_first, keep, other_core(send))
    att_own = jnp.concatenate([lower, upper], axis=0)
    raw_one = gather_chips(att_own)
    (layer_input, wg, wu, bg, bu, wd, ad, ag, au, wo, ao, bo, bd, segment, position, core, at_z, _) = after(
        att_own,
        layer_input, wg, wu, bg, bu, wd, ad, ag, au, wo, ao, bo, bd, segment, position, core, at_z,
    )
    is_first = core == 0
    hidden = layer_input[0].astype(F32)

    def output_half(k):
        wide = jnp.concatenate([m[:, 512 * k : 512 * k + 640] for m in (wo, bo, bd)], axis=0)
        narrow = jnp.pad(ao[:, 128 * k : 128 * k + 128], ((0, 4), (0, 0)))
        return jnp.concatenate([wide, narrow, jnp.pad((ag, au)[k], ((0, 3), (0, 0)))], axis=1)

    keep, send = pick(is_first, output_half(0), output_half(1))
    lower, upper = pick(is_first, keep, other_core(send))
    out_own = jnp.concatenate([lower, upper], axis=0)

    def column_of(k):
        return 2 * ((at_y + k // 2) % 4) + (core + k) % 2

    def column_shift(x, k):
        route = []
        for y in range(4):
            for c in range(2):
                route.append((2 * y + c, 2 * ((y + k // 2) % 4) + (c + k) % 2))
        return lax.ppermute(x, ("y", "c"), route)

    rows22 = jnp.pad(jnp.concatenate([wg, wu, bg, bu], axis=0), ((0, 2), (0, 0)))
    rows22 = jnp.concatenate([rows22[:, 864 * t : 864 * (t + 1)] for t in range(8)], axis=0)
    wider = jnp.arange(896, dtype=jnp.int32)
    wider = table(jnp.arange(864, dtype=jnp.int32), jnp.where(wider % 56 < 54, wider // 56 * 54 + wider % 56, -1))
    rows22 = dot(rows22, wider).astype(BF).reshape(8, 24, 896)
    slab = []
    for k in range(8):
        piece = lax.dynamic_index_in_dim(rows22, column_of(k), 0, keepdims=False)
        slab.append(column_shift(piece, k) if k else piece)
    slab = jnp.concatenate(slab, axis=0)
    back = jnp.arange(8, dtype=jnp.int32)
    sources = 2 * ((at_y - back // 2) % 4) + (core - back) % 2
    row = jnp.arange(176, dtype=jnp.int32)
    low = row - 144
    at_row = jnp.where(
        row < 72,
        row // 9 * 24 + row % 9,
        jnp.where(
            row < 144,
            (row - 72) // 9 * 24 + 9 + (row - 72) % 9,
            low % 16 // 2 * 24 + 18 + low // 16 * 2 + low % 2,
        ),
    )
    in_slab = jnp.arange(192, dtype=jnp.int32)
    in_slab = jnp.repeat(sources, 24) * 24 + in_slab % 24
    ff_own = dot(table(at_row, in_slab), slab).astype(BF)
    down_own = lax.ppermute(
        jnp.pad(jnp.concatenate([wd, ad], axis=1), ((0, 2), (0, 0))), EVERY, down_route()
    )
    raw_one, _ = after(ff_own, raw_one)
    raw_two = other_core(raw_one)
    marks = raw_one.reshape(128, 12, 1152)[:, 9, 768:896]
    gain_one_full = marks[:, :9].reshape(1, 1152).astype(F32)
    gain_two_full = marks[:, 9:18].reshape(1, 1152).astype(F32)
    valid_count = jnp.sum(marks[:, 18].astype(F32))
    out_own, _ = after(raw_one, out_own)
    out_wide = jnp.broadcast_to(out_own[None], (64, 24, 1024))
    out_one = exchange(out_wide, CHIPS)
    out_two = other_core(out_one)
    raw_out = [out_one.reshape(1536, 1024), out_two.reshape(1536, 1024)]
    raw_one, raw_two, _ = after(out_wide, raw_one, raw_two)
    raw = [raw_one.reshape(1536, 1152), raw_two.reshape(1536, 1152)]
    ff_own, _ = after(out_one, ff_own)
    ff_wide = jnp.broadcast_to(ff_own[None], (16, 176, 896))
    ff_all = exchange(ff_wide, PLANE)

    ids = jnp.arange(1536, dtype=jnp.int32)
    dev, j = 2 * (ids // 24) + (ids % 24) // 12, ids % 12
    halves = jnp.arange(256, dtype=jnp.int32)
    inner_ids = jnp.where(halves < 128, 128 * core + halves, 128 * (1 - core) + halves - 128)
    heads_at = jnp.arange(1024, dtype=jnp.int32)
    head_ids = jnp.where(heads_at < 512, 512 * core + heads_at, 512 * (1 - core) + heads_at - 512)
    features = jnp.arange(1152, dtype=jnp.int32)
    put_rows = table(features, jnp.where(j < 9, 9 * dev + j, -1))
    put_inner = table(inner_ids, jnp.where((j >= 9) & (j < 11), 2 * dev + j - 9, -1))
    take_b = table(halves, jnp.where((j >= 9) & (j < 11), 2 * dev + j - 9, -1))
    take_b_out = table(halves, jnp.where((j >= 8) & (j < 10), 2 * dev + j - 8, -1))
    put_mix = table(head_ids, jnp.where(j < 8, 8 * dev + j, -1))
    put_inner_out = table(inner_ids, jnp.where((j >= 8) & (j < 10), 2 * dev + j - 8, -1))
    put_inner_down = table(halves, jnp.where(j >= 10, 2 * dev + j - 10, -1))

    seq = (at_xh * 4 + at_y) * 2 + core
    tree_seg = segment[0]
    tree_pos = position[0]
    own_seg = lax.dynamic_slice_in_dim(tree_seg, seq * TOKENS, TOKENS)
    own_pos = lax.dynamic_slice_in_dim(tree_pos, seq * TOKENS, TOKENS)
    freq = ROPE_BASE ** (-(jnp.arange(128, dtype=F32) * 2.0 / WIDTH))
    angles = own_pos.astype(F32)[:, None] * freq[None, :]
    cos, sin = jnp.cos(angles), jnp.sin(angles)
    back = jnp.arange(16, dtype=jnp.int32)
    block_at = (((at_xh - (back % 8) // 4) % 2) * 4 + (at_y - back % 4) % 4) * 2 + jnp.where(
        back < 8, core, 1 - core
    )
    chosen = (block_at[:, None] == back[None, :]).astype(jnp.int32)[:, :, None]
    key_seg = jnp.sum(chosen * tree_seg.reshape(1, 16, TOKENS), axis=1).reshape(1, 2560)
    key_pos = jnp.sum(chosen * tree_pos.reshape(1, 16, TOKENS), axis=1).reshape(1, 2560)
    q_seg, q_pos = own_seg[:, None], own_pos[:, None]
    parent = (key_seg >= 1) & (key_seg <= 4) & (q_seg >= 5) & ((q_seg - 5) // 2 + 1 == key_seg)
    allowed = ((key_seg == q_seg) | (key_seg == 0) | parent) & (key_pos <= q_pos)
    allowed = jnp.concatenate([allowed] * HEADS, axis=0)

    scale_one, n_one, u_one = norm_parts(hidden, gain_one_full)
    u_rows = dot(u_one, put_rows).astype(BF)
    inner = [dot(u_rows, raw[i][:, 768:]).astype(BF) for i in (0, 1)]
    sides = []
    for i in range(3):
        part = jnp.concatenate([inner[0][:, 128 * i : 128 * i + 128], inner[1][:, 128 * i : 128 * i + 128]], axis=1)
        sides.append(u_rows + dot(part, put_inner).astype(BF))
    kk = pick(is_first, *[dot(sides[1], raw[i][:, 512:640]) for i in (0, 1)])
    vv = pick(is_first, *[dot(sides[2], raw[i][:, 640:768]) for i in (0, 1)])
    kv_own = jnp.concatenate([turn(jnp.concatenate(kk, axis=1), cos, sin), vv[0], vv[1]], axis=1).astype(BF)

    kv_line = gather_line(kv_own, "y").reshape(640, 512)
    kv_mine = jnp.concatenate([kv_line, other_half(kv_line)], axis=0)
    kv = jnp.concatenate([kv_mine, other_core(kv_mine)], axis=0)
    kv, _ = after(ff_wide, kv)
    keys, values = kv[:, :256], kv[:, 256:]
    queries = [dot(sides[0], raw[i][:, :512]) for i in (0, 1)]
    q_rows = jnp.concatenate(
        [turn(queries[h // 2][:, WIDTH * (h % 2) : WIDTH * (h % 2 + 1)], cos, sin) for h in range(HEADS)],
        axis=0,
    ).astype(BF)
    scores = jnp.where(allowed, dot_tr(q_rows, keys) * score_scale, MASKED_SCORE)
    top = jnp.max(scores, axis=-1, keepdims=True)
    ex = jnp.exp(scores - top)
    total = jnp.sum(ex, axis=-1, keepdims=True)
    lse = top + jnp.log(total)
    mix_rows = dot((ex / total).astype(BF), values).astype(BF)
    mix = jnp.concatenate([mix_rows[TOKENS * h : TOKENS * (h + 1)] for h in range(HEADS)], axis=1)
    mix_placed = dot(mix, put_mix).astype(BF)
    inner_out = jnp.concatenate([dot(mix_placed, raw_out[i][:, 640:768]) for i in (0, 1)], axis=1).astype(BF)
    side_out = mix_placed + dot(inner_out, put_inner_out).astype(BF)
    left, right = pick(is_first, *[dot(side_out, raw_out[i][:, :640]) for i in (0, 1)])
    after_att = hidden + jnp.concatenate([left, right[:, 128:]], axis=1)

    scale_two, n_two, u_two = norm_parts(after_att, gain_two_full)
    u_all = gather_tokens(u_two)

    raw_late, out_late, ff_all, _ = after(u_two, raw, raw_out, ff_all)
    down_own, _ = after(ff_all, down_own)
    down_raw = exchange(jnp.broadcast_to(down_own[None], (16, 56, 1408)), PLANE).reshape(896, 1408)
    b_left, b_right = pick(is_first, *[dot(take_b, raw_late[i][:, :768]).astype(BF) for i in (0, 1)])
    left, right = pick(is_first, *[dot(take_b_out, out_late[i][:, :640]).astype(BF) for i in (0, 1)])
    b_out = jnp.concatenate([left, right[:, 128:]], axis=1)
    left, right = pick(is_first, *[dot(put_inner_down, out_late[i][:, :640]).astype(BF) for i in (0, 1)])
    b_down = jnp.concatenate([left, right[:, 128:]], axis=1)
    a_gate, a_up = pick(is_first, *[dot(put_rows, out_late[i][:, 768:]).astype(BF) for i in (0, 1)])
    b_gate = ff_all[:, 144:160].reshape(256, 896)
    b_up = ff_all[:, 160:].reshape(256, 896)
    w_gate = (ff_all[:, :72].reshape(1152, 896).astype(F32) + dot(a_gate, b_gate)).astype(BF)
    w_up = (ff_all[:, 72:144].reshape(1152, 896).astype(F32) + dot(a_up, b_up)).astype(BF)

    a_down = down_raw[:, 1152:]
    w_down = (down_raw[:, :1152].astype(F32) + dot(a_down, b_down)).astype(BF)

    gate = dot(u_all, w_gate)
    up = dot(u_all, w_up)
    act, act_pull = jax.vjp(lambda g, u: jax.nn.gelu(g, approximate=True) * u, gate, up)
    act = act.astype(BF)
    result = after_att + scatter_tokens(dot(act, w_down))

    valid = loss_token_mask[0].astype(F32)[:, None]
    error = result - teacher[0].astype(F32)
    loss_here = jnp.sum(valid * error * error)
    grad_result = 2.0 * 20480.0 / valid_count * valid * error

    g_all = gather_tokens(grad_result.astype(BF))
    g_act = dot_tr(g_all, w_down).astype(BF)
    g_gate, g_up = act_pull(g_act.astype(F32))
    g_gate, g_up = g_gate.astype(BF), g_up.astype(BF)
    g_u_part = dot_tr(g_gate, w_gate) + dot_tr(g_up, w_up)
    g_u_two = scatter_tokens(g_u_part)
    u_all, act, g_all, g_gate, g_up, _ = after(g_u_part, u_all, act, g_all, g_gate, g_up)
    gw_gate = dot_tl(u_all, g_gate).astype(BF)
    gb_gate = dot_tl(a_gate, gw_gate).astype(BF)
    gate_grads = jnp.concatenate([gw_gate.reshape(16, 72, 896), gb_gate.reshape(16, 16, 896)], axis=1)
    gate_first = leave(gate_grads.reshape(4, 4, 88, 896), "z", 0, at_z, at_x)
    gate_first, _ = after(g_u_two, gate_first)
    gate_line = add(gate_first).astype(BF)
    gate_second = leave(gate_line, "x", 0, at_z, at_x)
    gw_up = dot_tl(u_all, g_up).astype(BF)
    gb_up = dot_tl(a_up, gw_up).astype(BF)
    up_grads = jnp.concatenate([gw_up.reshape(16, 72, 896), gb_up.reshape(16, 16, 896)], axis=1)
    up_first = leave(up_grads.reshape(4, 4, 88, 896), "x", 1, at_z, at_x)
    up_first, _ = after(g_u_two, up_first)
    up_line = add(up_first).astype(BF)
    up_second = leave(up_line, "z", 0, at_z, at_x)
    gw_down = dot_tl(act, g_all).astype(BF)
    gb_down = dot_tl(a_down, gw_down).astype(BF)
    down_first = leave(gw_down.reshape(4, 4, 56, 1152), "z", 0, at_z, at_x)

    norm_two_back = norm_back(scale_two, n_two, gain_two_full, g_u_two)
    g_after = grad_result + norm_two_back
    g_after_b = g_after.astype(BF)
    once = jnp.where(jnp.arange(640) < 128, 0, 1).astype(BF)[None]
    g_half = pick(is_first, g_after_b[:, :640], g_after_b[:, 512:])
    g_once = pick(is_first, g_after_b[:, :640], g_after_b[:, 512:] * once)
    d_out = dot_tr(g_once[0], raw_out[0][:, :640]) + dot_tr(g_once[1], raw_out[1][:, :640])
    gi_out = dot_tr(d_out.astype(BF), put_inner_out).astype(BF)
    d_out = (
        d_out
        + dot_tr(gi_out[:, :128], raw_out[0][:, 640:768])
        + dot_tr(gi_out[:, 128:], raw_out[1][:, 640:768])
    )
    g_mix = dot_tr(d_out.astype(BF), put_mix).astype(BF)
    g_rows = jnp.concatenate([g_mix[:, WIDTH * h : WIDTH * (h + 1)] for h in range(HEADS)], axis=0)
    scores_again = jnp.where(allowed, dot_tr(q_rows, keys) * score_scale, MASKED_SCORE)
    probs = jnp.where(allowed, jnp.exp(scores_again - lse), 0.0)
    g_probs = dot_tr(g_rows, values)
    g_scores = (probs * (g_probs - jnp.sum(probs * g_probs, axis=-1, keepdims=True))).astype(BF)
    g_scores, probs, _ = after((gate_line, up_line), g_scores, probs)
    g_keys = dot_tl(g_scores, q_rows) * score_scale
    g_values = dot_tl(probs.astype(BF), g_rows)
    g_kv = jnp.concatenate([g_keys, g_values], axis=1)
    n_mine = 8 * TOKENS
    g_kv_sum = g_kv[:n_mine] + other_core(g_kv[n_mine:].astype(BF)).astype(F32)
    g_kv_b = g_kv_sum.astype(BF)
    g_line = g_kv_sum[:640] + other_half(g_kv_b[640:]).astype(F32)
    g_kv_own = g_line[:TOKENS]
    g_line = g_line.astype(BF)
    for k in (1, 2, 3):
        g_kv_own = g_kv_own + shift(g_line[TOKENS * k : TOKENS * (k + 1)], "y", 4 - k).astype(F32)
    g_scores, side_out, gate_second, up_second, down_first, gb_down, _ = after(
        g_kv_b, g_scores, side_out, gate_second, up_second, down_first, gb_down
    )
    g_q_rows = dot(g_scores, keys) * score_scale
    g_q = [
        jnp.concatenate(
            [turn_back(g_q_rows[TOKENS * h : TOKENS * (h + 1)], cos, sin) for h in (2 * i, 2 * i + 1)],
            axis=1,
        ).astype(BF)
        for i in (0, 1)
    ]
    gate_sum, up_sum = add(gate_second).astype(BF), add(up_second).astype(BF)
    ga_part = jnp.concatenate(
        [dot_tr(gate_sum[:72], b_gate), dot_tr(up_sum[:72], b_up), jnp.zeros((72, 384), F32)], axis=1
    ).astype(BF)
    back_row = jnp.arange(256, dtype=jnp.int32)
    group, line = back_row // 32, back_row % 32
    take = jnp.where(
        line < 9,
        9 * group + line,
        jnp.where(
            line < 18,
            88 + 9 * group + line - 9,
            jnp.where(
                line < 22,
                72 + 88 * ((line - 18) // 2) + 2 * group + line % 2,
                jnp.where(line < 31, 176 + 9 * group + line - 22, -1),
            ),
        ),
    )
    leaving = dot(
        table(take, jnp.arange(248, dtype=jnp.int32)), jnp.concatenate([gate_sum, up_sum, ga_part], axis=0)
    ).astype(BF)
    slab = exchange(leaving.reshape(8, 32, 896), ("y", "c"))
    def of_chip(own, away):
        return (own.astype(F32) + other_core(away.astype(BF)).astype(F32)).astype(BF).reshape(64, 24, -1)

    def both_halves(owned):
        mine, away = pick(is_first, owned[:12], owned[12:])
        return pick(is_first, mine, other_core(away.astype(BF)).astype(F32))

    left, right = pick(is_first, gb_down[:, :640], gb_down[:, 512:])
    chip_out = of_chip(
        dot_tl(side_out, g_half[0]) + dot_tl(put_inner_down, left),
        dot_tl(side_out, g_half[1]) + dot_tl(put_inner_down, right),
    )
    loss_high, loss_rest = split_in_two(loss_here)
    loss_mid, loss_low = split_in_two(loss_rest)
    lines = jnp.arange(16, dtype=jnp.int32)
    loss_rows = jnp.where(
        lines == 0,
        loss_high.astype(F32),
        jnp.where(lines == 1, loss_mid.astype(F32), jnp.where(lines == 2, loss_low, 0.0)),
    )
    more_side = (loss_rows[:, None] * (j == 11)[None, :]).astype(BF)
    more_grad = table(jnp.where(lines < 3, lines + 3 * core, -1), jnp.arange(512, dtype=jnp.int32))
    chip_q = of_chip(
        *[(dot_tl(sides[0], g_q[i]) + dot_tl(more_side, more_grad)).astype(BF) for i in (0, 1)]
    )
    g_kv_own, _ = after((chip_q, chip_out, leaving), g_kv_own)
    g_k = turn_back(g_kv_own[:, :256], cos, sin).astype(BF)
    g_v = g_kv_own[:, 256:].astype(BF)
    g_k = pick(is_first, g_k[:, :128], g_k[:, 128:])
    g_v = pick(is_first, g_v[:, :128], g_v[:, 128:])
    chip_kv = of_chip(
        *[
            jnp.concatenate([dot_tl(sides[1], g_k[i]).astype(BF), dot_tl(sides[2], g_v[i]).astype(BF)], axis=1)
            for i in (0, 1)
        ]
    )
    chip_sums = jnp.concatenate([chip_q, chip_kv, chip_out], axis=2)
    parts = exchange(chip_sums, CHIPS)
    down_first, _ = after(g_kv_own, down_first)
    down_second = leave(add(down_first).astype(BF), "x", 0, at_z, at_x)
    slab, down_second, g_q, g_k, g_v, _ = after(chip_sums, slab, down_second, g_q, g_k, g_v)

    d_one = None
    for i, (g, first, last) in enumerate(((g_q, 0, 512), (g_k, 512, 640), (g_v, 640, 768))):
        d = dot_tr(g[0], raw[0][:, first:last]) + dot_tr(g[1], raw[1][:, first:last])
        gi = dot_tr(d.astype(BF), put_inner).astype(BF)
        inner_at = 768 + 128 * i
        d = d + dot_tr(gi[:, :128], raw[0][:, inner_at : inner_at + 128])
        d = d + dot_tr(gi[:, 128:], raw[1][:, inner_at : inner_at + 128])
        d_one = d if d_one is None else d_one + d
    g_u_one = select_back(d_one, put_rows)
    grad_hidden = (g_after + norm_back(scale_one, n_one, gain_one_full, g_u_one)).astype(BF)

    narrow = dot_tr(slab.reshape(256, 896), wider).reshape(8, 32, 864)
    wide = jnp.concatenate([narrow[t] for t in range(8)], axis=1)
    ga = jnp.sum(slab[:, 22:31, :512].astype(F32), axis=0)
    gw_down_own = lax.ppermute(
        add(down_second).astype(BF), EVERY, [(b, a) for a, b in down_route()]
    )[:54]
    ga_down_own = dot_tr(gw_down_own, b_down)

    def over_columns(pairs):
        return sum(jnp.sum(a.astype(F32) * b, axis=1) for a, b in pairs)

    gain_two_own = over_columns(
        ((wg, wide[:9]), (wu, wide[9:18]), (ag, ga[:, :256]), (au, ga[:, 256:]))
    ) / (1.0 + gain_two.astype(F32))

    owned = jnp.sum(parts.astype(F32), axis=0)
    loss_value = jnp.sum(owned[11, :6]) / (1152.0 * valid_count)
    left, right = both_halves(owned)
    own_out = jnp.concatenate([left[:, 768:], right[:, 896:]], axis=1)
    ga_out_own = dot_tr(own_out[:8].astype(BF), b_out)
    left_b, right_b = left[:9].astype(BF), right[:9].astype(BF)
    ga_own = [
        dot_tr(left_b[:, first:last], b_left[:, first:last])
        + dot_tr(right_b[:, first:last], b_right[:, first:last])
        for first, last in ((0, 512), (512, 640), (640, 768))
    ]

    def columns(first, last, rows):
        return jnp.concatenate([left[rows, first:last], right[rows, first:last]], axis=1)

    top_rows, low_rows = slice(0, 9), slice(9, 11)
    gw_own = [columns(0, 512, top_rows), columns(512, 640, top_rows), columns(640, 768, top_rows)]
    gain_one_own = over_columns(
        list(zip((wq, wk, wv), gw_own)) + list(zip((aq, ak, av), ga_own))
    ) / (1.0 + gain_one.astype(F32))

    return (
        result.astype(BF)[None],
        loss_value,
        grad_hidden[None],
        gain_one_own,
        *gw_own,
        own_out[:8],
        ga_own[0],
        columns(0, 512, low_rows),
        ga_own[1],
        columns(512, 640, low_rows),
        ga_own[2],
        columns(640, 768, low_rows),
        ga_out_own,
        own_out[8:10],
        gain_two_own,
        wide[:9],
        wide[9:18],
        gw_down_own.astype(F32),
        ga[:, :256],
        wide[18:20],
        ga[:, 256:],
        wide[20:22],
        ga_down_own,
        own_out[10:],
    )


def solution(mesh):
    mesh = Mesh(mesh.devices.reshape([SIZES[a] for a in EVERY]), EVERY)
    tree, seq = ("z", "xl"), ("xh", "y", "c")
    rows = P(EVERY, None)
    vector = P(EVERY)
    return jax.shard_map(
        on_device,
        mesh=mesh,
        in_specs=(
            P(tree, seq, None),
            P(tree, None),
            P(tree, None),
            P(tree, seq),
            P(tree, seq, None),
            vector,
        )
        + (rows,) * 12
        + (vector,)
        + (rows,) * 9,
        out_specs=(P(tree, seq, None), P(), P(tree, seq, None), vector)
        + (rows,) * 12
        + (vector,)
        + (rows,) * 9,
        check_vma=False,
    )
```

```python
import jax
import jax.numpy as jnp
from jax import lax
from jax.sharding import Mesh, PartitionSpec as P

EPSILON = 1e-06
ROPE_BASE = 10000.0
MASKED_SCORE = -1e30
BF = jnp.bfloat16
F32 = jnp.float32

PLANE = ("z", "xl", "xh")
CHIPS = ("z", "xl", "xh", "y")
EVERY = ("z", "xl", "xh", "y", "c")
SIZES = dict(z=4, xl=2, xh=2, y=4, c=2)
RING = dict(z="z", x=("xl", "xh"), y="y")
TOKENS = 160
HEADS = 4
WIDTH = 256


def dot(a, b):
    return jnp.dot(a, b, preferred_element_type=F32)


def dot_tl(a, b):
    return lax.dot_general(a, b, (((0,), (0,)), ((), ())), preferred_element_type=F32)


def dot_tr(a, b):
    return lax.dot_general(a, b, (((1,), (1,)), ((), ())), preferred_element_type=F32)


def exchange(x, axes):
    return lax.all_to_all(x, axes, split_axis=0, concat_axis=0, tiled=True)


def other_core(x):
    return lax.ppermute(x, "c", [(0, 1), (1, 0)])


def other_half(x):
    return lax.ppermute(x, "xh", [(0, 1), (1, 0)])


def shift(x, axis, k):
    number = [0, 2, 1, 3] if axis == "x" else [0, 1, 2, 3]
    return lax.ppermute(x, RING[axis], [(number[i], number[(i + k) % 4]) for i in range(4)])


def pick(cond, a, b):
    return jnp.where(cond, a, b), jnp.where(cond, b, a)


def split_in_two(x):
    high = x.astype(BF)
    return high, x - high.astype(F32)


def select_back(x, table):
    high, low = split_in_two(x)
    return dot_tr(high, table) + dot_tr(low.astype(BF), table)


def down_route():
    pairs = []
    for o in range(16):
        for t in range(8):
            pairs.append((8 * o + t, 8 * (8 * (o % 2) + t) + o // 2))
    return pairs


def gather_line(x, axis):
    return jnp.stack([x] + [shift(x, axis, k) for k in (1, 2, 3)])


def leave(x, axis, dim, at_z, at_x):
    parts = []
    for k in range(4):
        place = (at_z - k) % 4 if axis == "z" else (at_x - k) % 4 % 2 * 2 + (at_x - k) % 4 // 2
        block = lax.dynamic_index_in_dim(x, place, dim, keepdims=False)
        parts.append(shift(block, axis, 4 - k) if k else block)
    return parts


def add(parts):
    total = parts[0].astype(F32)
    for p in parts[1:]:
        total = total + p.astype(F32)
    return total


def norm_parts(values, gain):
    scale = lax.rsqrt(jnp.mean(values * values, axis=-1, keepdims=True) + EPSILON)
    n = values * scale
    return scale, n, (n * (1.0 + gain)).astype(BF)


def norm_back(scale, n, gain, grad):
    m = grad * (1.0 + gain)
    back = scale * (m - n * jnp.mean(m * n, axis=-1, keepdims=True))
    return back


def turn(x, cos, sin):
    h = cos.shape[-1]
    a, b = x[:, :h], x[:, h:]
    return jnp.concatenate([a * cos - b * sin, b * cos + a * sin], axis=-1)


def turn_back(x, cos, sin):
    return turn(x, cos, -sin)


def gather_tokens(x):
    mine = [x] + [shift(x, "y", k) for k in (1, 2, 3)]
    return jnp.concatenate(mine + [other_core(p) for p in mine], axis=0)


def scatter_tokens(part):
    blocks = part.reshape(2, 4, TOKENS, -1)
    total = None
    for k in (2, 1, 3, 0):
        piece = blocks[0, k] + other_core(blocks[1, k].astype(BF)).astype(F32)
        if k:
            piece = shift(piece.astype(BF), "y", 4 - k).astype(F32)
        total = piece if total is None else total + piece
    return total


def after(done, *values):
    return tuple(lax.optimization_barrier((v, done))[0] for v in values) + (done,)


def table(rows, columns):
    return (rows[:, None] == columns[None, :]).astype(BF)


def on_device(
    layer_input,
    segment,
    position,
    loss_token_mask,
    teacher,
    gain_one,
    wq,
    wk,
    wv,
    wo,
    aq,
    bq,
    ak,
    bk,
    av,
    bv,
    ao,
    bo,
    gain_two,
    wg,
    wu,
    wd,
    ag,
    bg,
    au,
    bu,
    ad,
    bd,
):
    core = lax.axis_index("c")
    at_z, at_y = lax.axis_index("z"), lax.axis_index("y")
    at_xl, at_xh = lax.axis_index("xl"), lax.axis_index("xh")
    at_x = 2 * at_xh + at_xl
    is_first = core == 0
    score_scale = WIDTH**-0.5
    count_here = jnp.sum(loss_token_mask[0]).astype(BF)

    extra = jnp.concatenate([gain_one[None], gain_two[None], count_here.reshape(1, 1)], axis=1)
    extra = jnp.pad(extra, ((0, 1), (0, 384 - 19)))

    def attention_half(k):
        top = jnp.concatenate(
            [m[:, m.shape[1] // 2 * k : m.shape[1] // 2 * (k + 1)] for m in (wq, wk, wv, aq, ak, av)],
            axis=1,
        )
        low = jnp.concatenate(
            [m[:, m.shape[1] // 2 * k : m.shape[1] // 2 * (k + 1)] for m in (bq, bk, bv)] + [extra],
            axis=1,
        )
        return jnp.concatenate([top, low, jnp.zeros((1, 1152), BF)], axis=0)

    keep, send = pick(is_first, attention_half(0), attention_half(1))
    lower, upper = pick(is_first, keep, other_core(send))
    att_own = jnp.concatenate([lower, upper], axis=0)
    att_wide = jnp.broadcast_to(att_own[None], (64, 24, 1152))
    raw_one = exchange(att_wide, CHIPS)
    (layer_input, wg, wu, bg, bu, wd, ad, ag, au, wo, ao, bo, bd, segment, position, core, at_z, _) = after(
        att_wide,
        layer_input, wg, wu, bg, bu, wd, ad, ag, au, wo, ao, bo, bd, segment, position, core, at_z,
    )
    is_first = core == 0
    hidden = layer_input[0].astype(F32)

    def output_half(k):
        wide = jnp.concatenate([m[:, 512 * k : 512 * k + 640] for m in (wo, bo, bd)], axis=0)
        narrow = jnp.pad(ao[:, 128 * k : 128 * k + 128], ((0, 4), (0, 0)))
        return jnp.concatenate([wide, narrow, jnp.pad((ag, au)[k], ((0, 3), (0, 0)))], axis=1)

    keep, send = pick(is_first, output_half(0), output_half(1))
    lower, upper = pick(is_first, keep, other_core(send))
    out_own = jnp.concatenate([lower, upper], axis=0)

    def column_of(k):
        return 2 * ((at_y + k // 2) % 4) + (core + k) % 2

    def column_shift(x, k):
        route = []
        for y in range(4):
            for c in range(2):
                route.append((2 * y + c, 2 * ((y + k // 2) % 4) + (c + k) % 2))
        return lax.ppermute(x, ("y", "c"), route)

    rows22 = jnp.pad(jnp.concatenate([wg, wu, bg, bu], axis=0), ((0, 2), (0, 0)))
    rows22 = jnp.concatenate([rows22[:, 864 * t : 864 * (t + 1)] for t in range(8)], axis=0)
    wider = jnp.arange(896, dtype=jnp.int32)
    wider = table(jnp.arange(864, dtype=jnp.int32), jnp.where(wider % 56 < 54, wider // 56 * 54 + wider % 56, -1))
    rows22 = dot(rows22, wider).astype(BF).reshape(8, 24, 896)
    slab = []
    for k in range(8):
        piece = lax.dynamic_index_in_dim(rows22, column_of(k), 0, keepdims=False)
        slab.append(column_shift(piece, k) if k else piece)
    slab = jnp.concatenate(slab, axis=0)
    back = jnp.arange(8, dtype=jnp.int32)
    sources = 2 * ((at_y - back // 2) % 4) + (core - back) % 2
    row = jnp.arange(176, dtype=jnp.int32)
    low = row - 144
    at_row = jnp.where(
        row < 72,
        row // 9 * 24 + row % 9,
        jnp.where(
            row < 144,
            (row - 72) // 9 * 24 + 9 + (row - 72) % 9,
            low % 16 // 2 * 24 + 18 + low // 16 * 2 + low % 2,
        ),
    )
    in_slab = jnp.arange(192, dtype=jnp.int32)
    in_slab = jnp.repeat(sources, 24) * 24 + in_slab % 24
    ff_own = dot(table(at_row, in_slab), slab).astype(BF)
    down_own = lax.ppermute(
        jnp.pad(jnp.concatenate([wd, ad], axis=1), ((0, 2), (0, 0))), EVERY, down_route()
    )
    seq = (at_xh * 4 + at_y) * 2 + core
    tree_seg = segment[0]
    tree_pos = position[0]
    own_seg = lax.dynamic_slice_in_dim(tree_seg, seq * TOKENS, TOKENS)
    own_pos = lax.dynamic_slice_in_dim(tree_pos, seq * TOKENS, TOKENS)
    freq = ROPE_BASE ** (-(jnp.arange(128, dtype=F32) * 2.0 / WIDTH))
    angles = own_pos.astype(F32)[:, None] * freq[None, :]
    cos, sin = jnp.cos(angles), jnp.sin(angles)
    back = jnp.arange(16, dtype=jnp.int32)
    block_at = (((at_xh - back % 2) % 2) * 4 + (at_y - back % 8 // 2) % 4) * 2 + jnp.where(
        back < 8, core, 1 - core
    )
    chosen = (block_at[:, None] == back[None, :]).astype(jnp.int32)[:, :, None]
    key_seg = jnp.sum(chosen * tree_seg.reshape(1, 16, TOKENS), axis=1).reshape(1, 2560)
    key_pos = jnp.sum(chosen * tree_pos.reshape(1, 16, TOKENS), axis=1).reshape(1, 2560)
    q_seg, q_pos = own_seg[:, None], own_pos[:, None]
    parent = (key_seg >= 1) & (key_seg <= 4) & (q_seg >= 5) & ((q_seg - 5) // 2 + 1 == key_seg)
    allowed = ((key_seg == q_seg) | (key_seg == 0) | parent) & (key_pos <= q_pos)

    scale_one = lax.rsqrt(jnp.mean(hidden * hidden, axis=-1, keepdims=True) + EPSILON)
    raw_one, _ = after((ff_own, out_own, down_own, cos, sin, allowed, scale_one), raw_one)
    raw_two = other_core(raw_one)
    marks = raw_one.reshape(128, 12, 1152)[:, 9, 768:896]
    gain_one_full = marks[:, :9].reshape(1, 1152).astype(F32)
    gain_two_full = marks[:, 9:18].reshape(1, 1152).astype(F32)
    valid_count = jnp.sum(marks[:, 18].astype(F32))
    out_own, _ = after(raw_one, out_own)
    out_wide = jnp.broadcast_to(out_own[None], (64, 24, 1024))
    out_one = exchange(out_wide, CHIPS)
    out_two = other_core(out_one)
    raw_out = [out_one.reshape(1536, 1024), out_two.reshape(1536, 1024)]
    raw_one, raw_two, _ = after(out_wide, raw_one, raw_two)
    raw = [raw_one.reshape(1536, 1152), raw_two.reshape(1536, 1152)]
    ff_own, _ = after(out_one, ff_own)
    ff_wide = jnp.broadcast_to(ff_own[None], (16, 176, 896))
    ff_all = exchange(ff_wide, PLANE)

    ids = jnp.arange(1536, dtype=jnp.int32)
    dev, j = 2 * (ids // 24) + (ids % 24) // 12, ids % 12
    halves = jnp.arange(256, dtype=jnp.int32)
    inner_ids = jnp.where(halves < 128, 128 * core + halves, 128 * (1 - core) + halves - 128)
    heads_at = jnp.arange(1024, dtype=jnp.int32)
    head_ids = jnp.where(heads_at < 512, 512 * core + heads_at, 512 * (1 - core) + heads_at - 512)
    features = jnp.arange(1152, dtype=jnp.int32)
    put_rows = table(features, jnp.where(j < 9, 9 * dev + j, -1))
    put_inner = table(inner_ids, jnp.where((j >= 9) & (j < 11), 2 * dev + j - 9, -1))
    take_b = table(halves, jnp.where((j >= 9) & (j < 11), 2 * dev + j - 9, -1))
    take_b_out = table(halves, jnp.where((j >= 8) & (j < 10), 2 * dev + j - 8, -1))
    put_mix = table(head_ids, jnp.where(j < 8, 8 * dev + j, -1))
    put_inner_out = table(inner_ids, jnp.where((j >= 8) & (j < 10), 2 * dev + j - 8, -1))
    put_inner_down = table(halves, jnp.where(j >= 10, 2 * dev + j - 10, -1))

    allowed = jnp.concatenate([allowed] * HEADS, axis=0)
    n_one = hidden * scale_one
    u_one = (n_one * (1.0 + gain_one_full)).astype(BF)
    u_rows = dot(u_one, put_rows).astype(BF)
    inner = [dot(u_rows, raw[i][:, 768:]).astype(BF) for i in (0, 1)]
    sides = []
    for i in range(3):
        part = jnp.concatenate([inner[0][:, 128 * i : 128 * i + 128], inner[1][:, 128 * i : 128 * i + 128]], axis=1)
        sides.append(u_rows + dot(part, put_inner).astype(BF))
    kk = pick(is_first, *[dot(sides[1], raw[i][:, 512:640]) for i in (0, 1)])
    vv = pick(is_first, *[dot(sides[2], raw[i][:, 640:768]) for i in (0, 1)])
    kv_own = jnp.concatenate([turn(jnp.concatenate(kk, axis=1), cos, sin), vv[0], vv[1]], axis=1).astype(BF)

    pair = jnp.concatenate([kv_own, other_half(kv_own)], axis=0)
    kv_parts = [pair] + list(after(ff_wide, *[shift(pair, "y", k) for k in (1, 2, 3)])[:3])
    kv_mine = jnp.concatenate(kv_parts, axis=0)
    kv = jnp.concatenate([kv_mine, other_core(kv_mine)], axis=0)
    keys, values = kv[:, :256], kv[:, 256:]
    queries = [dot(sides[0], raw[i][:, :512]) for i in (0, 1)]
    q_rows = jnp.concatenate(
        [turn(queries[h // 2][:, WIDTH * (h % 2) : WIDTH * (h % 2 + 1)], cos, sin) for h in range(HEADS)],
        axis=0,
    ).astype(BF)
    scores = jnp.where(allowed, dot_tr(q_rows, keys) * score_scale, MASKED_SCORE)
    top = jnp.max(scores, axis=-1, keepdims=True)
    ex = jnp.exp(scores - top)
    total = jnp.sum(ex, axis=-1, keepdims=True)
    lse = top + jnp.log(total)
    mix_rows = dot((ex / total).astype(BF), values).astype(BF)
    mix = jnp.concatenate([mix_rows[TOKENS * h : TOKENS * (h + 1)] for h in range(HEADS)], axis=1)
    mix_placed = dot(mix, put_mix).astype(BF)
    inner_out = jnp.concatenate([dot(mix_placed, raw_out[i][:, 640:768]) for i in (0, 1)], axis=1).astype(BF)
    side_out = mix_placed + dot(inner_out, put_inner_out).astype(BF)
    left, right = pick(is_first, *[dot(side_out, raw_out[i][:, :640]) for i in (0, 1)])
    after_att = hidden + jnp.concatenate([left, right[:, 128:]], axis=1)

    scale_two, n_two, u_two = norm_parts(after_att, gain_two_full)
    u_all = gather_tokens(u_two)

    raw_late, out_late, ff_all, _ = after(u_two, raw, raw_out, ff_all)
    down_own, _ = after(ff_all, down_own)
    down_raw = exchange(jnp.broadcast_to(down_own[None], (16, 56, 1408)), PLANE).reshape(896, 1408)
    b_left, b_right = pick(is_first, *[dot(take_b, raw_late[i][:, :768]).astype(BF) for i in (0, 1)])
    left, right = pick(is_first, *[dot(take_b_out, out_late[i][:, :640]).astype(BF) for i in (0, 1)])
    b_out = jnp.concatenate([left, right[:, 128:]], axis=1)
    left, right = pick(is_first, *[dot(put_inner_down, out_late[i][:, :640]).astype(BF) for i in (0, 1)])
    b_down = jnp.concatenate([left, right[:, 128:]], axis=1)
    a_gate, a_up = pick(is_first, *[dot(put_rows, out_late[i][:, 768:]).astype(BF) for i in (0, 1)])
    b_gate = ff_all[:, 144:160].reshape(256, 896)
    b_up = ff_all[:, 160:].reshape(256, 896)
    w_gate = (ff_all[:, :72].reshape(1152, 896).astype(F32) + dot(a_gate, b_gate)).astype(BF)
    w_up = (ff_all[:, 72:144].reshape(1152, 896).astype(F32) + dot(a_up, b_up)).astype(BF)

    a_down = down_raw[:, 1152:]
    w_down = (down_raw[:, :1152].astype(F32) + dot(a_down, b_down)).astype(BF)

    gate = dot(u_all, w_gate)
    up = dot(u_all, w_up)
    act, act_pull = jax.vjp(lambda g, u: jax.nn.gelu(g, approximate=True) * u, gate, up)
    act = act.astype(BF)
    result = after_att + scatter_tokens(dot(act, w_down))

    valid = loss_token_mask[0].astype(F32)[:, None]
    error = result - teacher[0].astype(F32)
    loss_here = jnp.sum(valid * error * error)
    grad_result = 2.0 * 20480.0 / valid_count * valid * error

    g_all = gather_tokens(grad_result.astype(BF))
    g_act = dot_tr(g_all, w_down).astype(BF)
    g_gate, g_up = act_pull(g_act.astype(F32))
    g_gate, g_up = g_gate.astype(BF), g_up.astype(BF)
    g_u_part = dot_tr(g_gate, w_gate) + dot_tr(g_up, w_up)
    g_u_two = scatter_tokens(g_u_part)
    u_all, act, g_all, g_gate, g_up, _ = after(g_u_part, u_all, act, g_all, g_gate, g_up)
    gw_gate = dot_tl(u_all, g_gate).astype(BF)
    gb_gate = dot_tl(a_gate, gw_gate).astype(BF)
    gate_grads = jnp.concatenate([gw_gate.reshape(16, 72, 896), gb_gate.reshape(16, 16, 896)], axis=1)
    gate_first = leave(gate_grads.reshape(4, 4, 88, 896), "z", 0, at_z, at_x)
    gw_up = dot_tl(u_all, g_up).astype(BF)
    gb_up = dot_tl(a_up, gw_up).astype(BF)
    up_grads = jnp.concatenate([gw_up.reshape(16, 72, 896), gb_up.reshape(16, 16, 896)], axis=1)
    up_first = leave(up_grads.reshape(4, 4, 88, 896), "x", 1, at_z, at_x)
    gw_down = dot_tl(act, g_all).astype(BF)
    gb_down = dot_tl(a_down, gw_down).astype(BF)
    down_first = leave(gw_down.reshape(4, 4, 56, 1152), "z", 0, at_z, at_x)

    norm_two_back = norm_back(scale_two, n_two, gain_two_full, g_u_two)
    g_after = grad_result + norm_two_back
    g_after_b = g_after.astype(BF)
    once = jnp.where(jnp.arange(640) < 128, 0, 1).astype(BF)[None]
    g_half = pick(is_first, g_after_b[:, :640], g_after_b[:, 512:])
    g_once = pick(is_first, g_after_b[:, :640], g_after_b[:, 512:] * once)
    d_out = dot_tr(g_once[0], raw_out[0][:, :640]) + dot_tr(g_once[1], raw_out[1][:, :640])
    gi_out = dot_tr(d_out.astype(BF), put_inner_out).astype(BF)
    d_out = (
        d_out
        + dot_tr(gi_out[:, :128], raw_out[0][:, 640:768])
        + dot_tr(gi_out[:, 128:], raw_out[1][:, 640:768])
    )
    g_mix = dot_tr(d_out.astype(BF), put_mix).astype(BF)
    g_rows = jnp.concatenate([g_mix[:, WIDTH * h : WIDTH * (h + 1)] for h in range(HEADS)], axis=0)
    scores_again = jnp.where(allowed, dot_tr(q_rows, keys) * score_scale, MASKED_SCORE)
    probs = jnp.where(allowed, jnp.exp(scores_again - lse), 0.0)
    g_probs = dot_tr(g_rows, values)
    g_scores = (probs * (g_probs - jnp.sum(probs * g_probs, axis=-1, keepdims=True))).astype(BF)
    gate_first, up_first, _ = after(g_scores, gate_first, up_first)
    gate_line, up_line = add(gate_first).astype(BF), add(up_first).astype(BF)
    gate_second = leave(gate_line, "x", 0, at_z, at_x)
    up_second = leave(up_line, "z", 0, at_z, at_x)
    g_scores, probs, _ = after((gate_line, up_line), g_scores, probs)
    g_keys = dot_tl(g_scores, q_rows) * score_scale
    g_values = dot_tl(probs.astype(BF), g_rows)
    g_kv = jnp.concatenate([g_keys, g_values], axis=1)
    n_mine = 8 * TOKENS
    g_kv_sum = g_kv[:n_mine] + other_core(g_kv[n_mine:].astype(BF)).astype(F32)
    g_kv_b = g_kv_sum.astype(BF)
    g_parts = [shift(g_kv_b[320 * k : 320 * (k + 1)], "y", 4 - k) for k in (1, 2, 3)]
    g_scores, side_out, gate_second, up_second, down_first, gb_down, _ = after(
        g_kv_b, g_scores, side_out, gate_second, up_second, down_first, gb_down
    )
    g_q_rows = dot(g_scores, keys) * score_scale
    g_q = [
        jnp.concatenate(
            [turn_back(g_q_rows[TOKENS * h : TOKENS * (h + 1)], cos, sin) for h in (2 * i, 2 * i + 1)],
            axis=1,
        ).astype(BF)
        for i in (0, 1)
    ]
    gate_sum, up_sum = add(gate_second).astype(BF), add(up_second).astype(BF)
    ga_part = jnp.concatenate(
        [dot_tr(gate_sum[:72], b_gate), dot_tr(up_sum[:72], b_up), jnp.zeros((72, 384), F32)], axis=1
    ).astype(BF)
    back_row = jnp.arange(256, dtype=jnp.int32)
    group, line = back_row // 32, back_row % 32
    take = jnp.where(
        line < 9,
        9 * group + line,
        jnp.where(
            line < 18,
            88 + 9 * group + line - 9,
            jnp.where(
                line < 22,
                72 + 88 * ((line - 18) // 2) + 2 * group + line % 2,
                jnp.where(line < 31, 176 + 9 * group + line - 22, -1),
            ),
        ),
    )
    leaving = dot(
        table(take, jnp.arange(248, dtype=jnp.int32)), jnp.concatenate([gate_sum, up_sum, ga_part], axis=0)
    ).astype(BF)
    slab = exchange(leaving.reshape(8, 32, 896), ("y", "c"))
    def of_chip(own, away):
        return (own.astype(F32) + other_core(away.astype(BF)).astype(F32)).astype(BF).reshape(64, 24, -1)

    def both_halves(owned):
        mine, away = pick(is_first, owned[:12], owned[12:])
        return pick(is_first, mine, other_core(away.astype(BF)).astype(F32))

    loss_high, loss_rest = split_in_two(loss_here)
    loss_mid, loss_low = split_in_two(loss_rest)
    lines = jnp.arange(16, dtype=jnp.int32)
    loss_rows = jnp.where(
        lines == 0,
        loss_high.astype(F32),
        jnp.where(lines == 1, loss_mid.astype(F32), jnp.where(lines == 2, loss_low, 0.0)),
    )
    more_side = (loss_rows[:, None] * (j == 11)[None, :]).astype(BF)
    more_grad = table(jnp.where(lines < 3, lines + 3 * core, -1), jnp.arange(512, dtype=jnp.int32))
    chip_q = of_chip(
        *[(dot_tl(sides[0], g_q[i]) + dot_tl(more_side, more_grad)).astype(BF) for i in (0, 1)]
    )
    g_parts = after(chip_q, *g_parts)[:3]
    g_pair = add([g_kv_sum[:320]] + list(g_parts))
    away = other_half(g_pair[160:].astype(BF))
    side_out, _ = after(g_pair, side_out)
    left, right = pick(is_first, gb_down[:, :640], gb_down[:, 512:])
    chip_out = of_chip(
        dot_tl(side_out, g_half[0]) + dot_tl(put_inner_down, left),
        dot_tl(side_out, g_half[1]) + dot_tl(put_inner_down, right),
    )
    g_kv_own = g_pair[:160] + after((leaving, chip_out), away)[0].astype(F32)
    g_k = turn_back(g_kv_own[:, :256], cos, sin).astype(BF)
    g_v = g_kv_own[:, 256:].astype(BF)
    g_k = pick(is_first, g_k[:, :128], g_k[:, 128:])
    g_v = pick(is_first, g_v[:, :128], g_v[:, 128:])
    chip_kv = of_chip(
        *[
            jnp.concatenate([dot_tl(sides[1], g_k[i]).astype(BF), dot_tl(sides[2], g_v[i]).astype(BF)], axis=1)
            for i in (0, 1)
        ]
    )
    chip_sums = jnp.concatenate([chip_q, chip_kv, chip_out], axis=2)
    parts = exchange(chip_sums, CHIPS)
    down_first, _ = after(g_kv_own, down_first)
    down_second = leave(add(down_first).astype(BF), "x", 0, at_z, at_x)
    slab, down_second, g_q, g_k, g_v, _ = after(chip_sums, slab, down_second, g_q, g_k, g_v)

    d_one = None
    for i, (g, first, last) in enumerate(((g_q, 0, 512), (g_k, 512, 640), (g_v, 640, 768))):
        d = dot_tr(g[0], raw[0][:, first:last]) + dot_tr(g[1], raw[1][:, first:last])
        gi = dot_tr(d.astype(BF), put_inner).astype(BF)
        inner_at = 768 + 128 * i
        d = d + dot_tr(gi[:, :128], raw[0][:, inner_at : inner_at + 128])
        d = d + dot_tr(gi[:, 128:], raw[1][:, inner_at : inner_at + 128])
        d_one = d if d_one is None else d_one + d
    g_u_one = select_back(d_one, put_rows)
    grad_hidden = (g_after + norm_back(scale_one, n_one, gain_one_full, g_u_one)).astype(BF)

    narrow = dot_tr(slab.reshape(256, 896), wider).reshape(8, 32, 864)
    wide = jnp.concatenate([narrow[t] for t in range(8)], axis=1)
    ga = jnp.sum(slab[:, 22:31, :512].astype(F32), axis=0)
    gw_down_own = lax.ppermute(
        add(down_second).astype(BF), EVERY, [(b, a) for a, b in down_route()]
    )[:54]
    ga_down_own = dot_tr(gw_down_own, b_down)

    def over_columns(pairs):
        return sum(jnp.sum(a.astype(F32) * b, axis=1) for a, b in pairs)

    gain_two_own = over_columns(
        ((wg, wide[:9]), (wu, wide[9:18]), (ag, ga[:, :256]), (au, ga[:, 256:]))
    ) / (1.0 + gain_two.astype(F32))

    owned = jnp.sum(parts.astype(F32), axis=0)
    loss_value = jnp.sum(owned[11, :6]) / (1152.0 * valid_count)
    left, right = both_halves(owned)
    own_out = jnp.concatenate([left[:, 768:], right[:, 896:]], axis=1)
    ga_out_own = dot_tr(own_out[:8].astype(BF), b_out)
    left_b, right_b = left[:9].astype(BF), right[:9].astype(BF)
    ga_own = [
        dot_tr(left_b[:, first:last], b_left[:, first:last])
        + dot_tr(right_b[:, first:last], b_right[:, first:last])
        for first, last in ((0, 512), (512, 640), (640, 768))
    ]

    def columns(first, last, rows):
        return jnp.concatenate([left[rows, first:last], right[rows, first:last]], axis=1)

    top_rows, low_rows = slice(0, 9), slice(9, 11)
    gw_own = [columns(0, 512, top_rows), columns(512, 640, top_rows), columns(640, 768, top_rows)]
    gain_one_own = over_columns(
        list(zip((wq, wk, wv), gw_own)) + list(zip((aq, ak, av), ga_own))
    ) / (1.0 + gain_one.astype(F32))

    return (
        result.astype(BF)[None],
        loss_value,
        grad_hidden[None],
        gain_one_own,
        *gw_own,
        own_out[:8],
        ga_own[0],
        columns(0, 512, low_rows),
        ga_own[1],
        columns(512, 640, low_rows),
        ga_own[2],
        columns(640, 768, low_rows),
        ga_out_own,
        own_out[8:10],
        gain_two_own,
        wide[:9],
        wide[9:18],
        gw_down_own.astype(F32),
        ga[:, :256],
        wide[18:20],
        ga[:, 256:],
        wide[20:22],
        ga_down_own,
        own_out[10:],
    )


def solution(mesh):
    mesh = Mesh(mesh.devices.reshape([SIZES[a] for a in EVERY]), EVERY)
    tree, seq = ("z", "xl"), ("xh", "y", "c")
    rows = P(EVERY, None)
    vector = P(EVERY)
    return jax.shard_map(
        on_device,
        mesh=mesh,
        in_specs=(
            P(tree, seq, None),
            P(tree, None),
            P(tree, None),
            P(tree, seq),
            P(tree, seq, None),
            vector,
        )
        + (rows,) * 12
        + (vector,)
        + (rows,) * 9,
        out_specs=(P(tree, seq, None), P(), P(tree, seq, None), vector)
        + (rows,) * 12
        + (vector,)
        + (rows,) * 9,
        check_vma=False,
    )
```

```python
import jax
import jax.numpy as jnp
from jax import lax
from jax.sharding import Mesh, PartitionSpec as P

EPSILON = 1e-06
ROPE_BASE = 10000.0
MASKED_SCORE = -1e30
BF = jnp.bfloat16
F32 = jnp.float32

PLANE = ("z", "xl", "xh")
CHIPS = ("z", "xl", "xh", "y")
EVERY = ("z", "xl", "xh", "y", "c")
SIZES = dict(z=4, xl=2, xh=2, y=4, c=2)
RING = dict(z="z", x=("xl", "xh"), y="y")
TOKENS = 160
HEADS = 4
WIDTH = 256


def dot(a, b):
    return jnp.dot(a, b, preferred_element_type=F32)


def dot_tl(a, b):
    return lax.dot_general(a, b, (((0,), (0,)), ((), ())), preferred_element_type=F32)


def dot_tr(a, b):
    return lax.dot_general(a, b, (((1,), (1,)), ((), ())), preferred_element_type=F32)


def exchange(x, axes):
    return lax.all_to_all(x, axes, split_axis=0, concat_axis=0, tiled=True)


def other_core(x):
    return lax.ppermute(x, "c", [(0, 1), (1, 0)])


def other_half(x):
    return lax.ppermute(x, "xh", [(0, 1), (1, 0)])


def shift(x, axis, k):
    number = [0, 2, 1, 3] if axis == "x" else [0, 1, 2, 3]
    return lax.ppermute(x, RING[axis], [(number[i], number[(i + k) % 4]) for i in range(4)])


def pick(cond, a, b):
    return jnp.where(cond, a, b), jnp.where(cond, b, a)


def split_in_two(x):
    high = x.astype(BF)
    return high, x - high.astype(F32)


def select_back(x, table):
    high, low = split_in_two(x)
    return dot_tr(high, table) + dot_tr(low.astype(BF), table)


def down_route():
    pairs = []
    for o in range(16):
        for t in range(8):
            block = 8 * (o % 2) + t
            pairs.append((8 * o + t, 8 * (block % 4 * 4 + block // 4) + o // 2))
    return pairs


def ring_place(axis, k, at_z, at_x):
    return (at_z - k) % 4 if axis == "z" else (at_x - k) % 4 % 2 * 2 + (at_x - k) % 4 // 2


def placed(parts, axis, at_z, at_x):
    stack = jnp.zeros((4,) + parts[0].shape, parts[0].dtype)
    for k, part in enumerate(parts):
        stack = lax.dynamic_update_index_in_dim(stack, part, ring_place(axis, k, at_z, at_x), 0)
    return stack


def leave(x, axis, dim, at_z, at_x):
    parts = []
    for k in range(4):
        block = lax.dynamic_index_in_dim(x, ring_place(axis, k, at_z, at_x), dim, keepdims=False)
        parts.append(shift(block, axis, 4 - k) if k else block)
    return parts


def add(parts):
    total = parts[0].astype(F32)
    for p in parts[1:]:
        total = total + p.astype(F32)
    return total


def norm_parts(values, gain):
    scale = lax.rsqrt(jnp.mean(values * values, axis=-1, keepdims=True) + EPSILON)
    n = values * scale
    return scale, n, (n * (1.0 + gain)).astype(BF)


def norm_back(scale, n, gain, grad):
    m = grad * (1.0 + gain)
    back = scale * (m - n * jnp.mean(m * n, axis=-1, keepdims=True))
    return back


def turn(x, cos, sin):
    h = cos.shape[-1]
    a, b = x[:, :h], x[:, h:]
    return jnp.concatenate([a * cos - b * sin, b * cos + a * sin], axis=-1)


def turn_back(x, cos, sin):
    return turn(x, cos, -sin)


def gather_tokens(x):
    mine = [x] + [shift(x, "y", k) for k in (1, 2, 3)]
    return jnp.concatenate(mine + [other_core(p) for p in mine], axis=0)


def scatter_tokens(part):
    blocks = part.reshape(2, 4, TOKENS, -1)
    total = None
    for k in (2, 1, 3, 0):
        piece = blocks[0, k] + other_core(blocks[1, k].astype(BF)).astype(F32)
        if k:
            piece = shift(piece.astype(BF), "y", 4 - k).astype(F32)
        total = piece if total is None else total + piece
    return total


def after(done, *values):
    return tuple(lax.optimization_barrier((v, done))[0] for v in values) + (done,)


def table(rows, columns):
    return (rows[:, None] == columns[None, :]).astype(BF)


def on_device(
    layer_input,
    segment,
    position,
    loss_token_mask,
    teacher,
    gain_one,
    wq,
    wk,
    wv,
    wo,
    aq,
    bq,
    ak,
    bk,
    av,
    bv,
    ao,
    bo,
    gain_two,
    wg,
    wu,
    wd,
    ag,
    bg,
    au,
    bu,
    ad,
    bd,
):
    core = lax.axis_index("c")
    at_z, at_y = lax.axis_index("z"), lax.axis_index("y")
    at_xl, at_xh = lax.axis_index("xl"), lax.axis_index("xh")
    at_x = 2 * at_xh + at_xl
    is_first = core == 0
    score_scale = WIDTH**-0.5
    count_here = jnp.sum(loss_token_mask[0]).astype(BF)

    extra = jnp.concatenate([gain_one[None], gain_two[None], count_here.reshape(1, 1)], axis=1)
    extra = jnp.pad(extra, ((0, 1), (0, 384 - 19)))

    def attention_half(k):
        top = jnp.concatenate(
            [m[:, m.shape[1] // 2 * k : m.shape[1] // 2 * (k + 1)] for m in (wq, wk, wv, aq, ak, av)],
            axis=1,
        )
        low = jnp.concatenate(
            [m[:, m.shape[1] // 2 * k : m.shape[1] // 2 * (k + 1)] for m in (bq, bk, bv)] + [extra],
            axis=1,
        )
        return jnp.concatenate([top, low, jnp.zeros((1, 1152), BF)], axis=0)

    keep, send = pick(is_first, attention_half(0), attention_half(1))
    lower, upper = pick(is_first, keep, other_core(send))
    att_own = jnp.concatenate([lower, upper], axis=0)
    att_wide = jnp.broadcast_to(att_own[None], (64, 24, 1152))
    raw_one = exchange(att_wide, CHIPS)
    (layer_input, wg, wu, bg, bu, wd, ad, ag, au, wo, ao, bo, bd, segment, position, core, at_z, _) = after(
        att_wide,
        layer_input, wg, wu, bg, bu, wd, ad, ag, au, wo, ao, bo, bd, segment, position, core, at_z,
    )
    is_first = core == 0
    hidden = layer_input[0].astype(F32)

    def output_half(k):
        wide = jnp.concatenate([m[:, 512 * k : 512 * k + 640] for m in (wo, bo, bd)], axis=0)
        narrow = jnp.pad(ao[:, 128 * k : 128 * k + 128], ((0, 4), (0, 0)))
        return jnp.concatenate([wide, narrow, jnp.pad((ag, au)[k], ((0, 3), (0, 0)))], axis=1)

    keep, send = pick(is_first, output_half(0), output_half(1))
    lower, upper = pick(is_first, keep, other_core(send))
    out_own = jnp.concatenate([lower, upper], axis=0)

    def column_of(k):
        return 2 * ((at_y + k // 2) % 4) + (core + k) % 2

    def column_shift(x, k):
        route = []
        for y in range(4):
            for c in range(2):
                route.append((2 * y + c, 2 * ((y + k // 2) % 4) + (c + k) % 2))
        return lax.ppermute(x, ("y", "c"), route)

    rows22 = jnp.pad(jnp.concatenate([wg, wu, bg, bu], axis=0), ((0, 2), (0, 0)))
    rows22 = jnp.concatenate([rows22[:, 864 * t : 864 * (t + 1)] for t in range(8)], axis=0)
    wider = jnp.arange(896, dtype=jnp.int32)
    wider = table(jnp.arange(864, dtype=jnp.int32), jnp.where(wider % 56 < 54, wider // 56 * 54 + wider % 56, -1))
    rows22 = dot(rows22, wider).astype(BF).reshape(8, 24, 896)
    down_own = lax.ppermute(
        jnp.pad(jnp.concatenate([wd, ad], axis=1), ((0, 2), (0, 0))), EVERY, down_route()
    )
    seq = (at_xh * 4 + at_y) * 2 + core
    tree_seg = segment[0]
    tree_pos = position[0]
    own_seg = lax.dynamic_slice_in_dim(tree_seg, seq * TOKENS, TOKENS)
    own_pos = lax.dynamic_slice_in_dim(tree_pos, seq * TOKENS, TOKENS)
    freq = ROPE_BASE ** (-(jnp.arange(128, dtype=F32) * 2.0 / WIDTH))
    angles = own_pos.astype(F32)[:, None] * freq[None, :]
    cos, sin = jnp.cos(angles), jnp.sin(angles)
    back = jnp.arange(16, dtype=jnp.int32)
    block_at = (((at_xh - back % 2) % 2) * 4 + (at_y - back % 8 // 2) % 4) * 2 + jnp.where(
        back < 8, core, 1 - core
    )
    chosen = (block_at[:, None] == back[None, :]).astype(jnp.int32)[:, :, None]
    key_seg = jnp.sum(chosen * tree_seg.reshape(1, 16, TOKENS), axis=1).reshape(1, 2560)
    key_pos = jnp.sum(chosen * tree_pos.reshape(1, 16, TOKENS), axis=1).reshape(1, 2560)
    q_seg, q_pos = own_seg[:, None], own_pos[:, None]
    parent = (key_seg >= 1) & (key_seg <= 4) & (q_seg >= 5) & ((q_seg - 5) // 2 + 1 == key_seg)
    allowed = ((key_seg == q_seg) | (key_seg == 0) | parent) & (key_pos <= q_pos)

    scale_one = lax.rsqrt(jnp.mean(hidden * hidden, axis=-1, keepdims=True) + EPSILON)
    raw_one, _ = after((rows22, out_own, down_own, cos, sin, allowed, scale_one), raw_one)
    raw_two = other_core(raw_one)
    marks = raw_one.reshape(128, 12, 1152)[:, 9, 768:896]
    gain_one_full = marks[:, :9].reshape(1, 1152).astype(F32)
    gain_two_full = marks[:, 9:18].reshape(1, 1152).astype(F32)
    valid_count = jnp.sum(marks[:, 18].astype(F32))
    out_own, _ = after(raw_one, out_own)
    out_wide = jnp.broadcast_to(out_own[None], (64, 24, 1024))
    out_one = exchange(out_wide, CHIPS)
    out_two = other_core(out_one)
    raw_out = [out_one.reshape(1536, 1024), out_two.reshape(1536, 1024)]
    raw_one, raw_two, _ = after(out_wide, raw_one, raw_two)
    raw = [raw_one.reshape(1536, 1152), raw_two.reshape(1536, 1152)]
    ids = jnp.arange(1536, dtype=jnp.int32)
    dev, j = 2 * (ids // 24) + (ids % 24) // 12, ids % 12
    halves = jnp.arange(256, dtype=jnp.int32)
    inner_ids = jnp.where(halves < 128, 128 * core + halves, 128 * (1 - core) + halves - 128)
    heads_at = jnp.arange(1024, dtype=jnp.int32)
    head_ids = jnp.where(heads_at < 512, 512 * core + heads_at, 512 * (1 - core) + heads_at - 512)
    features = jnp.arange(1152, dtype=jnp.int32)
    put_rows = table(features, jnp.where(j < 9, 9 * dev + j, -1))
    put_inner = table(inner_ids, jnp.where((j >= 9) & (j < 11), 2 * dev + j - 9, -1))
    take_b = table(halves, jnp.where((j >= 9) & (j < 11), 2 * dev + j - 9, -1))
    take_b_out = table(halves, jnp.where((j >= 8) & (j < 10), 2 * dev + j - 8, -1))
    put_mix = table(head_ids, jnp.where(j < 8, 8 * dev + j, -1))
    put_inner_out = table(inner_ids, jnp.where((j >= 8) & (j < 10), 2 * dev + j - 8, -1))
    put_inner_down = table(halves, jnp.where(j >= 10, 2 * dev + j - 10, -1))

    allowed = jnp.concatenate([allowed] * HEADS, axis=0)
    n_one = hidden * scale_one
    u_one = (n_one * (1.0 + gain_one_full)).astype(BF)
    u_rows = dot(u_one, put_rows).astype(BF)
    inner = [dot(u_rows, raw[i][:, 768:]).astype(BF) for i in (0, 1)]
    sides = []
    for i in range(3):
        part = jnp.concatenate([inner[0][:, 128 * i : 128 * i + 128], inner[1][:, 128 * i : 128 * i + 128]], axis=1)
        sides.append(u_rows + dot(part, put_inner).astype(BF))
    kk = pick(is_first, *[dot(sides[1], raw[i][:, 512:640]) for i in (0, 1)])
    vv = pick(is_first, *[dot(sides[2], raw[i][:, 640:768]) for i in (0, 1)])
    kv_own = jnp.concatenate([turn(jnp.concatenate(kk, axis=1), cos, sin), vv[0], vv[1]], axis=1).astype(BF)

    pair = jnp.concatenate([kv_own, other_half(kv_own)], axis=0)
    rows22, down_own, _ = after(kv_own, rows22, down_own)
    slab = []
    for k in range(8):
        piece = lax.dynamic_index_in_dim(rows22, column_of(k), 0, keepdims=False)
        slab.append(column_shift(piece, k) if k else piece)
    slab = jnp.concatenate(slab, axis=0)
    back = jnp.arange(8, dtype=jnp.int32)
    sources = 2 * ((at_y - back // 2) % 4) + (core - back) % 2
    row = jnp.arange(176, dtype=jnp.int32)
    low = row - 144
    at_row = jnp.where(
        row < 72,
        row // 9 * 24 + row % 9,
        jnp.where(
            row < 144,
            (row - 72) // 9 * 24 + 9 + (row - 72) % 9,
            low % 16 // 2 * 24 + 18 + low // 16 * 2 + low % 2,
        ),
    )
    in_slab = jnp.arange(192, dtype=jnp.int32)
    in_slab = jnp.repeat(sources, 24) * 24 + in_slab % 24
    ff_own = dot(table(at_row, in_slab), slab).astype(BF)
    down_line = placed([down_own] + [shift(down_own, "z", k) for k in (1, 2, 3)], "z", at_z, at_x)
    ff_own, _ = after((out_one, down_line), ff_own)
    ff_wide = jnp.broadcast_to(ff_own[None], (16, 176, 896))
    ff_all = exchange(ff_wide, PLANE)
    down_parts = [down_line] + [shift(down_line, "x", k) for k in (1, 2, 3)]
    kv_parts = [pair] + list(after(ff_wide, *[shift(pair, "y", k) for k in (1, 2, 3)])[:3])
    kv_mine = jnp.concatenate(kv_parts, axis=0)
    kv = jnp.concatenate([kv_mine, other_core(kv_mine)], axis=0)
    keys, values = kv[:, :256], kv[:, 256:]
    queries = [dot(sides[0], raw[i][:, :512]) for i in (0, 1)]
    q_rows = jnp.concatenate(
        [turn(queries[h // 2][:, WIDTH * (h % 2) : WIDTH * (h % 2 + 1)], cos, sin) for h in range(HEADS)],
        axis=0,
    ).astype(BF)
    scores = jnp.where(allowed, dot_tr(q_rows, keys) * score_scale, MASKED_SCORE)
    top = jnp.max(scores, axis=-1, keepdims=True)
    ex = jnp.exp(scores - top)
    total = jnp.sum(ex, axis=-1, keepdims=True)
    lse = top + jnp.log(total)
    mix_rows = dot((ex / total).astype(BF), values).astype(BF)
    mix = jnp.concatenate([mix_rows[TOKENS * h : TOKENS * (h + 1)] for h in range(HEADS)], axis=1)
    mix_placed = dot(mix, put_mix).astype(BF)
    inner_out = jnp.concatenate([dot(mix_placed, raw_out[i][:, 640:768]) for i in (0, 1)], axis=1).astype(BF)
    side_out = mix_placed + dot(inner_out, put_inner_out).astype(BF)
    left, right = pick(is_first, *[dot(side_out, raw_out[i][:, :640]) for i in (0, 1)])
    after_att = hidden + jnp.concatenate([left, right[:, 128:]], axis=1)

    scale_two, n_two, u_two = norm_parts(after_att, gain_two_full)
    u_all = gather_tokens(u_two)

    raw_late, out_late, _ = after(u_two, raw, raw_out)
    b_left, b_right = pick(is_first, *[dot(take_b, raw_late[i][:, :768]).astype(BF) for i in (0, 1)])
    left, right = pick(is_first, *[dot(take_b_out, out_late[i][:, :640]).astype(BF) for i in (0, 1)])
    b_out = jnp.concatenate([left, right[:, 128:]], axis=1)
    left, right = pick(is_first, *[dot(put_inner_down, out_late[i][:, :640]).astype(BF) for i in (0, 1)])
    b_down = jnp.concatenate([left, right[:, 128:]], axis=1)
    a_gate, a_up = pick(is_first, *[dot(put_rows, out_late[i][:, 768:]).astype(BF) for i in (0, 1)])
    ff_all, _ = after((b_left, b_right, b_out, b_down, a_gate, a_up), ff_all)
    b_gate = ff_all[:, 144:160].reshape(256, 896)
    b_up = ff_all[:, 160:].reshape(256, 896)
    w_gate = (ff_all[:, :72].astype(F32) + dot(a_gate, b_gate).reshape(16, 72, 896)).astype(BF)
    w_up = (ff_all[:, 72:144].astype(F32) + dot(a_up, b_up).reshape(16, 72, 896)).astype(BF)
    w_gate, w_up = w_gate.reshape(1152, 896), w_up.reshape(1152, 896)
    down_parts, _ = after(w_up, down_parts)
    down_raw = placed(down_parts, "x", at_z, at_x).reshape(896, 1408)
    a_down = down_raw[:, 1152:]
    w_down = (down_raw[:, :1152].astype(F32) + dot(a_down, b_down)).astype(BF)

    gate = dot(u_all, w_gate)
    up = dot(u_all, w_up)
    act, act_pull = jax.vjp(lambda g, u: jax.nn.gelu(g, approximate=True) * u, gate, up)
    act = act.astype(BF)
    result = after_att + scatter_tokens(dot(act, w_down))

    valid = loss_token_mask[0].astype(F32)[:, None]
    error = result - teacher[0].astype(F32)
    loss_here = jnp.sum(valid * error * error)
    grad_result = 2.0 * 20480.0 / valid_count * valid * error

    g_all = gather_tokens(grad_result.astype(BF))
    g_act = dot_tr(g_all, w_down).astype(BF)
    g_gate, g_up = act_pull(g_act.astype(F32))
    g_gate, g_up = g_gate.astype(BF), g_up.astype(BF)
    g_u_part = dot_tr(g_gate, w_gate) + dot_tr(g_up, w_up)
    g_u_two = scatter_tokens(g_u_part)
    u_all, act, g_all, g_gate, g_up, _ = after(g_u_part, u_all, act, g_all, g_gate, g_up)
    gw_gate = dot_tl(u_all, g_gate).astype(BF)
    gb_gate = dot_tl(a_gate, gw_gate).astype(BF)
    gate_grads = jnp.concatenate([gw_gate.reshape(16, 72, 896), gb_gate.reshape(16, 16, 896)], axis=1)
    gate_first = leave(gate_grads.reshape(4, 4, 88, 896), "z", 0, at_z, at_x)
    gw_up = dot_tl(u_all, g_up).astype(BF)
    gb_up = dot_tl(a_up, gw_up).astype(BF)
    up_grads = jnp.concatenate([gw_up.reshape(16, 72, 896), gb_up.reshape(16, 16, 896)], axis=1)
    up_first = leave(up_grads.reshape(4, 4, 88, 896), "x", 1, at_z, at_x)
    gw_down = dot_tl(act, g_all).astype(BF)
    gb_down = dot_tl(a_down, gw_down).astype(BF)

    norm_two_back = norm_back(scale_two, n_two, gain_two_full, g_u_two)
    g_after = grad_result + norm_two_back
    g_after_b = g_after.astype(BF)
    once = jnp.where(jnp.arange(640) < 128, 0, 1).astype(BF)[None]
    g_half = pick(is_first, g_after_b[:, :640], g_after_b[:, 512:])
    g_once = pick(is_first, g_after_b[:, :640], g_after_b[:, 512:] * once)
    d_out = dot_tr(g_once[0], raw_out[0][:, :640]) + dot_tr(g_once[1], raw_out[1][:, :640])
    gi_out = dot_tr(d_out.astype(BF), put_inner_out).astype(BF)
    d_out = (
        d_out
        + dot_tr(gi_out[:, :128], raw_out[0][:, 640:768])
        + dot_tr(gi_out[:, 128:], raw_out[1][:, 640:768])
    )
    g_mix = dot_tr(d_out.astype(BF), put_mix).astype(BF)
    g_rows = jnp.concatenate([g_mix[:, WIDTH * h : WIDTH * (h + 1)] for h in range(HEADS)], axis=0)
    scores_again = jnp.where(allowed, dot_tr(q_rows, keys) * score_scale, MASKED_SCORE)
    probs = jnp.where(allowed, jnp.exp(scores_again - lse), 0.0)
    g_probs = dot_tr(g_rows, values)
    g_scores = (probs * (g_probs - jnp.sum(probs * g_probs, axis=-1, keepdims=True))).astype(BF)
    g_keys = dot_tl(g_scores, q_rows) * score_scale
    g_values = dot_tl(probs.astype(BF), g_rows)
    g_kv = jnp.concatenate([g_keys, g_values], axis=1)
    n_mine = 8 * TOKENS
    gate_first, up_first, _ = after(g_kv, gate_first, up_first)
    gate_line, up_line = add(gate_first).astype(BF), add(up_first).astype(BF)
    gate_second = leave(gate_line, "x", 0, at_z, at_x)
    up_second = leave(up_line, "z", 0, at_z, at_x)
    g_away, _ = after((gate_line, up_line), g_kv[n_mine:].astype(BF))
    g_kv_sum = g_kv[:n_mine] + other_core(g_away).astype(F32)
    g_kv_b = g_kv_sum.astype(BF)
    g_parts = [shift(g_kv_b[320 * k : 320 * (k + 1)], "y", 4 - k) for k in (1, 2, 3)]
    g_scores, gb_down, _ = after(g_kv_b, g_scores, gb_down)
    g_pair = add([g_kv_sum[:320]] + list(g_parts))
    away = other_half(g_pair[160:].astype(BF))
    gate_second, up_second, gw_down, _ = after(g_pair, gate_second, up_second, gw_down)
    down_first = leave(gw_down.reshape(4, 4, 56, 1152), "z", 1, at_z, at_x)
    g_q_rows = dot(g_scores, keys) * score_scale
    g_q = [
        jnp.concatenate(
            [turn_back(g_q_rows[TOKENS * h : TOKENS * (h + 1)], cos, sin) for h in (2 * i, 2 * i + 1)],
            axis=1,
        ).astype(BF)
        for i in (0, 1)
    ]
    gate_sum, up_sum = add(gate_second).astype(BF), add(up_second).astype(BF)
    ga_part = jnp.concatenate(
        [dot_tr(gate_sum[:72], b_gate), dot_tr(up_sum[:72], b_up), jnp.zeros((72, 384), F32)], axis=1
    ).astype(BF)
    back_row = jnp.arange(256, dtype=jnp.int32)
    group, line = back_row // 32, back_row % 32
    take = jnp.where(
        line < 9,
        9 * group + line,
        jnp.where(
            line < 18,
            88 + 9 * group + line - 9,
            jnp.where(
                line < 22,
                72 + 88 * ((line - 18) // 2) + 2 * group + line % 2,
                jnp.where(line < 31, 176 + 9 * group + line - 22, -1),
            ),
        ),
    )
    leaving = dot(
        table(take, jnp.arange(248, dtype=jnp.int32)), jnp.concatenate([gate_sum, up_sum, ga_part], axis=0)
    ).astype(BF)
    slab = exchange(leaving.reshape(8, 32, 896), ("y", "c"))
    def of_chip(own, away):
        return (own.astype(F32) + other_core(away.astype(BF)).astype(F32)).astype(BF).reshape(64, 24, -1)

    def both_halves(owned):
        mine, away = pick(is_first, owned[:12], owned[12:])
        return pick(is_first, mine, other_core(away.astype(BF)).astype(F32))

    loss_high, loss_rest = split_in_two(loss_here)
    loss_mid, loss_low = split_in_two(loss_rest)
    lines = jnp.arange(16, dtype=jnp.int32)
    loss_rows = jnp.where(
        lines == 0,
        loss_high.astype(F32),
        jnp.where(lines == 1, loss_mid.astype(F32), jnp.where(lines == 2, loss_low, 0.0)),
    )
    more_side = (loss_rows[:, None] * (j == 11)[None, :]).astype(BF)
    more_grad = table(jnp.where(lines < 3, lines + 3 * core, -1), jnp.arange(512, dtype=jnp.int32))
    chip_q = of_chip(
        *[(dot_tl(sides[0], g_q[i]) + dot_tl(more_side, more_grad)).astype(BF) for i in (0, 1)]
    )
    side_out, _ = after(g_pair, side_out)
    left, right = pick(is_first, gb_down[:, :640], gb_down[:, 512:])
    chip_out = of_chip(
        dot_tl(side_out, g_half[0]) + dot_tl(put_inner_down, left),
        dot_tl(side_out, g_half[1]) + dot_tl(put_inner_down, right),
    )
    g_kv_own = g_pair[:160] + after(chip_q, away)[0].astype(F32)
    g_k = turn_back(g_kv_own[:, :256], cos, sin).astype(BF)
    g_v = g_kv_own[:, 256:].astype(BF)
    g_k = pick(is_first, g_k[:, :128], g_k[:, 128:])
    g_v = pick(is_first, g_v[:, :128], g_v[:, 128:])
    chip_kv = of_chip(
        *[
            jnp.concatenate([dot_tl(sides[1], g_k[i]).astype(BF), dot_tl(sides[2], g_v[i]).astype(BF)], axis=1)
            for i in (0, 1)
        ]
    )
    chip_kv, _ = after(slab, chip_kv)
    chip_sums = jnp.concatenate([chip_q, chip_kv, chip_out], axis=2)
    parts = exchange(chip_sums, CHIPS)
    down_first, _ = after(g_kv_own, down_first)
    down_second = leave(add(down_first).astype(BF), "x", 0, at_z, at_x)
    slab, down_second, g_q, g_k, g_v, _ = after(chip_sums, slab, down_second, g_q, g_k, g_v)

    d_one = None
    for i, (g, first, last) in enumerate(((g_q, 0, 512), (g_k, 512, 640), (g_v, 640, 768))):
        d = dot_tr(g[0], raw[0][:, first:last]) + dot_tr(g[1], raw[1][:, first:last])
        gi = dot_tr(d.astype(BF), put_inner).astype(BF)
        inner_at = 768 + 128 * i
        d = d + dot_tr(gi[:, :128], raw[0][:, inner_at : inner_at + 128])
        d = d + dot_tr(gi[:, 128:], raw[1][:, inner_at : inner_at + 128])
        d_one = d if d_one is None else d_one + d
    g_u_one = select_back(d_one, put_rows)
    grad_hidden = (g_after + norm_back(scale_one, n_one, gain_one_full, g_u_one)).astype(BF)

    narrow = dot_tr(slab.reshape(256, 896), wider).reshape(8, 32, 864)
    wide = jnp.concatenate([narrow[t] for t in range(8)], axis=1)
    ga = jnp.sum(slab[:, 22:31, :512].astype(F32), axis=0)
    gw_down_own = lax.ppermute(
        add(down_second).astype(BF), EVERY, [(b, a) for a, b in down_route()]
    )[:54]
    ga_down_own = dot_tr(gw_down_own, b_down)

    def over_columns(pairs):
        return sum(jnp.sum(a.astype(F32) * b, axis=1) for a, b in pairs)

    gain_two_own = over_columns(
        ((wg, wide[:9]), (wu, wide[9:18]), (ag, ga[:, :256]), (au, ga[:, 256:]))
    ) / (1.0 + gain_two.astype(F32))

    owned = jnp.sum(parts.astype(F32), axis=0)
    loss_value = jnp.sum(owned[11, :6]) / (1152.0 * valid_count)
    left, right = both_halves(owned)
    own_out = jnp.concatenate([left[:, 768:], right[:, 896:]], axis=1)
    ga_out_own = dot_tr(own_out[:8].astype(BF), b_out)
    left_b, right_b = left[:9].astype(BF), right[:9].astype(BF)
    ga_own = [
        dot_tr(left_b[:, first:last], b_left[:, first:last])
        + dot_tr(right_b[:, first:last], b_right[:, first:last])
        for first, last in ((0, 512), (512, 640), (640, 768))
    ]

    def columns(first, last, rows):
        return jnp.concatenate([left[rows, first:last], right[rows, first:last]], axis=1)

    top_rows, low_rows = slice(0, 9), slice(9, 11)
    gw_own = [columns(0, 512, top_rows), columns(512, 640, top_rows), columns(640, 768, top_rows)]
    gain_one_own = over_columns(
        list(zip((wq, wk, wv), gw_own)) + list(zip((aq, ak, av), ga_own))
    ) / (1.0 + gain_one.astype(F32))

    return (
        result.astype(BF)[None],
        loss_value,
        grad_hidden[None],
        gain_one_own,
        *gw_own,
        own_out[:8],
        ga_own[0],
        columns(0, 512, low_rows),
        ga_own[1],
        columns(512, 640, low_rows),
        ga_own[2],
        columns(640, 768, low_rows),
        ga_out_own,
        own_out[8:10],
        gain_two_own,
        wide[:9],
        wide[9:18],
        gw_down_own.astype(F32),
        ga[:, :256],
        wide[18:20],
        ga[:, 256:],
        wide[20:22],
        ga_down_own,
        own_out[10:],
    )


def solution(mesh):
    mesh = Mesh(mesh.devices.reshape([SIZES[a] for a in EVERY]), EVERY)
    tree, seq = ("z", "xl"), ("xh", "y", "c")
    rows = P(EVERY, None)
    vector = P(EVERY)
    return jax.shard_map(
        on_device,
        mesh=mesh,
        in_specs=(
            P(tree, seq, None),
            P(tree, None),
            P(tree, None),
            P(tree, seq),
            P(tree, seq, None),
            vector,
        )
        + (rows,) * 12
        + (vector,)
        + (rows,) * 9,
        out_specs=(P(tree, seq, None), P(), P(tree, seq, None), vector)
        + (rows,) * 12
        + (vector,)
        + (rows,) * 9,
        check_vma=False,
    )
```

```python
import jax
import jax.numpy as jnp
from jax import lax
from jax.sharding import Mesh, PartitionSpec as P

EPSILON = 1e-06
ROPE_BASE = 10000.0
MASKED_SCORE = -1e30
BF = jnp.bfloat16
F32 = jnp.float32

PLANE = ("z", "xl", "xh")
CHIPS = ("z", "xl", "xh", "y")
EVERY = ("z", "xl", "xh", "y", "c")
SIZES = dict(z=4, xl=2, xh=2, y=4, c=2)
RING = dict(z="z", x=("xl", "xh"), y="y")
TOKENS = 160
HEADS = 4
WIDTH = 256


def dot(a, b):
    return jnp.dot(a, b, preferred_element_type=F32)


def dot_tl(a, b):
    return lax.dot_general(a, b, (((0,), (0,)), ((), ())), preferred_element_type=F32)


def dot_tr(a, b):
    return lax.dot_general(a, b, (((1,), (1,)), ((), ())), preferred_element_type=F32)


def exchange(x, axes):
    return lax.all_to_all(x, axes, split_axis=0, concat_axis=0, tiled=True)


def other_core(x):
    return lax.ppermute(x, "c", [(0, 1), (1, 0)])


def other_half(x):
    return lax.ppermute(x, "xh", [(0, 1), (1, 0)])


def shift(x, axis, k):
    number = [0, 2, 1, 3] if axis == "x" else [0, 1, 2, 3]
    return lax.ppermute(x, RING[axis], [(number[i], number[(i + k) % 4]) for i in range(4)])


def pick(cond, a, b):
    return jnp.where(cond, a, b), jnp.where(cond, b, a)


def split_in_two(x):
    high = x.astype(BF)
    return high, x - high.astype(F32)


def select_back(x, table):
    high, low = split_in_two(x)
    return dot_tr(high, table) + dot_tr(low.astype(BF), table)


def down_route():
    pairs = []
    for o in range(16):
        for t in range(8):
            block = 8 * (o % 2) + t
            pairs.append((8 * o + t, 8 * (block % 4 * 4 + block // 4) + o // 2))
    return pairs


def ring_place(axis, k, at_z, at_x):
    return (at_z - k) % 4 if axis == "z" else (at_x - k) % 4 % 2 * 2 + (at_x - k) % 4 // 2


def placed(parts, axis, at_z, at_x):
    stack = jnp.zeros((4,) + parts[0].shape, parts[0].dtype)
    for k, part in enumerate(parts):
        stack = lax.dynamic_update_index_in_dim(stack, part, ring_place(axis, k, at_z, at_x), 0)
    return stack


def leave(x, axis, dim, at_z, at_x):
    parts = []
    for k in range(4):
        block = lax.dynamic_index_in_dim(x, ring_place(axis, k, at_z, at_x), dim, keepdims=False)
        parts.append(shift(block, axis, 4 - k) if k else block)
    return parts


def add(parts):
    total = parts[0].astype(F32)
    for p in parts[1:]:
        total = total + p.astype(F32)
    return total


def norm_parts(values, gain):
    scale = lax.rsqrt(jnp.mean(values * values, axis=-1, keepdims=True) + EPSILON)
    n = values * scale
    return scale, n, (n * (1.0 + gain)).astype(BF)


def norm_back(scale, n, gain, grad):
    m = grad * (1.0 + gain)
    back = scale * (m - n * jnp.mean(m * n, axis=-1, keepdims=True))
    return back


def turn(x, cos, sin):
    h = cos.shape[-1]
    a, b = x[:, :h], x[:, h:]
    return jnp.concatenate([a * cos - b * sin, b * cos + a * sin], axis=-1)


def turn_back(x, cos, sin):
    return turn(x, cos, -sin)


def gather_tokens(x):
    mine = [x] + [shift(x, "y", k) for k in (1, 2, 3)]
    return jnp.concatenate(mine + [other_core(p) for p in mine], axis=0)


def scatter_tokens(part):
    blocks = part.reshape(2, 4, TOKENS, -1)
    total = None
    for k in (2, 1, 3, 0):
        piece = blocks[0, k] + other_core(blocks[1, k].astype(BF)).astype(F32)
        if k:
            piece = shift(piece.astype(BF), "y", 4 - k).astype(F32)
        total = piece if total is None else total + piece
    return total


def after(done, *values):
    return tuple(lax.optimization_barrier((v, done))[0] for v in values) + (done,)


def table(rows, columns):
    return (rows[:, None] == columns[None, :]).astype(BF)


def on_device(
    layer_input,
    segment,
    position,
    loss_token_mask,
    teacher,
    gain_one,
    wq,
    wk,
    wv,
    wo,
    aq,
    bq,
    ak,
    bk,
    av,
    bv,
    ao,
    bo,
    gain_two,
    wg,
    wu,
    wd,
    ag,
    bg,
    au,
    bu,
    ad,
    bd,
):
    core = lax.axis_index("c")
    at_z, at_y = lax.axis_index("z"), lax.axis_index("y")
    at_xl, at_xh = lax.axis_index("xl"), lax.axis_index("xh")
    at_x = 2 * at_xh + at_xl
    is_first = core == 0
    score_scale = WIDTH**-0.5
    count_here = jnp.sum(loss_token_mask[0]).astype(BF)

    extra = jnp.concatenate([gain_one[None], gain_two[None], count_here.reshape(1, 1)], axis=1)
    extra = jnp.pad(extra, ((0, 1), (0, 384 - 19)))

    def attention_half(k):
        top = jnp.concatenate(
            [m[:, m.shape[1] // 2 * k : m.shape[1] // 2 * (k + 1)] for m in (wq, wk, wv, aq, ak, av)],
            axis=1,
        )
        low = jnp.concatenate(
            [m[:, m.shape[1] // 2 * k : m.shape[1] // 2 * (k + 1)] for m in (bq, bk, bv)] + [extra],
            axis=1,
        )
        return jnp.concatenate([top, low, jnp.zeros((1, 1152), BF)], axis=0)

    keep, send = pick(is_first, attention_half(0), attention_half(1))
    lower, upper = pick(is_first, keep, other_core(send))
    att_own = jnp.concatenate([lower, upper], axis=0)
    att_wide = jnp.broadcast_to(att_own[None], (64, 24, 1152))
    raw_one = exchange(att_wide, CHIPS)
    (layer_input, wg, wu, bg, bu, wd, ad, ag, au, wo, ao, bo, bd, segment, position, core, at_z, _) = after(
        att_wide,
        layer_input, wg, wu, bg, bu, wd, ad, ag, au, wo, ao, bo, bd, segment, position, core, at_z,
    )
    is_first = core == 0
    hidden = layer_input[0].astype(F32)

    def output_half(k):
        wide = jnp.concatenate([m[:, 512 * k : 512 * k + 640] for m in (wo, bo, bd)], axis=0)
        narrow = jnp.pad(ao[:, 128 * k : 128 * k + 128], ((0, 4), (0, 0)))
        return jnp.concatenate([wide, narrow, jnp.pad((ag, au)[k], ((0, 3), (0, 0)))], axis=1)

    keep, send = pick(is_first, output_half(0), output_half(1))
    lower, upper = pick(is_first, keep, other_core(send))
    out_own = jnp.concatenate([lower, upper], axis=0)

    rows22 = jnp.pad(jnp.concatenate([wg, wu, bg, bu], axis=0), ((0, 2), (0, 0)))
    rows22 = jnp.concatenate([rows22[:, 864 * t : 864 * (t + 1)] for t in range(8)], axis=0)
    wider = jnp.arange(896, dtype=jnp.int32)
    wider = table(jnp.arange(864, dtype=jnp.int32), jnp.where(wider % 56 < 54, wider // 56 * 54 + wider % 56, -1))
    rows22 = dot(rows22, wider).astype(BF).reshape(8, 24, 896)
    columns_of = rows22.reshape(4, 2, 24, 896)
    mine = lax.dynamic_index_in_dim(columns_of, core, 1, keepdims=False)
    theirs = lax.dynamic_index_in_dim(columns_of, 1 - core, 1, keepdims=False)
    columns_of = jnp.stack([mine, other_core(theirs)], axis=1).reshape(4, 48, 896)
    slab = []
    for k in range(4):
        piece = lax.dynamic_index_in_dim(columns_of, (at_y + k) % 4, 0, keepdims=False)
        slab.append(shift(piece, "y", k) if k else piece)
    slab = jnp.concatenate(slab, axis=0)
    back = jnp.arange(8, dtype=jnp.int32)
    sources = 2 * ((at_y - back // 2) % 4) + (core - back) % 2
    row = jnp.arange(176, dtype=jnp.int32)
    low = row - 144
    at_row = jnp.where(
        row < 72,
        row // 9 * 24 + row % 9,
        jnp.where(
            row < 144,
            (row - 72) // 9 * 24 + 9 + (row - 72) % 9,
            low % 16 // 2 * 24 + 18 + low // 16 * 2 + low % 2,
        ),
    )
    in_slab = jnp.arange(192, dtype=jnp.int32)
    in_slab = jnp.repeat(sources, 24) * 24 + in_slab % 24
    ff_own = dot(table(at_row, in_slab), slab).astype(BF)
    down_own = lax.ppermute(
        jnp.pad(jnp.concatenate([wd, ad], axis=1), ((0, 2), (0, 0))), EVERY, down_route()
    )
    seq = (at_xh * 4 + at_y) * 2 + core
    tree_seg = segment[0]
    tree_pos = position[0]
    own_seg = lax.dynamic_slice_in_dim(tree_seg, seq * TOKENS, TOKENS)
    own_pos = lax.dynamic_slice_in_dim(tree_pos, seq * TOKENS, TOKENS)
    freq = ROPE_BASE ** (-(jnp.arange(128, dtype=F32) * 2.0 / WIDTH))
    angles = own_pos.astype(F32)[:, None] * freq[None, :]
    cos, sin = jnp.cos(angles), jnp.sin(angles)
    back = jnp.arange(16, dtype=jnp.int32)
    block_at = (((at_xh - back % 2) % 2) * 4 + (at_y - back % 8 // 2) % 4) * 2 + jnp.where(
        back < 8, core, 1 - core
    )
    chosen = (block_at[:, None] == back[None, :]).astype(jnp.int32)[:, :, None]
    key_seg = jnp.sum(chosen * tree_seg.reshape(1, 16, TOKENS), axis=1).reshape(1, 2560)
    key_pos = jnp.sum(chosen * tree_pos.reshape(1, 16, TOKENS), axis=1).reshape(1, 2560)
    q_seg, q_pos = own_seg[:, None], own_pos[:, None]
    parent = (key_seg >= 1) & (key_seg <= 4) & (q_seg >= 5) & ((q_seg - 5) // 2 + 1 == key_seg)
    allowed = ((key_seg == q_seg) | (key_seg == 0) | parent) & (key_pos <= q_pos)

    scale_one = lax.rsqrt(jnp.mean(hidden * hidden, axis=-1, keepdims=True) + EPSILON)
    raw_one, _ = after((ff_own, out_own, down_own, cos, sin, allowed, scale_one), raw_one)
    raw_two = other_core(raw_one)
    marks = raw_one.reshape(128, 12, 1152)[:, 9, 768:896]
    gain_one_full = marks[:, :9].reshape(1, 1152).astype(F32)
    gain_two_full = marks[:, 9:18].reshape(1, 1152).astype(F32)
    valid_count = jnp.sum(marks[:, 18].astype(F32))
    out_own, _ = after(raw_one, out_own)
    out_wide = jnp.broadcast_to(out_own[None], (64, 24, 1024))
    out_one = exchange(out_wide, CHIPS)
    out_two = other_core(out_one)
    raw_out = [out_one.reshape(1536, 1024), out_two.reshape(1536, 1024)]
    raw_one, raw_two, _ = after(out_wide, raw_one, raw_two)
    raw = [raw_one.reshape(1536, 1152), raw_two.reshape(1536, 1152)]
    ids = jnp.arange(1536, dtype=jnp.int32)
    dev, j = 2 * (ids // 24) + (ids % 24) // 12, ids % 12
    halves = jnp.arange(256, dtype=jnp.int32)
    inner_ids = jnp.where(halves < 128, 128 * core + halves, 128 * (1 - core) + halves - 128)
    heads_at = jnp.arange(1024, dtype=jnp.int32)
    head_ids = jnp.where(heads_at < 512, 512 * core + heads_at, 512 * (1 - core) + heads_at - 512)
    features = jnp.arange(1152, dtype=jnp.int32)
    put_rows = table(features, jnp.where(j < 9, 9 * dev + j, -1))
    put_inner = table(inner_ids, jnp.where((j >= 9) & (j < 11), 2 * dev + j - 9, -1))
    take_b = table(halves, jnp.where((j >= 9) & (j < 11), 2 * dev + j - 9, -1))
    take_b_out = table(halves, jnp.where((j >= 8) & (j < 10), 2 * dev + j - 8, -1))
    put_mix = table(head_ids, jnp.where(j < 8, 8 * dev + j, -1))
    put_inner_out = table(inner_ids, jnp.where((j >= 8) & (j < 10), 2 * dev + j - 8, -1))
    put_inner_down = table(halves, jnp.where(j >= 10, 2 * dev + j - 10, -1))

    allowed = jnp.concatenate([allowed] * HEADS, axis=0)
    n_one = hidden * scale_one
    u_one = (n_one * (1.0 + gain_one_full)).astype(BF)
    u_rows = dot(u_one, put_rows).astype(BF)
    inner = [dot(u_rows, raw[i][:, 768:]).astype(BF) for i in (0, 1)]
    sides = []
    for i in range(3):
        part = jnp.concatenate([inner[0][:, 128 * i : 128 * i + 128], inner[1][:, 128 * i : 128 * i + 128]], axis=1)
        sides.append(u_rows + dot(part, put_inner).astype(BF))
    kk = pick(is_first, *[dot(sides[1], raw[i][:, 512:640]) for i in (0, 1)])
    vv = pick(is_first, *[dot(sides[2], raw[i][:, 640:768]) for i in (0, 1)])
    kv_own = jnp.concatenate([turn(jnp.concatenate(kk, axis=1), cos, sin), vv[0], vv[1]], axis=1).astype(BF)

    pair = jnp.concatenate([kv_own, other_half(kv_own)], axis=0)
    down_own, _ = after(kv_own, down_own)
    down_line = placed([down_own] + [shift(down_own, "z", k) for k in (1, 2, 3)], "z", at_z, at_x)
    ff_own, _ = after((out_one, down_line), ff_own)
    ff_wide = jnp.broadcast_to(ff_own[None], (16, 176, 896))
    ff_all = exchange(ff_wide, PLANE)
    down_parts = [down_line] + [shift(down_line, "x", k) for k in (1, 2, 3)]
    kv_parts = [pair] + list(after(ff_wide, *[shift(pair, "y", k) for k in (1, 2, 3)])[:3])
    kv_mine = jnp.concatenate(kv_parts, axis=0)
    kv = jnp.concatenate([kv_mine, other_core(kv_mine)], axis=0)
    keys, values = kv[:, :256], kv[:, 256:]
    queries = [dot(sides[0], raw[i][:, :512]) for i in (0, 1)]
    q_rows = jnp.concatenate(
        [turn(queries[h // 2][:, WIDTH * (h % 2) : WIDTH * (h % 2 + 1)], cos, sin) for h in range(HEADS)],
        axis=0,
    ).astype(BF)
    scores = jnp.where(allowed, dot_tr(q_rows, keys) * score_scale, MASKED_SCORE)
    top = jnp.max(scores, axis=-1, keepdims=True)
    ex = jnp.exp(scores - top)
    total = jnp.sum(ex, axis=-1, keepdims=True)
    lse = top + jnp.log(total)
    mix_rows = dot((ex / total).astype(BF), values).astype(BF)
    mix = jnp.concatenate([mix_rows[TOKENS * h : TOKENS * (h + 1)] for h in range(HEADS)], axis=1)
    mix_placed = dot(mix, put_mix).astype(BF)
    inner_out = jnp.concatenate([dot(mix_placed, raw_out[i][:, 640:768]) for i in (0, 1)], axis=1).astype(BF)
    side_out = mix_placed + dot(inner_out, put_inner_out).astype(BF)
    left, right = pick(is_first, *[dot(side_out, raw_out[i][:, :640]) for i in (0, 1)])
    after_att = hidden + jnp.concatenate([left, right[:, 128:]], axis=1)

    scale_two, n_two, u_two = norm_parts(after_att, gain_two_full)
    u_all = gather_tokens(u_two)

    raw_late, out_late, _ = after(u_two, raw, raw_out)
    b_left, b_right = pick(is_first, *[dot(take_b, raw_late[i][:, :768]).astype(BF) for i in (0, 1)])
    left, right = pick(is_first, *[dot(take_b_out, out_late[i][:, :640]).astype(BF) for i in (0, 1)])
    b_out = jnp.concatenate([left, right[:, 128:]], axis=1)
    left, right = pick(is_first, *[dot(put_inner_down, out_late[i][:, :640]).astype(BF) for i in (0, 1)])
    b_down = jnp.concatenate([left, right[:, 128:]], axis=1)
    a_gate, a_up = pick(is_first, *[dot(put_rows, out_late[i][:, 768:]).astype(BF) for i in (0, 1)])
    ff_all, _ = after((b_left, b_right, b_out, b_down, a_gate, a_up), ff_all)
    b_gate = ff_all[:, 144:160].reshape(256, 896)
    b_up = ff_all[:, 160:].reshape(256, 896)
    w_gate = (ff_all[:, :72].astype(F32) + dot(a_gate, b_gate).reshape(16, 72, 896)).astype(BF)
    w_up = (ff_all[:, 72:144].astype(F32) + dot(a_up, b_up).reshape(16, 72, 896)).astype(BF)
    w_gate, w_up = w_gate.reshape(1152, 896), w_up.reshape(1152, 896)
    down_parts, _ = after(w_up, down_parts)
    down_raw = placed(down_parts, "x", at_z, at_x).reshape(896, 1408)
    a_down = down_raw[:, 1152:]
    w_down = (down_raw[:, :1152].astype(F32) + dot(a_down, b_down)).astype(BF)

    gate = dot(u_all, w_gate)
    up = dot(u_all, w_up)
    act, act_pull = jax.vjp(lambda g, u: jax.nn.gelu(g, approximate=True) * u, gate, up)
    act = act.astype(BF)
    result = after_att + scatter_tokens(dot(act, w_down))

    valid = loss_token_mask[0].astype(F32)[:, None]
    error = result - teacher[0].astype(F32)
    loss_here = jnp.sum(valid * error * error)
    grad_result = 2.0 * 20480.0 / valid_count * valid * error

    g_all = gather_tokens(grad_result.astype(BF))
    g_act = dot_tr(g_all, w_down).astype(BF)
    g_gate, g_up = act_pull(g_act.astype(F32))
    g_gate, g_up = g_gate.astype(BF), g_up.astype(BF)
    g_u_part = dot_tr(g_gate, w_gate) + dot_tr(g_up, w_up)
    g_u_two = scatter_tokens(g_u_part)
    u_all, act, g_all, g_gate, g_up, _ = after(g_u_part, u_all, act, g_all, g_gate, g_up)
    gw_gate = dot_tl(u_all, g_gate).astype(BF)
    gb_gate = dot_tl(a_gate, gw_gate).astype(BF)
    gate_grads = jnp.concatenate([gw_gate.reshape(16, 72, 896), gb_gate.reshape(16, 16, 896)], axis=1)
    gate_first = leave(gate_grads.reshape(4, 4, 88, 896), "z", 0, at_z, at_x)
    gw_up = dot_tl(u_all, g_up).astype(BF)
    gb_up = dot_tl(a_up, gw_up).astype(BF)
    up_grads = jnp.concatenate([gw_up.reshape(16, 72, 896), gb_up.reshape(16, 16, 896)], axis=1)
    up_first = leave(up_grads.reshape(4, 4, 88, 896), "x", 1, at_z, at_x)
    gw_down = dot_tl(act, g_all).astype(BF)
    gb_down = dot_tl(a_down, gw_down).astype(BF)

    norm_two_back = norm_back(scale_two, n_two, gain_two_full, g_u_two)
    g_after = grad_result + norm_two_back
    g_after_b = g_after.astype(BF)
    once = jnp.where(jnp.arange(640) < 128, 0, 1).astype(BF)[None]
    g_half = pick(is_first, g_after_b[:, :640], g_after_b[:, 512:])
    g_once = pick(is_first, g_after_b[:, :640], g_after_b[:, 512:] * once)
    d_out = dot_tr(g_once[0], raw_out[0][:, :640]) + dot_tr(g_once[1], raw_out[1][:, :640])
    gi_out = dot_tr(d_out.astype(BF), put_inner_out).astype(BF)
    d_out = (
        d_out
        + dot_tr(gi_out[:, :128], raw_out[0][:, 640:768])
        + dot_tr(gi_out[:, 128:], raw_out[1][:, 640:768])
    )
    g_mix = dot_tr(d_out.astype(BF), put_mix).astype(BF)
    gate_first, _ = after(g_mix, gate_first)
    gate_line = add(gate_first).astype(BF)
    g_mix, _ = after(gate_line, g_mix)
    gate_second = leave(gate_line, "x", 0, at_z, at_x)
    g_rows = jnp.concatenate([g_mix[:, WIDTH * h : WIDTH * (h + 1)] for h in range(HEADS)], axis=0)
    scores_again = jnp.where(allowed, dot_tr(q_rows, keys) * score_scale, MASKED_SCORE)
    probs = jnp.where(allowed, jnp.exp(scores_again - lse), 0.0)
    g_probs = dot_tr(g_rows, values)
    g_scores = (probs * (g_probs - jnp.sum(probs * g_probs, axis=-1, keepdims=True))).astype(BF)
    g_keys = dot_tl(g_scores, q_rows) * score_scale
    g_values = dot_tl(probs.astype(BF), g_rows)
    g_kv = jnp.concatenate([g_keys, g_values], axis=1)
    n_mine = 8 * TOKENS
    up_first, g_kv = lax.optimization_barrier((up_first, g_kv))
    up_line = add(up_first).astype(BF)
    up_second = leave(up_line, "z", 0, at_z, at_x)
    g_away, _ = after(up_line, g_kv[n_mine:].astype(BF))
    g_kv_sum = g_kv[:n_mine] + other_core(g_away).astype(F32)
    g_kv_b = g_kv_sum.astype(BF)
    g_parts = [shift(g_kv_b[320 * k : 320 * (k + 1)], "y", 4 - k) for k in (1, 2, 3)]
    g_scores, gb_down, _ = after(g_kv_b, g_scores, gb_down)
    g_pair = add([g_kv_sum[:320]] + list(g_parts))
    away = other_half(g_pair[160:].astype(BF))
    gate_second, up_second, gw_down, _ = after(g_pair, gate_second, up_second, gw_down)
    down_first = leave(gw_down.reshape(4, 4, 56, 1152), "z", 1, at_z, at_x)
    g_q_rows = dot(g_scores, keys) * score_scale
    g_q = [
        jnp.concatenate(
            [turn_back(g_q_rows[TOKENS * h : TOKENS * (h + 1)], cos, sin) for h in (2 * i, 2 * i + 1)],
            axis=1,
        ).astype(BF)
        for i in (0, 1)
    ]
    gate_sum, up_sum = add(gate_second).astype(BF), add(up_second).astype(BF)
    ga_part = jnp.concatenate(
        [dot_tr(gate_sum[:72], b_gate), dot_tr(up_sum[:72], b_up), jnp.zeros((72, 384), F32)], axis=1
    ).astype(BF)
    back_row = jnp.arange(256, dtype=jnp.int32)
    group, line = back_row // 32, back_row % 32
    take = jnp.where(
        line < 9,
        9 * group + line,
        jnp.where(
            line < 18,
            88 + 9 * group + line - 9,
            jnp.where(
                line < 22,
                72 + 88 * ((line - 18) // 2) + 2 * group + line % 2,
                jnp.where(line < 31, 176 + 9 * group + line - 22, -1),
            ),
        ),
    )
    leaving = dot(
        table(take, jnp.arange(248, dtype=jnp.int32)), jnp.concatenate([gate_sum, up_sum, ga_part], axis=0)
    ).astype(BF)
    slab = exchange(leaving.reshape(8, 32, 896), ("y", "c"))
    def of_chip(own, away):
        return (own.astype(F32) + other_core(away.astype(BF)).astype(F32)).astype(BF).reshape(64, 24, -1)

    def both_halves(owned):
        mine, away = pick(is_first, owned[:12], owned[12:])
        return pick(is_first, mine, other_core(away.astype(BF)).astype(F32))

    loss_high, loss_rest = split_in_two(loss_here)
    loss_mid, loss_low = split_in_two(loss_rest)
    lines = jnp.arange(16, dtype=jnp.int32)
    loss_rows = jnp.where(
        lines == 0,
        loss_high.astype(F32),
        jnp.where(lines == 1, loss_mid.astype(F32), jnp.where(lines == 2, loss_low, 0.0)),
    )
    more_side = (loss_rows[:, None] * (j == 11)[None, :]).astype(BF)
    more_grad = table(jnp.where(lines < 3, lines + 3 * core, -1), jnp.arange(512, dtype=jnp.int32))
    chip_q = of_chip(
        *[(dot_tl(sides[0], g_q[i]) + dot_tl(more_side, more_grad)).astype(BF) for i in (0, 1)]
    )
    side_out, _ = after(g_pair, side_out)
    left, right = pick(is_first, gb_down[:, :640], gb_down[:, 512:])
    chip_out = of_chip(
        dot_tl(side_out, g_half[0]) + dot_tl(put_inner_down, left),
        dot_tl(side_out, g_half[1]) + dot_tl(put_inner_down, right),
    )
    g_kv_own = g_pair[:160] + after(chip_q, away)[0].astype(F32)
    g_k = turn_back(g_kv_own[:, :256], cos, sin).astype(BF)
    g_v = g_kv_own[:, 256:].astype(BF)
    g_k = pick(is_first, g_k[:, :128], g_k[:, 128:])
    g_v = pick(is_first, g_v[:, :128], g_v[:, 128:])
    chip_kv = of_chip(
        *[
            jnp.concatenate([dot_tl(sides[1], g_k[i]).astype(BF), dot_tl(sides[2], g_v[i]).astype(BF)], axis=1)
            for i in (0, 1)
        ]
    )
    chip_kv, _ = after(slab, chip_kv)
    chip_sums = jnp.concatenate([chip_q, chip_kv, chip_out], axis=2)
    parts = exchange(chip_sums, CHIPS)
    down_first, _ = after(chip_sums, down_first)
    down_second = leave(add(down_first).astype(BF), "x", 0, at_z, at_x)
    slab, g_q, g_k, g_v, _ = after(chip_sums, slab, g_q, g_k, g_v)

    d_one = None
    for i, (g, first, last) in enumerate(((g_q, 0, 512), (g_k, 512, 640), (g_v, 640, 768))):
        d = dot_tr(g[0], raw[0][:, first:last]) + dot_tr(g[1], raw[1][:, first:last])
        gi = dot_tr(d.astype(BF), put_inner).astype(BF)
        inner_at = 768 + 128 * i
        d = d + dot_tr(gi[:, :128], raw[0][:, inner_at : inner_at + 128])
        d = d + dot_tr(gi[:, 128:], raw[1][:, inner_at : inner_at + 128])
        d_one = d if d_one is None else d_one + d
    g_u_one = select_back(d_one, put_rows)
    grad_hidden = (g_after + norm_back(scale_one, n_one, gain_one_full, g_u_one)).astype(BF)

    narrow = dot_tr(slab.reshape(256, 896), wider).reshape(8, 32, 864)
    wide = jnp.concatenate([narrow[t] for t in range(8)], axis=1)
    ga = jnp.sum(slab[:, 22:31, :512].astype(F32), axis=0)
    gw_down_own = lax.ppermute(
        add(down_second).astype(BF), EVERY, [(b, a) for a, b in down_route()]
    )[:54]
    ga_down_own = dot_tr(gw_down_own, b_down)

    def over_columns(pairs):
        return sum(jnp.sum(a.astype(F32) * b, axis=1) for a, b in pairs)

    gain_two_own = over_columns(
        ((wg, wide[:9]), (wu, wide[9:18]), (ag, ga[:, :256]), (au, ga[:, 256:]))
    ) / (1.0 + gain_two.astype(F32))

    owned = jnp.sum(parts.astype(F32), axis=0)
    loss_value = jnp.sum(owned[11, :6]) / (1152.0 * valid_count)
    left, right = both_halves(owned)
    own_out = jnp.concatenate([left[:, 768:], right[:, 896:]], axis=1)
    ga_out_own = dot_tr(own_out[:8].astype(BF), b_out)
    left_b, right_b = left[:9].astype(BF), right[:9].astype(BF)
    ga_own = [
        dot_tr(left_b[:, first:last], b_left[:, first:last])
        + dot_tr(right_b[:, first:last], b_right[:, first:last])
        for first, last in ((0, 512), (512, 640), (640, 768))
    ]

    def columns(first, last, rows):
        return jnp.concatenate([left[rows, first:last], right[rows, first:last]], axis=1)

    top_rows, low_rows = slice(0, 9), slice(9, 11)
    gw_own = [columns(0, 512, top_rows), columns(512, 640, top_rows), columns(640, 768, top_rows)]
    gain_one_own = over_columns(
        list(zip((wq, wk, wv), gw_own)) + list(zip((aq, ak, av), ga_own))
    ) / (1.0 + gain_one.astype(F32))

    return (
        result.astype(BF)[None],
        loss_value,
        grad_hidden[None],
        gain_one_own,
        *gw_own,
        own_out[:8],
        ga_own[0],
        columns(0, 512, low_rows),
        ga_own[1],
        columns(512, 640, low_rows),
        ga_own[2],
        columns(640, 768, low_rows),
        ga_out_own,
        own_out[8:10],
        gain_two_own,
        wide[:9],
        wide[9:18],
        gw_down_own.astype(F32),
        ga[:, :256],
        wide[18:20],
        ga[:, 256:],
        wide[20:22],
        ga_down_own,
        own_out[10:],
    )


def solution(mesh):
    mesh = Mesh(mesh.devices.reshape([SIZES[a] for a in EVERY]), EVERY)
    tree, seq = ("z", "xl"), ("xh", "y", "c")
    rows = P(EVERY, None)
    vector = P(EVERY)
    return jax.shard_map(
        on_device,
        mesh=mesh,
        in_specs=(
            P(tree, seq, None),
            P(tree, None),
            P(tree, None),
            P(tree, seq),
            P(tree, seq, None),
            vector,
        )
        + (rows,) * 12
        + (vector,)
        + (rows,) * 9,
        out_specs=(P(tree, seq, None), P(), P(tree, seq, None), vector)
        + (rows,) * 12
        + (vector,)
        + (rows,) * 9,
        check_vma=False,
    )
```

```python
import jax
import jax.numpy as jnp
from jax import lax
from jax.sharding import Mesh, PartitionSpec as P

EPSILON = 1e-06
ROPE_BASE = 10000.0
MASKED_SCORE = -1e30
BF = jnp.bfloat16
F32 = jnp.float32

PLANE = ("z", "xl", "xh")
CHIPS = ("z", "xl", "xh", "y")
EVERY = ("z", "xl", "xh", "y", "c")
SIZES = dict(z=4, xl=2, xh=2, y=4, c=2)
RING = dict(z="z", x=("xl", "xh"), y="y")
TOKENS = 160
HEADS = 4
WIDTH = 256


def dot(a, b):
    return jnp.dot(a, b, preferred_element_type=F32)


def dot_tl(a, b):
    return lax.dot_general(a, b, (((0,), (0,)), ((), ())), preferred_element_type=F32)


def dot_tr(a, b):
    return lax.dot_general(a, b, (((1,), (1,)), ((), ())), preferred_element_type=F32)


def exchange(x, axes):
    return lax.all_to_all(x, axes, split_axis=0, concat_axis=0, tiled=True)


def other_core(x):
    return lax.ppermute(x, "c", [(0, 1), (1, 0)])


def other_half(x):
    return lax.ppermute(x, "xh", [(0, 1), (1, 0)])


def shift(x, axis, k):
    number = [0, 2, 1, 3] if axis == "x" else [0, 1, 2, 3]
    return lax.ppermute(x, RING[axis], [(number[i], number[(i + k) % 4]) for i in range(4)])


def pick(cond, a, b):
    return jnp.where(cond, a, b), jnp.where(cond, b, a)


def split_in_two(x):
    high = x.astype(BF)
    return high, x - high.astype(F32)


def select_back(x, table):
    high, low = split_in_two(x)
    return dot_tr(high, table) + dot_tr(low.astype(BF), table)


def down_route():
    pairs = []
    for o in range(16):
        for t in range(8):
            block = 8 * (o % 2) + t
            pairs.append((8 * o + t, 8 * (block % 4 * 4 + block // 4) + o // 2))
    return pairs


def ring_place(axis, k, at_z, at_x):
    return (at_z - k) % 4 if axis == "z" else (at_x - k) % 4 % 2 * 2 + (at_x - k) % 4 // 2


def placed(parts, axis, at_z, at_x):
    stack = jnp.zeros((4,) + parts[0].shape, parts[0].dtype)
    for k, part in enumerate(parts):
        stack = lax.dynamic_update_index_in_dim(stack, part, ring_place(axis, k, at_z, at_x), 0)
    return stack


def leave(x, axis, dim, at_z, at_x):
    parts = []
    for k in range(4):
        block = lax.dynamic_index_in_dim(x, ring_place(axis, k, at_z, at_x), dim, keepdims=False)
        parts.append(shift(block, axis, 4 - k) if k else block)
    return parts


def add(parts):
    total = parts[0].astype(F32)
    for p in parts[1:]:
        total = total + p.astype(F32)
    return total


def norm_parts(values, gain):
    scale = lax.rsqrt(jnp.mean(values * values, axis=-1, keepdims=True) + EPSILON)
    n = values * scale
    return scale, n, (n * (1.0 + gain)).astype(BF)


def norm_back(scale, n, gain, grad):
    m = grad * (1.0 + gain)
    back = scale * (m - n * jnp.mean(m * n, axis=-1, keepdims=True))
    return back


def turn(x, cos, sin):
    h = cos.shape[-1]
    a, b = x[:, :h], x[:, h:]
    return jnp.concatenate([a * cos - b * sin, b * cos + a * sin], axis=-1)


def turn_back(x, cos, sin):
    return turn(x, cos, -sin)


def gather_tokens(x):
    mine = [x] + [shift(x, "y", k) for k in (1, 2, 3)]
    return jnp.concatenate(mine + [other_core(p) for p in mine], axis=0)


def scatter_tokens(part):
    blocks = part.reshape(2, 4, TOKENS, -1)
    total = None
    for k in (2, 1, 3, 0):
        piece = blocks[0, k] + other_core(blocks[1, k].astype(BF)).astype(F32)
        if k:
            piece = shift(piece.astype(BF), "y", 4 - k).astype(F32)
        total = piece if total is None else total + piece
    return total


def after(done, *values):
    return tuple(lax.optimization_barrier((v, done))[0] for v in values) + (done,)


def table(rows, columns):
    return (rows[:, None] == columns[None, :]).astype(BF)


def on_device(
    layer_input,
    segment,
    position,
    loss_token_mask,
    teacher,
    gain_one,
    wq,
    wk,
    wv,
    wo,
    aq,
    bq,
    ak,
    bk,
    av,
    bv,
    ao,
    bo,
    gain_two,
    wg,
    wu,
    wd,
    ag,
    bg,
    au,
    bu,
    ad,
    bd,
):
    core = lax.axis_index("c")
    at_z, at_y = lax.axis_index("z"), lax.axis_index("y")
    at_xl, at_xh = lax.axis_index("xl"), lax.axis_index("xh")
    at_x = 2 * at_xh + at_xl
    is_first = core == 0
    score_scale = WIDTH**-0.5
    count_here = jnp.sum(loss_token_mask[0]).astype(BF)

    extra = jnp.concatenate([gain_one[None], gain_two[None], count_here.reshape(1, 1)], axis=1)
    extra = jnp.pad(extra, ((0, 1), (0, 384 - 19)))

    def attention_half(k):
        top = jnp.concatenate(
            [m[:, m.shape[1] // 2 * k : m.shape[1] // 2 * (k + 1)] for m in (wq, wk, wv, aq, ak, av)],
            axis=1,
        )
        low = jnp.concatenate(
            [m[:, m.shape[1] // 2 * k : m.shape[1] // 2 * (k + 1)] for m in (bq, bk, bv)] + [extra],
            axis=1,
        )
        return jnp.concatenate([top, low, jnp.zeros((1, 1152), BF)], axis=0)

    keep, send = pick(is_first, attention_half(0), attention_half(1))
    lower, upper = pick(is_first, keep, other_core(send))
    att_own = jnp.concatenate([lower, upper], axis=0)
    att_wide = jnp.broadcast_to(att_own[None], (64, 24, 1152))
    raw_one = exchange(att_wide, CHIPS)
    (layer_input, wg, wu, bg, bu, wd, ad, ag, au, wo, ao, bo, bd, segment, position, core, at_z, _) = after(
        att_wide,
        layer_input, wg, wu, bg, bu, wd, ad, ag, au, wo, ao, bo, bd, segment, position, core, at_z,
    )
    is_first = core == 0
    hidden = layer_input[0].astype(F32)

    def output_half(k):
        wide = jnp.concatenate([m[:, 512 * k : 512 * k + 640] for m in (wo, bo, bd)], axis=0)
        narrow = jnp.pad(ao[:, 128 * k : 128 * k + 128], ((0, 4), (0, 0)))
        return jnp.concatenate([wide, narrow, jnp.pad((ag, au)[k], ((0, 3), (0, 0)))], axis=1)

    keep, send = pick(is_first, output_half(0), output_half(1))
    lower, upper = pick(is_first, keep, other_core(send))
    out_own = jnp.concatenate([lower, upper], axis=0)

    rows22 = jnp.pad(jnp.concatenate([wg, wu, bg, bu], axis=0), ((0, 2), (0, 0)))
    rows22 = jnp.concatenate([rows22[:, 864 * t : 864 * (t + 1)] for t in range(8)], axis=0)
    wider = jnp.arange(896, dtype=jnp.int32)
    wider = table(jnp.arange(864, dtype=jnp.int32), jnp.where(wider % 56 < 54, wider // 56 * 54 + wider % 56, -1))
    rows22 = dot(rows22, wider).astype(BF).reshape(8, 24, 896)
    columns_of = rows22.reshape(4, 2, 24, 896)
    mine = lax.dynamic_index_in_dim(columns_of, core, 1, keepdims=False)
    theirs = lax.dynamic_index_in_dim(columns_of, 1 - core, 1, keepdims=False)
    columns_of = jnp.stack([mine, other_core(theirs)], axis=1).reshape(4, 48, 896)
    slab = []
    for k in range(4):
        piece = lax.dynamic_index_in_dim(columns_of, (at_y + k) % 4, 0, keepdims=False)
        slab.append(shift(piece, "y", k) if k else piece)
    slab = jnp.concatenate(slab, axis=0)
    back = jnp.arange(8, dtype=jnp.int32)
    sources = 2 * ((at_y - back // 2) % 4) + (core - back) % 2
    row = jnp.arange(176, dtype=jnp.int32)
    low = row - 144
    at_row = jnp.where(
        row < 72,
        row // 9 * 24 + row % 9,
        jnp.where(
            row < 144,
            (row - 72) // 9 * 24 + 9 + (row - 72) % 9,
            low % 16 // 2 * 24 + 18 + low // 16 * 2 + low % 2,
        ),
    )
    in_slab = jnp.arange(192, dtype=jnp.int32)
    in_slab = jnp.repeat(sources, 24) * 24 + in_slab % 24
    ff_own = dot(table(at_row, in_slab), slab).astype(BF)
    down_own = lax.ppermute(
        jnp.pad(jnp.concatenate([wd, ad], axis=1), ((0, 2), (0, 0))), EVERY, down_route()
    )
    seq = (at_xh * 4 + at_y) * 2 + core
    tree_seg = segment[0]
    tree_pos = position[0]
    own_seg = lax.dynamic_slice_in_dim(tree_seg, seq * TOKENS, TOKENS)
    own_pos = lax.dynamic_slice_in_dim(tree_pos, seq * TOKENS, TOKENS)
    freq = ROPE_BASE ** (-(jnp.arange(128, dtype=F32) * 2.0 / WIDTH))
    angles = own_pos.astype(F32)[:, None] * freq[None, :]
    cos, sin = jnp.cos(angles), jnp.sin(angles)
    back = jnp.arange(16, dtype=jnp.int32)
    block_at = (((at_xh - back % 2) % 2) * 4 + (at_y - back % 8 // 2) % 4) * 2 + jnp.where(
        back < 8, core, 1 - core
    )
    chosen = (block_at[:, None] == back[None, :]).astype(jnp.int32)[:, :, None]
    key_seg = jnp.sum(chosen * tree_seg.reshape(1, 16, TOKENS), axis=1).reshape(1, 2560)
    key_pos = jnp.sum(chosen * tree_pos.reshape(1, 16, TOKENS), axis=1).reshape(1, 2560)
    q_seg, q_pos = own_seg[:, None], own_pos[:, None]
    parent = (key_seg >= 1) & (key_seg <= 4) & (q_seg >= 5) & ((q_seg - 5) // 2 + 1 == key_seg)
    allowed = ((key_seg == q_seg) | (key_seg == 0) | parent) & (key_pos <= q_pos)

    scale_one = lax.rsqrt(jnp.mean(hidden * hidden, axis=-1, keepdims=True) + EPSILON)
    raw_one, _ = after((ff_own, out_own, down_own, cos, sin, allowed, scale_one), raw_one)
    raw_two = other_core(raw_one)
    marks = raw_one.reshape(128, 12, 1152)[:, 9, 768:896]
    gain_one_full = marks[:, :9].reshape(1, 1152).astype(F32)
    gain_two_full = marks[:, 9:18].reshape(1, 1152).astype(F32)
    valid_count = jnp.sum(marks[:, 18].astype(F32))
    out_own, _ = after(raw_one, out_own)
    out_wide = jnp.broadcast_to(out_own[None], (64, 24, 1024))
    down_z = [shift(down_own, "z", k) for k in (1, 2, 3)]
    out_wide, down_z = lax.optimization_barrier((out_wide, down_z))
    out_one = exchange(out_wide, CHIPS)
    out_two = other_core(out_one)
    raw_out = [out_one.reshape(1536, 1024), out_two.reshape(1536, 1024)]
    raw_one, raw_two, _ = after(out_wide, raw_one, raw_two)
    raw = [raw_one.reshape(1536, 1152), raw_two.reshape(1536, 1152)]
    ids = jnp.arange(1536, dtype=jnp.int32)
    dev, j = 2 * (ids // 24) + (ids % 24) // 12, ids % 12
    halves = jnp.arange(256, dtype=jnp.int32)
    inner_ids = jnp.where(halves < 128, 128 * core + halves, 128 * (1 - core) + halves - 128)
    heads_at = jnp.arange(1024, dtype=jnp.int32)
    head_ids = jnp.where(heads_at < 512, 512 * core + heads_at, 512 * (1 - core) + heads_at - 512)
    features = jnp.arange(1152, dtype=jnp.int32)
    put_rows = table(features, jnp.where(j < 9, 9 * dev + j, -1))
    put_inner = table(inner_ids, jnp.where((j >= 9) & (j < 11), 2 * dev + j - 9, -1))
    take_b = table(halves, jnp.where((j >= 9) & (j < 11), 2 * dev + j - 9, -1))
    take_b_out = table(halves, jnp.where((j >= 8) & (j < 10), 2 * dev + j - 8, -1))
    put_mix = table(head_ids, jnp.where(j < 8, 8 * dev + j, -1))
    put_inner_out = table(inner_ids, jnp.where((j >= 8) & (j < 10), 2 * dev + j - 8, -1))
    put_inner_down = table(halves, jnp.where(j >= 10, 2 * dev + j - 10, -1))

    allowed = jnp.concatenate([allowed] * HEADS, axis=0)
    n_one = hidden * scale_one
    u_one = (n_one * (1.0 + gain_one_full)).astype(BF)
    u_rows = dot(u_one, put_rows).astype(BF)
    inner = [dot(u_rows, raw[i][:, 768:]).astype(BF) for i in (0, 1)]
    sides = []
    for i in range(3):
        part = jnp.concatenate([inner[0][:, 128 * i : 128 * i + 128], inner[1][:, 128 * i : 128 * i + 128]], axis=1)
        sides.append(u_rows + dot(part, put_inner).astype(BF))
    kk = pick(is_first, *[dot(sides[1], raw[i][:, 512:640]) for i in (0, 1)])
    vv = pick(is_first, *[dot(sides[2], raw[i][:, 640:768]) for i in (0, 1)])
    kv_own = jnp.concatenate([turn(jnp.concatenate(kk, axis=1), cos, sin), vv[0], vv[1]], axis=1).astype(BF)

    pair = jnp.concatenate([kv_own, other_half(kv_own)], axis=0)
    down_line = placed([down_own] + down_z, "z", at_z, at_x)
    ff_own, _ = after((out_one, down_line), ff_own)
    ff_wide = jnp.broadcast_to(ff_own[None], (16, 176, 896))
    ff_all = exchange(ff_wide, PLANE)
    down_parts = [down_line] + [shift(down_line, "x", k) for k in (1, 2, 3)]
    kv_parts = [pair] + list(after(ff_wide, *[shift(pair, "y", k) for k in (1, 2, 3)])[:3])
    kv_mine = jnp.concatenate(kv_parts, axis=0)
    kv = jnp.concatenate([kv_mine, other_core(kv_mine)], axis=0)
    keys, values = kv[:, :256], kv[:, 256:]
    queries = [dot(sides[0], raw[i][:, :512]) for i in (0, 1)]
    q_rows = jnp.concatenate(
        [turn(queries[h // 2][:, WIDTH * (h % 2) : WIDTH * (h % 2 + 1)], cos, sin) for h in range(HEADS)],
        axis=0,
    ).astype(BF)
    scores = jnp.where(allowed, dot_tr(q_rows, keys) * score_scale, MASKED_SCORE)
    top = jnp.max(scores, axis=-1, keepdims=True)
    ex = jnp.exp(scores - top)
    total = jnp.sum(ex, axis=-1, keepdims=True)
    lse = top + jnp.log(total)
    mix_rows = dot((ex / total).astype(BF), values).astype(BF)
    mix = jnp.concatenate([mix_rows[TOKENS * h : TOKENS * (h + 1)] for h in range(HEADS)], axis=1)
    mix_placed = dot(mix, put_mix).astype(BF)
    inner_out = jnp.concatenate([dot(mix_placed, raw_out[i][:, 640:768]) for i in (0, 1)], axis=1).astype(BF)
    side_out = mix_placed + dot(inner_out, put_inner_out).astype(BF)
    left, right = pick(is_first, *[dot(side_out, raw_out[i][:, :640]) for i in (0, 1)])
    after_att = hidden + jnp.concatenate([left, right[:, 128:]], axis=1)

    scale_two, n_two, u_two = norm_parts(after_att, gain_two_full)
    u_all = gather_tokens(u_two)

    raw_late, out_late, _ = after(u_two, raw, raw_out)
    b_left, b_right = pick(is_first, *[dot(take_b, raw_late[i][:, :768]).astype(BF) for i in (0, 1)])
    left, right = pick(is_first, *[dot(take_b_out, out_late[i][:, :640]).astype(BF) for i in (0, 1)])
    b_out = jnp.concatenate([left, right[:, 128:]], axis=1)
    left, right = pick(is_first, *[dot(put_inner_down, out_late[i][:, :640]).astype(BF) for i in (0, 1)])
    b_down = jnp.concatenate([left, right[:, 128:]], axis=1)
    a_gate, a_up = pick(is_first, *[dot(put_rows, out_late[i][:, 768:]).astype(BF) for i in (0, 1)])
    ff_all, _ = after((b_left, b_right, b_out, b_down, a_gate, a_up), ff_all)
    b_gate = ff_all[:, 144:160].reshape(256, 896)
    b_up = ff_all[:, 160:].reshape(256, 896)
    w_gate = (ff_all[:, :72].astype(F32) + dot(a_gate, b_gate).reshape(16, 72, 896)).astype(BF)
    w_up = (ff_all[:, 72:144].astype(F32) + dot(a_up, b_up).reshape(16, 72, 896)).astype(BF)
    w_gate, w_up = w_gate.reshape(1152, 896), w_up.reshape(1152, 896)
    down_parts, _ = after(w_up, down_parts)
    down_raw = placed(down_parts, "x", at_z, at_x).reshape(896, 1408)
    a_down = down_raw[:, 1152:]
    w_down = (down_raw[:, :1152].astype(F32) + dot(a_down, b_down)).astype(BF)

    gate = dot(u_all, w_gate)
    up = dot(u_all, w_up)
    act, act_pull = jax.vjp(lambda g, u: jax.nn.gelu(g, approximate=True) * u, gate, up)
    act = act.astype(BF)
    result = after_att + scatter_tokens(dot(act, w_down))

    valid = loss_token_mask[0].astype(F32)[:, None]
    error = result - teacher[0].astype(F32)
    loss_here = jnp.sum(valid * error * error)
    grad_result = 2.0 * 20480.0 / valid_count * valid * error

    g_all = gather_tokens(grad_result.astype(BF))
    g_act = dot_tr(g_all, w_down).astype(BF)
    g_gate, g_up = act_pull(g_act.astype(F32))
    g_gate, g_up = g_gate.astype(BF), g_up.astype(BF)
    g_u_part = dot_tr(g_gate, w_gate) + dot_tr(g_up, w_up)
    g_u_two = scatter_tokens(g_u_part)
    u_all, act, g_all, g_gate, g_up, _ = after(g_u_part, u_all, act, g_all, g_gate, g_up)
    gw_gate = dot_tl(u_all, g_gate).astype(BF)
    gb_gate = dot_tl(a_gate, gw_gate).astype(BF)
    gate_grads = jnp.concatenate([gw_gate.reshape(16, 72, 896), gb_gate.reshape(16, 16, 896)], axis=1)
    gate_first = leave(gate_grads.reshape(4, 4, 88, 896), "z", 0, at_z, at_x)
    gw_up = dot_tl(u_all, g_up).astype(BF)
    gb_up = dot_tl(a_up, gw_up).astype(BF)
    up_grads = jnp.concatenate([gw_up.reshape(16, 72, 896), gb_up.reshape(16, 16, 896)], axis=1)
    up_first = leave(up_grads.reshape(4, 4, 88, 896), "x", 1, at_z, at_x)
    gw_down = dot_tl(act, g_all).astype(BF)
    gb_down = dot_tl(a_down, gw_down).astype(BF)

    norm_two_back = norm_back(scale_two, n_two, gain_two_full, g_u_two)
    g_after = grad_result + norm_two_back
    g_after_b = g_after.astype(BF)
    once = jnp.where(jnp.arange(640) < 128, 0, 1).astype(BF)[None]
    g_half = pick(is_first, g_after_b[:, :640], g_after_b[:, 512:])
    g_once = pick(is_first, g_after_b[:, :640], g_after_b[:, 512:] * once)
    d_out = dot_tr(g_once[0], raw_out[0][:, :640]) + dot_tr(g_once[1], raw_out[1][:, :640])
    gi_out = dot_tr(d_out.astype(BF), put_inner_out).astype(BF)
    d_out = (
        d_out
        + dot_tr(gi_out[:, :128], raw_out[0][:, 640:768])
        + dot_tr(gi_out[:, 128:], raw_out[1][:, 640:768])
    )
    g_mix = dot_tr(d_out.astype(BF), put_mix).astype(BF)
    gate_first, _ = after(g_mix, gate_first)
    gate_line = add(gate_first).astype(BF)
    g_mix, _ = after(gate_line, g_mix)
    gate_second = leave(gate_line, "x", 0, at_z, at_x)
    g_rows = jnp.concatenate([g_mix[:, WIDTH * h : WIDTH * (h + 1)] for h in range(HEADS)], axis=0)
    scores_again = jnp.where(allowed, dot_tr(q_rows, keys) * score_scale, MASKED_SCORE)
    probs = jnp.where(allowed, jnp.exp(scores_again - lse), 0.0)
    g_probs = dot_tr(g_rows, values)
    g_scores = (probs * (g_probs - jnp.sum(probs * g_probs, axis=-1, keepdims=True))).astype(BF)
    g_keys = dot_tl(g_scores, q_rows) * score_scale
    g_values = dot_tl(probs.astype(BF), g_rows)
    g_kv = jnp.concatenate([g_keys, g_values], axis=1)
    n_mine = 8 * TOKENS
    up_first, g_kv = lax.optimization_barrier((up_first, g_kv))
    up_line = add(up_first).astype(BF)
    up_second = leave(up_line, "z", 0, at_z, at_x)
    g_away, _ = after(up_line, g_kv[n_mine:].astype(BF))
    g_kv_sum = g_kv[:n_mine] + other_core(g_away).astype(F32)
    g_kv_b = g_kv_sum.astype(BF)
    g_kv_b, gw_down = lax.optimization_barrier((g_kv_b, gw_down))
    down_first = leave(gw_down.reshape(4, 4, 56, 1152), "z", 1, at_z, at_x)
    g_parts = [shift(g_kv_b[320 * k : 320 * (k + 1)], "y", 4 - k) for k in (1, 2, 3)]
    g_scores, gb_down, _ = after(g_kv_b, g_scores, gb_down)
    g_pair = add([g_kv_sum[:320]] + list(g_parts))
    away = other_half(g_pair[160:].astype(BF))
    gate_second, up_second, _ = after(g_pair, gate_second, up_second)
    g_q_rows = dot(g_scores, keys) * score_scale
    g_q = [
        jnp.concatenate(
            [turn_back(g_q_rows[TOKENS * h : TOKENS * (h + 1)], cos, sin) for h in (2 * i, 2 * i + 1)],
            axis=1,
        ).astype(BF)
        for i in (0, 1)
    ]
    gate_sum, up_sum = add(gate_second).astype(BF), add(up_second).astype(BF)
    ga_part = jnp.concatenate(
        [dot_tr(gate_sum[:72], b_gate), dot_tr(up_sum[:72], b_up), jnp.zeros((72, 384), F32)], axis=1
    ).astype(BF)
    back_row = jnp.arange(256, dtype=jnp.int32)
    group, line = back_row // 32, back_row % 32
    take = jnp.where(
        line < 9,
        9 * group + line,
        jnp.where(
            line < 18,
            88 + 9 * group + line - 9,
            jnp.where(
                line < 22,
                72 + 88 * ((line - 18) // 2) + 2 * group + line % 2,
                jnp.where(line < 31, 176 + 9 * group + line - 22, -1),
            ),
        ),
    )
    leaving = dot(
        table(take, jnp.arange(248, dtype=jnp.int32)), jnp.concatenate([gate_sum, up_sum, ga_part], axis=0)
    ).astype(BF)
    slab = exchange(leaving.reshape(8, 32, 896), ("y", "c"))
    def of_chip(own, away):
        return (own.astype(F32) + other_core(away.astype(BF)).astype(F32)).astype(BF).reshape(64, 24, -1)

    def both_halves(owned):
        mine, away = pick(is_first, owned[:12], owned[12:])
        return pick(is_first, mine, other_core(away.astype(BF)).astype(F32))

    loss_high, loss_rest = split_in_two(loss_here)
    loss_mid, loss_low = split_in_two(loss_rest)
    lines = jnp.arange(16, dtype=jnp.int32)
    loss_rows = jnp.where(
        lines == 0,
        loss_high.astype(F32),
        jnp.where(lines == 1, loss_mid.astype(F32), jnp.where(lines == 2, loss_low, 0.0)),
    )
    more_side = (loss_rows[:, None] * (j == 11)[None, :]).astype(BF)
    more_grad = table(jnp.where(lines < 3, lines + 3 * core, -1), jnp.arange(512, dtype=jnp.int32))
    chip_q = of_chip(
        *[(dot_tl(sides[0], g_q[i]) + dot_tl(more_side, more_grad)).astype(BF) for i in (0, 1)]
    )
    side_out, _ = after(g_pair, side_out)
    left, right = pick(is_first, gb_down[:, :640], gb_down[:, 512:])
    chip_out = of_chip(
        dot_tl(side_out, g_half[0]) + dot_tl(put_inner_down, left),
        dot_tl(side_out, g_half[1]) + dot_tl(put_inner_down, right),
    )
    g_kv_own = g_pair[:160] + after(chip_q, away)[0].astype(F32)
    g_kv_own, down_first = lax.optimization_barrier((g_kv_own, down_first))
    down_second = leave(add(down_first).astype(BF), "x", 0, at_z, at_x)
    g_k = turn_back(g_kv_own[:, :256], cos, sin).astype(BF)
    g_v = g_kv_own[:, 256:].astype(BF)
    g_k = pick(is_first, g_k[:, :128], g_k[:, 128:])
    g_v = pick(is_first, g_v[:, :128], g_v[:, 128:])
    chip_kv = of_chip(
        *[
            jnp.concatenate([dot_tl(sides[1], g_k[i]).astype(BF), dot_tl(sides[2], g_v[i]).astype(BF)], axis=1)
            for i in (0, 1)
        ]
    )
    chip_sums = jnp.concatenate([chip_q, chip_kv, chip_out], axis=2)
    chip_sums, slab, g_q, g_k, g_v = lax.optimization_barrier((chip_sums, slab, g_q, g_k, g_v))
    parts = exchange(chip_sums, CHIPS)
    g_q, down_second = lax.optimization_barrier((g_q, down_second))

    d_one = None
    for i, (g, first, last) in enumerate(((g_q, 0, 512), (g_k, 512, 640), (g_v, 640, 768))):
        d = dot_tr(g[0], raw[0][:, first:last]) + dot_tr(g[1], raw[1][:, first:last])
        gi = dot_tr(d.astype(BF), put_inner).astype(BF)
        inner_at = 768 + 128 * i
        d = d + dot_tr(gi[:, :128], raw[0][:, inner_at : inner_at + 128])
        d = d + dot_tr(gi[:, 128:], raw[1][:, inner_at : inner_at + 128])
        d_one = d if d_one is None else d_one + d
    g_u_one = select_back(d_one, put_rows)
    grad_hidden = (g_after + norm_back(scale_one, n_one, gain_one_full, g_u_one)).astype(BF)

    narrow = dot_tr(slab.reshape(256, 896), wider).reshape(8, 32, 864)
    wide = jnp.concatenate([narrow[t] for t in range(8)], axis=1)
    ga = jnp.sum(slab[:, 22:31, :512].astype(F32), axis=0)
    gw_down_own = lax.ppermute(
        add(down_second).astype(BF), EVERY, [(b, a) for a, b in down_route()]
    )[:54]
    ga_down_own = dot_tr(gw_down_own, b_down)

    def over_columns(pairs):
        return sum(jnp.sum(a.astype(F32) * b, axis=1) for a, b in pairs)

    gain_two_own = over_columns(
        ((wg, wide[:9]), (wu, wide[9:18]), (ag, ga[:, :256]), (au, ga[:, 256:]))
    ) / (1.0 + gain_two.astype(F32))

    owned = jnp.sum(parts.astype(F32), axis=0)
    loss_value = jnp.sum(owned[11, :6]) / (1152.0 * valid_count)
    left, right = both_halves(owned)
    own_out = jnp.concatenate([left[:, 768:], right[:, 896:]], axis=1)
    ga_out_own = dot_tr(own_out[:8].astype(BF), b_out)
    left_b, right_b = left[:9].astype(BF), right[:9].astype(BF)
    ga_own = [
        dot_tr(left_b[:, first:last], b_left[:, first:last])
        + dot_tr(right_b[:, first:last], b_right[:, first:last])
        for first, last in ((0, 512), (512, 640), (640, 768))
    ]

    def columns(first, last, rows):
        return jnp.concatenate([left[rows, first:last], right[rows, first:last]], axis=1)

    top_rows, low_rows = slice(0, 9), slice(9, 11)
    gw_own = [columns(0, 512, top_rows), columns(512, 640, top_rows), columns(640, 768, top_rows)]
    gain_one_own = over_columns(
        list(zip((wq, wk, wv), gw_own)) + list(zip((aq, ak, av), ga_own))
    ) / (1.0 + gain_one.astype(F32))

    return (
        result.astype(BF)[None],
        loss_value,
        grad_hidden[None],
        gain_one_own,
        *gw_own,
        own_out[:8],
        ga_own[0],
        columns(0, 512, low_rows),
        ga_own[1],
        columns(512, 640, low_rows),
        ga_own[2],
        columns(640, 768, low_rows),
        ga_out_own,
        own_out[8:10],
        gain_two_own,
        wide[:9],
        wide[9:18],
        gw_down_own.astype(F32),
        ga[:, :256],
        wide[18:20],
        ga[:, 256:],
        wide[20:22],
        ga_down_own,
        own_out[10:],
    )


def solution(mesh):
    mesh = Mesh(mesh.devices.reshape([SIZES[a] for a in EVERY]), EVERY)
    tree, seq = ("z", "xl"), ("xh", "y", "c")
    rows = P(EVERY, None)
    vector = P(EVERY)
    return jax.shard_map(
        on_device,
        mesh=mesh,
        in_specs=(
            P(tree, seq, None),
            P(tree, None),
            P(tree, None),
            P(tree, seq),
            P(tree, seq, None),
            vector,
        )
        + (rows,) * 12
        + (vector,)
        + (rows,) * 9,
        out_specs=(P(tree, seq, None), P(), P(tree, seq, None), vector)
        + (rows,) * 12
        + (vector,)
        + (rows,) * 9,
        check_vma=False,
    )
```

```python
import jax
import jax.numpy as jnp
from jax import lax
from jax.sharding import Mesh, PartitionSpec as P

EPSILON = 1e-06
ROPE_BASE = 10000.0
MASKED_SCORE = -1e30
BF = jnp.bfloat16
F32 = jnp.float32

PLANE = ("z", "xl", "xh")
CHIPS = ("z", "xl", "xh", "y")
EVERY = ("z", "xl", "xh", "y", "c")
SIZES = dict(z=4, xl=2, xh=2, y=4, c=2)
RING = dict(z="z", x=("xl", "xh"), y="y")
TOKENS = 160
HEADS = 4
WIDTH = 256


def dot(a, b):
    return jnp.dot(a, b, preferred_element_type=F32)


def dot_tl(a, b):
    return lax.dot_general(a, b, (((0,), (0,)), ((), ())), preferred_element_type=F32)


def dot_tr(a, b):
    return lax.dot_general(a, b, (((1,), (1,)), ((), ())), preferred_element_type=F32)


def exchange(x, axes):
    return lax.all_to_all(x, axes, split_axis=0, concat_axis=0, tiled=True)


def other_core(x):
    return lax.ppermute(x, "c", [(0, 1), (1, 0)])


def other_half(x):
    return lax.ppermute(x, "xh", [(0, 1), (1, 0)])


def shift(x, axis, k):
    number = [0, 2, 1, 3] if axis == "x" else [0, 1, 2, 3]
    return lax.ppermute(x, RING[axis], [(number[i], number[(i + k) % 4]) for i in range(4)])


def pick(cond, a, b):
    return jnp.where(cond, a, b), jnp.where(cond, b, a)


def split_in_two(x):
    high = x.astype(BF)
    return high, x - high.astype(F32)


def select_back(x, table):
    high, low = split_in_two(x)
    return dot_tr(high, table) + dot_tr(low.astype(BF), table)


def down_route():
    pairs = []
    for o in range(16):
        for t in range(8):
            block = 8 * (o % 2) + t
            pairs.append((8 * o + t, 8 * (block % 4 * 4 + block // 4) + o // 2))
    return pairs


def ring_place(axis, k, at_z, at_x):
    return (at_z - k) % 4 if axis == "z" else (at_x - k) % 4 % 2 * 2 + (at_x - k) % 4 // 2


def placed(parts, axis, at_z, at_x):
    stack = jnp.zeros((4,) + parts[0].shape, parts[0].dtype)
    for k, part in enumerate(parts):
        stack = lax.dynamic_update_index_in_dim(stack, part, ring_place(axis, k, at_z, at_x), 0)
    return stack


def leave(x, axis, dim, at_z, at_x):
    parts = []
    for k in range(4):
        block = lax.dynamic_index_in_dim(x, ring_place(axis, k, at_z, at_x), dim, keepdims=False)
        parts.append(shift(block, axis, 4 - k) if k else block)
    return parts


def add(parts):
    total = parts[0].astype(F32)
    for p in parts[1:]:
        total = total + p.astype(F32)
    return total


def norm_parts(values, gain):
    scale = lax.rsqrt(jnp.mean(values * values, axis=-1, keepdims=True) + EPSILON)
    n = values * scale
    return scale, n, (n * (1.0 + gain)).astype(BF)


def norm_back(scale, n, gain, grad):
    m = grad * (1.0 + gain)
    back = scale * (m - n * jnp.mean(m * n, axis=-1, keepdims=True))
    return back


def turn(x, cos, sin):
    h = cos.shape[-1]
    a, b = x[:, :h], x[:, h:]
    return jnp.concatenate([a * cos - b * sin, b * cos + a * sin], axis=-1)


def turn_back(x, cos, sin):
    return turn(x, cos, -sin)


def gather_tokens(x):
    mine = [x] + [shift(x, "y", k) for k in (1, 2, 3)]
    return jnp.concatenate(mine + [other_core(p) for p in mine], axis=0)


def scatter_tokens(part):
    blocks = part.reshape(2, 4, TOKENS, -1)
    total = None
    for k in (2, 1, 3, 0):
        piece = blocks[0, k] + other_core(blocks[1, k].astype(BF)).astype(F32)
        if k:
            piece = shift(piece.astype(BF), "y", 4 - k).astype(F32)
        total = piece if total is None else total + piece
    return total


def after(done, *values):
    return tuple(lax.optimization_barrier((v, done))[0] for v in values) + (done,)


def table(rows, columns):
    return (rows[:, None] == columns[None, :]).astype(BF)


def on_device(
    layer_input,
    segment,
    position,
    loss_token_mask,
    teacher,
    gain_one,
    wq,
    wk,
    wv,
    wo,
    aq,
    bq,
    ak,
    bk,
    av,
    bv,
    ao,
    bo,
    gain_two,
    wg,
    wu,
    wd,
    ag,
    bg,
    au,
    bu,
    ad,
    bd,
):
    core = lax.axis_index("c")
    at_z, at_y = lax.axis_index("z"), lax.axis_index("y")
    at_xl, at_xh = lax.axis_index("xl"), lax.axis_index("xh")
    at_x = 2 * at_xh + at_xl
    is_first = core == 0
    score_scale = WIDTH**-0.5
    count_here = jnp.sum(loss_token_mask[0]).astype(BF)

    extra = jnp.concatenate([gain_one[None], gain_two[None], count_here.reshape(1, 1)], axis=1)
    extra = jnp.pad(extra, ((0, 1), (0, 384 - 19)))

    def attention_half(k):
        top = jnp.concatenate(
            [m[:, m.shape[1] // 2 * k : m.shape[1] // 2 * (k + 1)] for m in (wq, wk, wv, aq, ak, av)],
            axis=1,
        )
        low = jnp.concatenate(
            [m[:, m.shape[1] // 2 * k : m.shape[1] // 2 * (k + 1)] for m in (bq, bk, bv)] + [extra],
            axis=1,
        )
        return jnp.concatenate([top, low, jnp.zeros((1, 1152), BF)], axis=0)

    keep, send = pick(is_first, attention_half(0), attention_half(1))
    lower, upper = pick(is_first, keep, other_core(send))
    att_own = jnp.concatenate([lower, upper], axis=0)
    att_wide = jnp.broadcast_to(att_own[None], (64, 24, 1152))
    raw_one = exchange(att_wide, CHIPS)
    (layer_input, wg, wu, bg, bu, wd, ad, ag, au, wo, ao, bo, bd, segment, position, core, at_z, _) = after(
        att_wide,
        layer_input, wg, wu, bg, bu, wd, ad, ag, au, wo, ao, bo, bd, segment, position, core, at_z,
    )
    is_first = core == 0
    hidden = layer_input[0].astype(F32)

    def output_half(k):
        wide = jnp.concatenate([m[:, 512 * k : 512 * k + 640] for m in (wo, bo, bd)], axis=0)
        narrow = jnp.pad(ao[:, 128 * k : 128 * k + 128], ((0, 4), (0, 0)))
        return jnp.concatenate([wide, narrow, jnp.pad((ag, au)[k], ((0, 3), (0, 0)))], axis=1)

    keep, send = pick(is_first, output_half(0), output_half(1))
    lower, upper = pick(is_first, keep, other_core(send))
    out_own = jnp.concatenate([lower, upper], axis=0)

    rows22 = jnp.pad(jnp.concatenate([wg, wu, bg, bu], axis=0), ((0, 2), (0, 0)))
    rows22 = jnp.concatenate([rows22[:, 864 * t : 864 * (t + 1)] for t in range(8)], axis=0)
    wider = jnp.arange(896, dtype=jnp.int32)
    wider = table(jnp.arange(864, dtype=jnp.int32), jnp.where(wider % 56 < 54, wider // 56 * 54 + wider % 56, -1))
    rows22 = dot(rows22, wider).astype(BF).reshape(8, 24, 896)
    columns_of = rows22.reshape(4, 2, 24, 896)
    mine = lax.dynamic_index_in_dim(columns_of, core, 1, keepdims=False)
    theirs = lax.dynamic_index_in_dim(columns_of, 1 - core, 1, keepdims=False)
    columns_of = jnp.stack([mine, other_core(theirs)], axis=1).reshape(4, 48, 896)
    slab = []
    for k in range(4):
        piece = lax.dynamic_index_in_dim(columns_of, (at_y + k) % 4, 0, keepdims=False)
        slab.append(shift(piece, "y", k) if k else piece)
    slab = jnp.concatenate(slab, axis=0)
    back = jnp.arange(8, dtype=jnp.int32)
    sources = 2 * ((at_y - back // 2) % 4) + (core - back) % 2
    row = jnp.arange(176, dtype=jnp.int32)
    low = row - 144
    at_row = jnp.where(
        row < 72,
        row // 9 * 24 + row % 9,
        jnp.where(
            row < 144,
            (row - 72) // 9 * 24 + 9 + (row - 72) % 9,
            low % 16 // 2 * 24 + 18 + low // 16 * 2 + low % 2,
        ),
    )
    in_slab = jnp.arange(192, dtype=jnp.int32)
    in_slab = jnp.repeat(sources, 24) * 24 + in_slab % 24
    ff_own = dot(table(at_row, in_slab), slab).astype(BF)
    down_own = lax.ppermute(
        jnp.pad(jnp.concatenate([wd, ad], axis=1), ((0, 2), (0, 0))), EVERY, down_route()
    )
    seq = (at_xh * 4 + at_y) * 2 + core
    tree_seg = segment[0]
    tree_pos = position[0]
    own_seg = lax.dynamic_slice_in_dim(tree_seg, seq * TOKENS, TOKENS)
    own_pos = lax.dynamic_slice_in_dim(tree_pos, seq * TOKENS, TOKENS)
    freq = ROPE_BASE ** (-(jnp.arange(128, dtype=F32) * 2.0 / WIDTH))
    angles = own_pos.astype(F32)[:, None] * freq[None, :]
    cos, sin = jnp.cos(angles), jnp.sin(angles)
    back = jnp.arange(16, dtype=jnp.int32)
    block_at = (((at_xh - back % 2) % 2) * 4 + (at_y - back % 8 // 2) % 4) * 2 + jnp.where(
        back < 8, core, 1 - core
    )
    chosen = (block_at[:, None] == back[None, :]).astype(jnp.int32)[:, :, None]
    key_seg = jnp.sum(chosen * tree_seg.reshape(1, 16, TOKENS), axis=1).reshape(1, 2560)
    key_pos = jnp.sum(chosen * tree_pos.reshape(1, 16, TOKENS), axis=1).reshape(1, 2560)
    q_seg, q_pos = own_seg[:, None], own_pos[:, None]
    parent = (key_seg >= 1) & (key_seg <= 4) & (q_seg >= 5) & ((q_seg - 5) // 2 + 1 == key_seg)
    allowed = ((key_seg == q_seg) | (key_seg == 0) | parent) & (key_pos <= q_pos)

    scale_one = lax.rsqrt(jnp.mean(hidden * hidden, axis=-1, keepdims=True) + EPSILON)
    raw_one, _ = after((ff_own, out_own, down_own, cos, sin, allowed, scale_one), raw_one)
    raw_two = other_core(raw_one)
    marks = raw_one.reshape(128, 12, 1152)[:, 9, 768:896]
    gain_one_full = marks[:, :9].reshape(1, 1152).astype(F32)
    gain_two_full = marks[:, 9:18].reshape(1, 1152).astype(F32)
    valid_count = jnp.sum(marks[:, 18].astype(F32))
    out_own, _ = after(raw_one, out_own)
    out_wide = jnp.broadcast_to(out_own[None], (64, 24, 1024))
    down_z = [shift(down_own, "z", k) for k in (1, 2, 3)]
    out_wide, down_z = lax.optimization_barrier((out_wide, down_z))
    out_one = exchange(out_wide, CHIPS)
    out_two = other_core(out_one)
    raw_out = [out_one.reshape(1536, 1024), out_two.reshape(1536, 1024)]
    raw_one, raw_two, _ = after(out_wide, raw_one, raw_two)
    raw = [raw_one.reshape(1536, 1152), raw_two.reshape(1536, 1152)]
    ids = jnp.arange(1536, dtype=jnp.int32)
    dev, j = 2 * (ids // 24) + (ids % 24) // 12, ids % 12
    halves = jnp.arange(256, dtype=jnp.int32)
    inner_ids = jnp.where(halves < 128, 128 * core + halves, 128 * (1 - core) + halves - 128)
    heads_at = jnp.arange(1024, dtype=jnp.int32)
    head_ids = jnp.where(heads_at < 512, 512 * core + heads_at, 512 * (1 - core) + heads_at - 512)
    features = jnp.arange(1152, dtype=jnp.int32)
    put_rows = table(features, jnp.where(j < 9, 9 * dev + j, -1))
    put_inner = table(inner_ids, jnp.where((j >= 9) & (j < 11), 2 * dev + j - 9, -1))
    take_b = table(halves, jnp.where((j >= 9) & (j < 11), 2 * dev + j - 9, -1))
    take_b_out = table(halves, jnp.where((j >= 8) & (j < 10), 2 * dev + j - 8, -1))
    put_mix = table(head_ids, jnp.where(j < 8, 8 * dev + j, -1))
    put_inner_out = table(inner_ids, jnp.where((j >= 8) & (j < 10), 2 * dev + j - 8, -1))
    put_inner_down = table(halves, jnp.where(j >= 10, 2 * dev + j - 10, -1))

    allowed = jnp.concatenate([allowed] * HEADS, axis=0)
    n_one = hidden * scale_one
    u_one = (n_one * (1.0 + gain_one_full)).astype(BF)
    u_rows = dot(u_one, put_rows).astype(BF)
    inner = [dot(u_rows, raw[i][:, 768:]).astype(BF) for i in (0, 1)]
    sides = []
    for i in range(3):
        part = jnp.concatenate([inner[0][:, 128 * i : 128 * i + 128], inner[1][:, 128 * i : 128 * i + 128]], axis=1)
        sides.append(u_rows + dot(part, put_inner).astype(BF))
    kk = pick(is_first, *[dot(sides[1], raw[i][:, 512:640]) for i in (0, 1)])
    vv = pick(is_first, *[dot(sides[2], raw[i][:, 640:768]) for i in (0, 1)])
    kv_own = jnp.concatenate([turn(jnp.concatenate(kk, axis=1), cos, sin), vv[0], vv[1]], axis=1).astype(BF)

    pair = jnp.concatenate([kv_own, other_half(kv_own)], axis=0)
    down_line = placed([down_own] + down_z, "z", at_z, at_x)
    ff_own, _ = after((out_one, down_line), ff_own)
    ff_wide = jnp.broadcast_to(ff_own[None], (16, 176, 896))
    ff_all = exchange(ff_wide, PLANE)
    kv_parts = [pair] + list(after(ff_wide, *[shift(pair, "y", k) for k in (1, 2, 3)])[:3])
    kv_mine = jnp.concatenate(kv_parts, axis=0)
    kv = jnp.concatenate([kv_mine, other_core(kv_mine)], axis=0)
    kv, down_line = lax.optimization_barrier((kv, down_line))
    down_parts = [down_line] + [shift(down_line, "x", k) for k in (1, 2, 3)]
    keys, values = kv[:, :256], kv[:, 256:]
    queries = [dot(sides[0], raw[i][:, :512]) for i in (0, 1)]
    q_rows = jnp.concatenate(
        [turn(queries[h // 2][:, WIDTH * (h % 2) : WIDTH * (h % 2 + 1)], cos, sin) for h in range(HEADS)],
        axis=0,
    ).astype(BF)
    scores = jnp.where(allowed, dot_tr(q_rows, keys) * score_scale, MASKED_SCORE)
    top = jnp.max(scores, axis=-1, keepdims=True)
    ex = jnp.exp(scores - top)
    total = jnp.sum(ex, axis=-1, keepdims=True)
    lse = top + jnp.log(total)
    mix_rows = dot((ex / total).astype(BF), values).astype(BF)
    mix = jnp.concatenate([mix_rows[TOKENS * h : TOKENS * (h + 1)] for h in range(HEADS)], axis=1)
    mix_placed = dot(mix, put_mix).astype(BF)
    inner_out = jnp.concatenate([dot(mix_placed, raw_out[i][:, 640:768]) for i in (0, 1)], axis=1).astype(BF)
    side_out = mix_placed + dot(inner_out, put_inner_out).astype(BF)
    left, right = pick(is_first, *[dot(side_out, raw_out[i][:, :640]) for i in (0, 1)])
    after_att = hidden + jnp.concatenate([left, right[:, 128:]], axis=1)

    scale_two, n_two, u_two = norm_parts(after_att, gain_two_full)
    u_all = gather_tokens(u_two)

    raw_late, out_late, _ = after(u_two, raw, raw_out)
    b_left, b_right = pick(is_first, *[dot(take_b, raw_late[i][:, :768]).astype(BF) for i in (0, 1)])
    left, right = pick(is_first, *[dot(take_b_out, out_late[i][:, :640]).astype(BF) for i in (0, 1)])
    b_out = jnp.concatenate([left, right[:, 128:]], axis=1)
    left, right = pick(is_first, *[dot(put_inner_down, out_late[i][:, :640]).astype(BF) for i in (0, 1)])
    b_down = jnp.concatenate([left, right[:, 128:]], axis=1)
    a_gate, a_up = pick(is_first, *[dot(put_rows, out_late[i][:, 768:]).astype(BF) for i in (0, 1)])
    ff_all, _ = after((b_left, b_right, b_out, b_down, a_gate, a_up), ff_all)
    b_gate = ff_all[:, 144:160].reshape(256, 896)
    b_up = ff_all[:, 160:].reshape(256, 896)
    w_gate = (ff_all[:, :72].astype(F32) + dot(a_gate, b_gate).reshape(16, 72, 896)).astype(BF)
    w_up = (ff_all[:, 72:144].astype(F32) + dot(a_up, b_up).reshape(16, 72, 896)).astype(BF)
    w_gate, w_up = w_gate.reshape(1152, 896), w_up.reshape(1152, 896)
    down_parts, _ = after(w_up, down_parts)
    down_raw = placed(down_parts, "x", at_z, at_x).reshape(896, 1408)
    a_down = down_raw[:, 1152:]
    w_down = (down_raw[:, :1152].astype(F32) + dot(a_down, b_down)).astype(BF)

    gate = dot(u_all, w_gate)
    up = dot(u_all, w_up)
    act, act_pull = jax.vjp(lambda g, u: jax.nn.gelu(g, approximate=True) * u, gate, up)
    act = act.astype(BF)
    result = after_att + scatter_tokens(dot(act, w_down))

    valid = loss_token_mask[0].astype(F32)[:, None]
    error = result - teacher[0].astype(F32)
    loss_here = jnp.sum(valid * error * error)
    grad_result = 2.0 * 20480.0 / valid_count * valid * error

    g_all = gather_tokens(grad_result.astype(BF))
    g_act = dot_tr(g_all, w_down).astype(BF)
    g_gate, g_up = act_pull(g_act.astype(F32))
    g_gate, g_up = g_gate.astype(BF), g_up.astype(BF)
    g_u_part = dot_tr(g_gate, w_gate) + dot_tr(g_up, w_up)
    g_u_two = scatter_tokens(g_u_part)
    u_all, act, g_all, g_gate, g_up, _ = after(g_u_part, u_all, act, g_all, g_gate, g_up)
    gw_gate = dot_tl(u_all, g_gate).astype(BF)
    gb_gate = dot_tl(a_gate, gw_gate).astype(BF)
    gate_grads = jnp.concatenate([gw_gate.reshape(16, 72, 896), gb_gate.reshape(16, 16, 896)], axis=1)
    gate_first = leave(gate_grads.reshape(4, 4, 88, 896), "z", 0, at_z, at_x)
    gw_up = dot_tl(u_all, g_up).astype(BF)
    gb_up = dot_tl(a_up, gw_up).astype(BF)
    up_grads = jnp.concatenate([gw_up.reshape(16, 72, 896), gb_up.reshape(16, 16, 896)], axis=1)
    up_first = leave(up_grads.reshape(4, 4, 88, 896), "x", 1, at_z, at_x)
    gw_down = dot_tl(act, g_all).astype(BF)
    gb_down = dot_tl(a_down, gw_down).astype(BF)

    norm_two_back = norm_back(scale_two, n_two, gain_two_full, g_u_two)
    g_after = grad_result + norm_two_back
    g_after_b = g_after.astype(BF)
    once = jnp.where(jnp.arange(640) < 128, 0, 1).astype(BF)[None]
    g_half = pick(is_first, g_after_b[:, :640], g_after_b[:, 512:])
    g_once = pick(is_first, g_after_b[:, :640], g_after_b[:, 512:] * once)
    d_out = dot_tr(g_once[0], raw_out[0][:, :640]) + dot_tr(g_once[1], raw_out[1][:, :640])
    gi_out = dot_tr(d_out.astype(BF), put_inner_out).astype(BF)
    d_out = (
        d_out
        + dot_tr(gi_out[:, :128], raw_out[0][:, 640:768])
        + dot_tr(gi_out[:, 128:], raw_out[1][:, 640:768])
    )
    g_mix = dot_tr(d_out.astype(BF), put_mix).astype(BF)
    gate_first, _ = after(g_mix, gate_first)
    gate_line = add(gate_first).astype(BF)
    g_mix, _ = after(gate_line, g_mix)
    gate_second = leave(gate_line, "x", 0, at_z, at_x)
    g_rows = jnp.concatenate([g_mix[:, WIDTH * h : WIDTH * (h + 1)] for h in range(HEADS)], axis=0)
    scores_again = jnp.where(allowed, dot_tr(q_rows, keys) * score_scale, MASKED_SCORE)
    probs = jnp.where(allowed, jnp.exp(scores_again - lse), 0.0)
    g_probs = dot_tr(g_rows, values)
    g_scores = (probs * (g_probs - jnp.sum(probs * g_probs, axis=-1, keepdims=True))).astype(BF)
    g_keys = dot_tl(g_scores, q_rows) * score_scale
    g_values = dot_tl(probs.astype(BF), g_rows)
    g_kv = jnp.concatenate([g_keys, g_values], axis=1)
    n_mine = 8 * TOKENS
    up_first, g_kv = lax.optimization_barrier((up_first, g_kv))
    up_line = add(up_first).astype(BF)
    up_second = leave(up_line, "z", 0, at_z, at_x)
    g_away, _ = after(up_line, g_kv[n_mine:].astype(BF))
    g_kv_sum = g_kv[:n_mine] + other_core(g_away).astype(F32)
    g_kv_b = g_kv_sum.astype(BF)
    g_kv_b, gw_down = lax.optimization_barrier((g_kv_b, gw_down))
    down_first = leave(gw_down.reshape(4, 4, 56, 1152), "z", 1, at_z, at_x)
    g_parts = [shift(g_kv_b[320 * k : 320 * (k + 1)], "y", 4 - k) for k in (1, 2, 3)]
    g_scores, gb_down, _ = after(g_kv_b, g_scores, gb_down)
    g_pair = add([g_kv_sum[:320]] + list(g_parts))
    away = other_half(g_pair[160:].astype(BF))
    gate_second, up_second, _ = after(g_pair, gate_second, up_second)
    g_q_rows = dot(g_scores, keys) * score_scale
    g_q = [
        jnp.concatenate(
            [turn_back(g_q_rows[TOKENS * h : TOKENS * (h + 1)], cos, sin) for h in (2 * i, 2 * i + 1)],
            axis=1,
        ).astype(BF)
        for i in (0, 1)
    ]
    gate_sum, up_sum = add(gate_second).astype(BF), add(up_second).astype(BF)
    ga_part = jnp.concatenate(
        [dot_tr(gate_sum[:72], b_gate), dot_tr(up_sum[:72], b_up), jnp.zeros((72, 384), F32)], axis=1
    ).astype(BF)
    back_row = jnp.arange(256, dtype=jnp.int32)
    group, line = back_row // 32, back_row % 32
    take = jnp.where(
        line < 9,
        9 * group + line,
        jnp.where(
            line < 18,
            88 + 9 * group + line - 9,
            jnp.where(
                line < 22,
                72 + 88 * ((line - 18) // 2) + 2 * group + line % 2,
                jnp.where(line < 31, 176 + 9 * group + line - 22, -1),
            ),
        ),
    )
    leaving = dot(
        table(take, jnp.arange(248, dtype=jnp.int32)), jnp.concatenate([gate_sum, up_sum, ga_part], axis=0)
    ).astype(BF)
    slab = exchange(leaving.reshape(8, 32, 896), ("y", "c"))
    def of_chip(own, away):
        return (own.astype(F32) + other_core(away.astype(BF)).astype(F32)).astype(BF).reshape(64, 24, -1)

    def both_halves(owned):
        mine, away = pick(is_first, owned[:12], owned[12:])
        return pick(is_first, mine, other_core(away.astype(BF)).astype(F32))

    loss_high, loss_rest = split_in_two(loss_here)
    loss_mid, loss_low = split_in_two(loss_rest)
    lines = jnp.arange(16, dtype=jnp.int32)
    loss_rows = jnp.where(
        lines == 0,
        loss_high.astype(F32),
        jnp.where(lines == 1, loss_mid.astype(F32), jnp.where(lines == 2, loss_low, 0.0)),
    )
    more_side = (loss_rows[:, None] * (j == 11)[None, :]).astype(BF)
    more_grad = table(jnp.where(lines < 3, lines + 3 * core, -1), jnp.arange(512, dtype=jnp.int32))
    chip_q = of_chip(
        *[(dot_tl(sides[0], g_q[i]) + dot_tl(more_side, more_grad)).astype(BF) for i in (0, 1)]
    )
    side_out, _ = after(g_pair, side_out)
    left, right = pick(is_first, gb_down[:, :640], gb_down[:, 512:])
    chip_out = of_chip(
        dot_tl(side_out, g_half[0]) + dot_tl(put_inner_down, left),
        dot_tl(side_out, g_half[1]) + dot_tl(put_inner_down, right),
    )
    g_kv_own = g_pair[:160] + after(chip_q, away)[0].astype(F32)
    g_kv_own, down_first = lax.optimization_barrier((g_kv_own, down_first))
    down_second = leave(add(down_first).astype(BF), "x", 0, at_z, at_x)
    g_k = turn_back(g_kv_own[:, :256], cos, sin).astype(BF)
    g_v = g_kv_own[:, 256:].astype(BF)
    g_k = pick(is_first, g_k[:, :128], g_k[:, 128:])
    g_v = pick(is_first, g_v[:, :128], g_v[:, 128:])
    chip_kv = of_chip(
        *[
            jnp.concatenate([dot_tl(sides[1], g_k[i]).astype(BF), dot_tl(sides[2], g_v[i]).astype(BF)], axis=1)
            for i in (0, 1)
        ]
    )
    chip_sums = jnp.concatenate([chip_q, chip_kv, chip_out], axis=2)
    chip_sums, slab, g_q, g_k, g_v = lax.optimization_barrier((chip_sums, slab, g_q, g_k, g_v))
    parts = exchange(chip_sums, CHIPS)
    g_q, down_second = lax.optimization_barrier((g_q, down_second))

    d_one = None
    for i, (g, first, last) in enumerate(((g_q, 0, 512), (g_k, 512, 640), (g_v, 640, 768))):
        d = dot_tr(g[0], raw[0][:, first:last]) + dot_tr(g[1], raw[1][:, first:last])
        gi = dot_tr(d.astype(BF), put_inner).astype(BF)
        inner_at = 768 + 128 * i
        d = d + dot_tr(gi[:, :128], raw[0][:, inner_at : inner_at + 128])
        d = d + dot_tr(gi[:, 128:], raw[1][:, inner_at : inner_at + 128])
        d_one = d if d_one is None else d_one + d
    g_u_one = select_back(d_one, put_rows)
    grad_hidden = (g_after + norm_back(scale_one, n_one, gain_one_full, g_u_one)).astype(BF)

    narrow = dot_tr(slab.reshape(256, 896), wider).reshape(8, 32, 864)
    wide = jnp.concatenate([narrow[t] for t in range(8)], axis=1)
    ga = jnp.sum(slab[:, 22:31, :512].astype(F32), axis=0)
    gw_down_own = lax.ppermute(
        add(down_second).astype(BF), EVERY, [(b, a) for a, b in down_route()]
    )[:54]
    ga_down_own = dot_tr(gw_down_own, b_down)

    def over_columns(pairs):
        return sum(jnp.sum(a.astype(F32) * b, axis=1) for a, b in pairs)

    gain_two_own = over_columns(
        ((wg, wide[:9]), (wu, wide[9:18]), (ag, ga[:, :256]), (au, ga[:, 256:]))
    ) / (1.0 + gain_two.astype(F32))

    owned = jnp.sum(parts.astype(F32), axis=0)
    loss_value = jnp.sum(owned[11, :6]) / (1152.0 * valid_count)
    left, right = both_halves(owned)
    own_out = jnp.concatenate([left[:, 768:], right[:, 896:]], axis=1)
    ga_out_own = dot_tr(own_out[:8].astype(BF), b_out)
    left_b, right_b = left[:9].astype(BF), right[:9].astype(BF)
    ga_own = [
        dot_tr(left_b[:, first:last], b_left[:, first:last])
        + dot_tr(right_b[:, first:last], b_right[:, first:last])
        for first, last in ((0, 512), (512, 640), (640, 768))
    ]

    def columns(first, last, rows):
        return jnp.concatenate([left[rows, first:last], right[rows, first:last]], axis=1)

    top_rows, low_rows = slice(0, 9), slice(9, 11)
    gw_own = [columns(0, 512, top_rows), columns(512, 640, top_rows), columns(640, 768, top_rows)]
    gain_one_own = over_columns(
        list(zip((wq, wk, wv), gw_own)) + list(zip((aq, ak, av), ga_own))
    ) / (1.0 + gain_one.astype(F32))

    return (
        result.astype(BF)[None],
        loss_value,
        grad_hidden[None],
        gain_one_own,
        *gw_own,
        own_out[:8],
        ga_own[0],
        columns(0, 512, low_rows),
        ga_own[1],
        columns(512, 640, low_rows),
        ga_own[2],
        columns(640, 768, low_rows),
        ga_out_own,
        own_out[8:10],
        gain_two_own,
        wide[:9],
        wide[9:18],
        gw_down_own.astype(F32),
        ga[:, :256],
        wide[18:20],
        ga[:, 256:],
        wide[20:22],
        ga_down_own,
        own_out[10:],
    )


def solution(mesh):
    mesh = Mesh(mesh.devices.reshape([SIZES[a] for a in EVERY]), EVERY)
    tree, seq = ("z", "xl"), ("xh", "y", "c")
    rows = P(EVERY, None)
    vector = P(EVERY)
    return jax.shard_map(
        on_device,
        mesh=mesh,
        in_specs=(
            P(tree, seq, None),
            P(tree, None),
            P(tree, None),
            P(tree, seq),
            P(tree, seq, None),
            vector,
        )
        + (rows,) * 12
        + (vector,)
        + (rows,) * 9,
        out_specs=(P(tree, seq, None), P(), P(tree, seq, None), vector)
        + (rows,) * 12
        + (vector,)
        + (rows,) * 9,
        check_vma=False,
    )
```

```python
import jax
import jax.numpy as jnp
from jax import lax
from jax.sharding import Mesh, PartitionSpec as P

EPSILON = 1e-06
ROPE_BASE = 10000.0
MASKED_SCORE = -1e30
BF = jnp.bfloat16
F32 = jnp.float32

PLANE = ("z", "xl", "xh")
CHIPS = ("z", "xl", "xh", "y")
EVERY = ("z", "xl", "xh", "y", "c")
SIZES = dict(z=4, xl=2, xh=2, y=4, c=2)
RING = dict(z="z", x=("xl", "xh"), y="y")
TOKENS = 160
HEADS = 4
WIDTH = 256


def dot(a, b):
    return jnp.dot(a, b, preferred_element_type=F32)


def dot_tl(a, b):
    return lax.dot_general(a, b, (((0,), (0,)), ((), ())), preferred_element_type=F32)


def dot_tr(a, b):
    return lax.dot_general(a, b, (((1,), (1,)), ((), ())), preferred_element_type=F32)


def exchange(x, axes):
    return lax.all_to_all(x, axes, split_axis=0, concat_axis=0, tiled=True)


def other_core(x):
    return lax.ppermute(x, "c", [(0, 1), (1, 0)])


def other_half(x):
    return lax.ppermute(x, "xh", [(0, 1), (1, 0)])


def shift(x, axis, k):
    number = [0, 2, 1, 3] if axis == "x" else [0, 1, 2, 3]
    return lax.ppermute(x, RING[axis], [(number[i], number[(i + k) % 4]) for i in range(4)])


def pick(cond, a, b):
    return jnp.where(cond, a, b), jnp.where(cond, b, a)


def split_in_two(x):
    high = x.astype(BF)
    return high, x - high.astype(F32)


def select_back(x, table):
    high, low = split_in_two(x)
    return dot_tr(high, table) + dot_tr(low.astype(BF), table)


def down_route():
    pairs = []
    for o in range(16):
        for t in range(8):
            block = 8 * (o % 2) + t
            pairs.append((8 * o + t, 8 * (block % 4 * 4 + block // 4) + o // 2))
    return pairs


def ring_place(axis, k, at_z, at_x):
    return (at_z - k) % 4 if axis == "z" else (at_x - k) % 4 % 2 * 2 + (at_x - k) % 4 // 2


def placed(parts, axis, at_z, at_x):
    stack = jnp.zeros((4,) + parts[0].shape, parts[0].dtype)
    for k, part in enumerate(parts):
        stack = lax.dynamic_update_index_in_dim(stack, part, ring_place(axis, k, at_z, at_x), 0)
    return stack


def leave(x, axis, dim, at_z, at_x):
    parts = []
    for k in range(4):
        block = lax.dynamic_index_in_dim(x, ring_place(axis, k, at_z, at_x), dim, keepdims=False)
        parts.append(shift(block, axis, 4 - k) if k else block)
    return parts


def add(parts):
    total = parts[0].astype(F32)
    for p in parts[1:]:
        total = total + p.astype(F32)
    return total


def norm_parts(values, gain):
    scale = lax.rsqrt(jnp.mean(values * values, axis=-1, keepdims=True) + EPSILON)
    n = values * scale
    return scale, n, (n * (1.0 + gain)).astype(BF)


def norm_back(scale, n, gain, grad):
    m = grad * (1.0 + gain)
    back = scale * (m - n * jnp.mean(m * n, axis=-1, keepdims=True))
    return back


def turn(x, cos, sin):
    h = cos.shape[-1]
    a, b = x[:, :h], x[:, h:]
    return jnp.concatenate([a * cos - b * sin, b * cos + a * sin], axis=-1)


def turn_back(x, cos, sin):
    return turn(x, cos, -sin)


def gather_tokens(x):
    mine = [x] + [shift(x, "y", k) for k in (1, 2, 3)]
    return jnp.concatenate(mine + [other_core(p) for p in mine], axis=0)


def scatter_tokens(part):
    blocks = part.reshape(2, 4, TOKENS, -1)
    total = None
    for k in (2, 1, 3, 0):
        piece = blocks[0, k] + other_core(blocks[1, k].astype(BF)).astype(F32)
        if k:
            piece = shift(piece.astype(BF), "y", 4 - k).astype(F32)
        total = piece if total is None else total + piece
    return total


def after(done, *values):
    return tuple(lax.optimization_barrier((v, done))[0] for v in values) + (done,)


def table(rows, columns):
    return (rows[:, None] == columns[None, :]).astype(BF)


def on_device(
    layer_input,
    segment,
    position,
    loss_token_mask,
    teacher,
    gain_one,
    wq,
    wk,
    wv,
    wo,
    aq,
    bq,
    ak,
    bk,
    av,
    bv,
    ao,
    bo,
    gain_two,
    wg,
    wu,
    wd,
    ag,
    bg,
    au,
    bu,
    ad,
    bd,
):
    core = lax.axis_index("c")
    at_z, at_y = lax.axis_index("z"), lax.axis_index("y")
    at_xl, at_xh = lax.axis_index("xl"), lax.axis_index("xh")
    at_x = 2 * at_xh + at_xl
    is_first = core == 0
    score_scale = WIDTH**-0.5
    count_here = jnp.sum(loss_token_mask[0]).astype(BF)

    extra = jnp.concatenate([gain_one[None], gain_two[None], count_here.reshape(1, 1)], axis=1)
    extra = jnp.pad(extra, ((0, 1), (0, 384 - 19)))

    def attention_half(k):
        top = jnp.concatenate(
            [m[:, m.shape[1] // 2 * k : m.shape[1] // 2 * (k + 1)] for m in (wq, wk, wv, aq, ak, av)],
            axis=1,
        )
        low = jnp.concatenate(
            [m[:, m.shape[1] // 2 * k : m.shape[1] // 2 * (k + 1)] for m in (bq, bk, bv)] + [extra],
            axis=1,
        )
        return jnp.concatenate([top, low, jnp.zeros((1, 1152), BF)], axis=0)

    keep, send = pick(is_first, attention_half(0), attention_half(1))
    lower, upper = pick(is_first, keep, other_core(send))
    att_own = jnp.concatenate([lower, upper], axis=0)
    att_wide = jnp.broadcast_to(att_own[None], (64, 24, 1152))
    raw_one = exchange(att_wide, CHIPS)
    (layer_input, wg, wu, bg, bu, wd, ad, ag, au, wo, ao, bo, bd, segment, position, core, at_z, _) = after(
        att_wide,
        layer_input, wg, wu, bg, bu, wd, ad, ag, au, wo, ao, bo, bd, segment, position, core, at_z,
    )
    is_first = core == 0
    hidden = layer_input[0].astype(F32)

    def output_half(k):
        wide = jnp.concatenate([m[:, 512 * k : 512 * k + 640] for m in (wo, bo, bd)], axis=0)
        narrow = jnp.pad(ao[:, 128 * k : 128 * k + 128], ((0, 4), (0, 0)))
        return jnp.concatenate([wide, narrow, jnp.pad((ag, au)[k], ((0, 3), (0, 0)))], axis=1)

    keep, send = pick(is_first, output_half(0), output_half(1))
    lower, upper = pick(is_first, keep, other_core(send))
    out_own = jnp.concatenate([lower, upper], axis=0)

    rows22 = jnp.pad(jnp.concatenate([wg, wu, bg, bu], axis=0), ((0, 2), (0, 0)))
    rows22 = jnp.concatenate([rows22[:, 864 * t : 864 * (t + 1)] for t in range(8)], axis=0)
    wider = jnp.arange(896, dtype=jnp.int32)
    wider = table(jnp.arange(864, dtype=jnp.int32), jnp.where(wider % 56 < 54, wider // 56 * 54 + wider % 56, -1))
    rows22 = dot(rows22, wider).astype(BF).reshape(8, 24, 896)
    columns_of = rows22.reshape(4, 2, 24, 896)
    mine = lax.dynamic_index_in_dim(columns_of, core, 1, keepdims=False)
    theirs = lax.dynamic_index_in_dim(columns_of, 1 - core, 1, keepdims=False)
    columns_of = jnp.stack([mine, other_core(theirs)], axis=1).reshape(4, 48, 896)
    slab = []
    for k in range(4):
        piece = lax.dynamic_index_in_dim(columns_of, (at_y + k) % 4, 0, keepdims=False)
        slab.append(shift(piece, "y", k) if k else piece)
    slab = jnp.concatenate(slab, axis=0)
    back = jnp.arange(8, dtype=jnp.int32)
    sources = 2 * ((at_y - back // 2) % 4) + (core - back) % 2
    row = jnp.arange(176, dtype=jnp.int32)
    low = row - 144
    at_row = jnp.where(
        row < 72,
        row // 9 * 24 + row % 9,
        jnp.where(
            row < 144,
            (row - 72) // 9 * 24 + 9 + (row - 72) % 9,
            low % 16 // 2 * 24 + 18 + low // 16 * 2 + low % 2,
        ),
    )
    in_slab = jnp.arange(192, dtype=jnp.int32)
    in_slab = jnp.repeat(sources, 24) * 24 + in_slab % 24
    ff_own = dot(table(at_row, in_slab), slab).astype(BF)
    down_own = lax.ppermute(
        jnp.pad(jnp.concatenate([wd, ad], axis=1), ((0, 2), (0, 0))), EVERY, down_route()
    )
    seq = (at_xh * 4 + at_y) * 2 + core
    tree_seg = segment[0]
    tree_pos = position[0]
    own_seg = lax.dynamic_slice_in_dim(tree_seg, seq * TOKENS, TOKENS)
    own_pos = lax.dynamic_slice_in_dim(tree_pos, seq * TOKENS, TOKENS)
    freq = ROPE_BASE ** (-(jnp.arange(128, dtype=F32) * 2.0 / WIDTH))
    angles = own_pos.astype(F32)[:, None] * freq[None, :]
    cos, sin = jnp.cos(angles), jnp.sin(angles)
    back = jnp.arange(16, dtype=jnp.int32)
    block_at = (((at_xh - back % 2) % 2) * 4 + (at_y - back % 8 // 2) % 4) * 2 + jnp.where(
        back < 8, core, 1 - core
    )
    chosen = (block_at[:, None] == back[None, :]).astype(jnp.int32)[:, :, None]
    key_seg = jnp.sum(chosen * tree_seg.reshape(1, 16, TOKENS), axis=1).reshape(1, 2560)
    key_pos = jnp.sum(chosen * tree_pos.reshape(1, 16, TOKENS), axis=1).reshape(1, 2560)
    q_seg, q_pos = own_seg[:, None], own_pos[:, None]
    parent = (key_seg >= 1) & (key_seg <= 4) & (q_seg >= 5) & ((q_seg - 5) // 2 + 1 == key_seg)
    allowed = ((key_seg == q_seg) | (key_seg == 0) | parent) & (key_pos <= q_pos)

    scale_one = lax.rsqrt(jnp.mean(hidden * hidden, axis=-1, keepdims=True) + EPSILON)
    raw_one, _ = after((ff_own, out_own, down_own, cos, sin, allowed, scale_one), raw_one)
    raw_two = other_core(raw_one)
    marks = raw_one.reshape(128, 12, 1152)[:, 9, 768:896]
    gain_one_full = marks[:, :9].reshape(1, 1152).astype(F32)
    gain_two_full = marks[:, 9:18].reshape(1, 1152).astype(F32)
    valid_count = jnp.sum(marks[:, 18].astype(F32))
    out_own, _ = after(raw_one, out_own)
    out_wide = jnp.broadcast_to(out_own[None], (64, 24, 1024))
    down_z = [shift(down_own, "z", k) for k in (1, 2, 3)]
    out_wide, down_z = lax.optimization_barrier((out_wide, down_z))
    out_one = exchange(out_wide, CHIPS)
    out_two = other_core(out_one)
    raw_out = [out_one.reshape(1536, 1024), out_two.reshape(1536, 1024)]
    raw_one, raw_two, _ = after(out_wide, raw_one, raw_two)
    raw = [raw_one.reshape(1536, 1152), raw_two.reshape(1536, 1152)]
    ids = jnp.arange(1536, dtype=jnp.int32)
    dev, j = 2 * (ids // 24) + (ids % 24) // 12, ids % 12
    halves = jnp.arange(256, dtype=jnp.int32)
    inner_ids = jnp.where(halves < 128, 128 * core + halves, 128 * (1 - core) + halves - 128)
    heads_at = jnp.arange(1024, dtype=jnp.int32)
    head_ids = jnp.where(heads_at < 512, 512 * core + heads_at, 512 * (1 - core) + heads_at - 512)
    features = jnp.arange(1152, dtype=jnp.int32)
    put_rows = table(features, jnp.where(j < 9, 9 * dev + j, -1))
    put_inner = table(inner_ids, jnp.where((j >= 9) & (j < 11), 2 * dev + j - 9, -1))
    take_b = table(halves, jnp.where((j >= 9) & (j < 11), 2 * dev + j - 9, -1))
    take_b_out = table(halves, jnp.where((j >= 8) & (j < 10), 2 * dev + j - 8, -1))
    put_mix = table(head_ids, jnp.where(j < 8, 8 * dev + j, -1))
    put_inner_out = table(inner_ids, jnp.where((j >= 8) & (j < 10), 2 * dev + j - 8, -1))
    put_inner_down = table(halves, jnp.where(j >= 10, 2 * dev + j - 10, -1))

    allowed = jnp.concatenate([allowed] * HEADS, axis=0)
    n_one = hidden * scale_one
    u_one = (n_one * (1.0 + gain_one_full)).astype(BF)
    u_rows = dot(u_one, put_rows).astype(BF)
    inner = [dot(u_rows, raw[i][:, 768:]).astype(BF) for i in (0, 1)]
    sides = []
    for i in range(3):
        part = jnp.concatenate([inner[0][:, 128 * i : 128 * i + 128], inner[1][:, 128 * i : 128 * i + 128]], axis=1)
        sides.append(u_rows + dot(part, put_inner).astype(BF))
    kk = pick(is_first, *[dot(sides[1], raw[i][:, 512:640]) for i in (0, 1)])
    vv = pick(is_first, *[dot(sides[2], raw[i][:, 640:768]) for i in (0, 1)])
    kv_own = jnp.concatenate([turn(jnp.concatenate(kk, axis=1), cos, sin), vv[0], vv[1]], axis=1).astype(BF)

    pair = jnp.concatenate([kv_own, other_half(kv_own)], axis=0)
    down_line = placed([down_own] + down_z, "z", at_z, at_x)
    ff_own, _ = after((out_one, down_line), ff_own)
    ff_wide = jnp.broadcast_to(ff_own[None], (16, 176, 896))
    ff_all = exchange(ff_wide, PLANE)
    kv_parts = [pair] + list(after(ff_wide, *[shift(pair, "y", k) for k in (1, 2, 3)])[:3])
    kv_mine = jnp.concatenate(kv_parts, axis=0)
    kv = jnp.concatenate([kv_mine, other_core(kv_mine)], axis=0)
    kv, down_line = lax.optimization_barrier((kv, down_line))
    down_parts = [down_line] + [shift(down_line, "x", k) for k in (1, 2, 3)]
    keys, values = kv[:, :256], kv[:, 256:]
    queries = [dot(sides[0], raw[i][:, :512]) for i in (0, 1)]
    q_rows = jnp.concatenate(
        [turn(queries[h // 2][:, WIDTH * (h % 2) : WIDTH * (h % 2 + 1)], cos, sin) for h in range(HEADS)],
        axis=0,
    ).astype(BF)
    scores = jnp.where(allowed, dot_tr(q_rows, keys) * score_scale, MASKED_SCORE)
    top = jnp.max(scores, axis=-1, keepdims=True)
    ex = jnp.exp(scores - top)
    total = jnp.sum(ex, axis=-1, keepdims=True)
    lse = top + jnp.log(total)
    mix_rows = dot((ex / total).astype(BF), values).astype(BF)
    mix = jnp.concatenate([mix_rows[TOKENS * h : TOKENS * (h + 1)] for h in range(HEADS)], axis=1)
    mix_placed = dot(mix, put_mix).astype(BF)
    inner_out = jnp.concatenate([dot(mix_placed, raw_out[i][:, 640:768]) for i in (0, 1)], axis=1).astype(BF)
    side_out = mix_placed + dot(inner_out, put_inner_out).astype(BF)
    left, right = pick(is_first, *[dot(side_out, raw_out[i][:, :640]) for i in (0, 1)])
    after_att = hidden + jnp.concatenate([left, right[:, 128:]], axis=1)

    scale_two, n_two, u_two = norm_parts(after_att, gain_two_full)
    u_all = gather_tokens(u_two)

    raw_late, out_late, _ = after(u_two, raw, raw_out)
    b_left, b_right = pick(is_first, *[dot(take_b, raw_late[i][:, :768]).astype(BF) for i in (0, 1)])
    left, right = pick(is_first, *[dot(take_b_out, out_late[i][:, :640]).astype(BF) for i in (0, 1)])
    b_out = jnp.concatenate([left, right[:, 128:]], axis=1)
    left, right = pick(is_first, *[dot(put_inner_down, out_late[i][:, :640]).astype(BF) for i in (0, 1)])
    b_down = jnp.concatenate([left, right[:, 128:]], axis=1)
    a_gate, a_up = pick(is_first, *[dot(put_rows, out_late[i][:, 768:]).astype(BF) for i in (0, 1)])
    ff_all, _ = after((b_left, b_right, b_out, b_down, a_gate, a_up), ff_all)
    b_gate = ff_all[:, 144:160].reshape(256, 896)
    b_up = ff_all[:, 160:].reshape(256, 896)
    w_gate = (ff_all[:, :72].astype(F32) + dot(a_gate, b_gate).reshape(16, 72, 896)).astype(BF)
    w_up = (ff_all[:, 72:144].astype(F32) + dot(a_up, b_up).reshape(16, 72, 896)).astype(BF)
    w_gate, w_up = w_gate.reshape(1152, 896), w_up.reshape(1152, 896)
    down_parts, _ = after(w_up, down_parts)
    down_raw = placed(down_parts, "x", at_z, at_x).reshape(896, 1408)
    a_down = down_raw[:, 1152:]
    w_down = (down_raw[:, :1152].astype(F32) + dot(a_down, b_down)).astype(BF)

    gate = dot(u_all, w_gate)
    up = dot(u_all, w_up)
    act, act_pull = jax.vjp(lambda g, u: jax.nn.gelu(g, approximate=True) * u, gate, up)
    act = act.astype(BF)
    result = after_att + scatter_tokens(dot(act, w_down))

    valid = loss_token_mask[0].astype(F32)[:, None]
    error = result - teacher[0].astype(F32)
    loss_here = jnp.sum(valid * error * error)
    grad_result = 2.0 * 20480.0 / valid_count * valid * error

    g_all = gather_tokens(grad_result.astype(BF))
    g_act = dot_tr(g_all, w_down).astype(BF)
    g_gate, g_up = act_pull(g_act.astype(F32))
    g_gate, g_up = g_gate.astype(BF), g_up.astype(BF)
    g_u_part = dot_tr(g_gate, w_gate) + dot_tr(g_up, w_up)
    g_u_two = scatter_tokens(g_u_part)
    u_all, act, g_all, g_gate, g_up, _ = after(g_u_part, u_all, act, g_all, g_gate, g_up)
    gw_gate = dot_tl(u_all, g_gate).astype(BF)
    gb_gate = dot_tl(a_gate, gw_gate).astype(BF)
    gate_grads = jnp.concatenate([gw_gate.reshape(16, 72, 896), gb_gate.reshape(16, 16, 896)], axis=1)
    gate_first = leave(gate_grads.reshape(4, 4, 88, 896), "z", 0, at_z, at_x)
    gw_up = dot_tl(u_all, g_up).astype(BF)
    gb_up = dot_tl(a_up, gw_up).astype(BF)
    up_grads = jnp.concatenate([gw_up.reshape(16, 72, 896), gb_up.reshape(16, 16, 896)], axis=1)
    up_first = leave(up_grads.reshape(4, 4, 88, 896), "x", 1, at_z, at_x)
    gw_down = dot_tl(act, g_all).astype(BF)
    gb_down = dot_tl(a_down, gw_down).astype(BF)

    norm_two_back = norm_back(scale_two, n_two, gain_two_full, g_u_two)
    g_after = grad_result + norm_two_back
    g_after_b = g_after.astype(BF)
    once = jnp.where(jnp.arange(640) < 128, 0, 1).astype(BF)[None]
    g_half = pick(is_first, g_after_b[:, :640], g_after_b[:, 512:])
    g_once = pick(is_first, g_after_b[:, :640], g_after_b[:, 512:] * once)
    d_out = dot_tr(g_once[0], raw_out[0][:, :640]) + dot_tr(g_once[1], raw_out[1][:, :640])
    gi_out = dot_tr(d_out.astype(BF), put_inner_out).astype(BF)
    d_out = (
        d_out
        + dot_tr(gi_out[:, :128], raw_out[0][:, 640:768])
        + dot_tr(gi_out[:, 128:], raw_out[1][:, 640:768])
    )
    g_mix = dot_tr(d_out.astype(BF), put_mix).astype(BF)
    gate_first, _ = after(g_mix, gate_first)
    gate_line = add(gate_first).astype(BF)
    g_mix, _ = after(gate_line, g_mix)
    gate_second = leave(gate_line, "x", 0, at_z, at_x)
    g_rows = jnp.concatenate([g_mix[:, WIDTH * h : WIDTH * (h + 1)] for h in range(HEADS)], axis=0)
    scores_again = jnp.where(allowed, dot_tr(q_rows, keys) * score_scale, MASKED_SCORE)
    probs = jnp.where(allowed, jnp.exp(scores_again - lse), 0.0)
    g_probs = dot_tr(g_rows, values)
    g_scores = (probs * (g_probs - jnp.sum(probs * g_probs, axis=-1, keepdims=True))).astype(BF)
    g_keys = dot_tl(g_scores, q_rows) * score_scale
    g_values = dot_tl(probs.astype(BF), g_rows)
    g_kv = jnp.concatenate([g_keys, g_values], axis=1)
    n_mine = 8 * TOKENS
    up_first, g_kv = lax.optimization_barrier((up_first, g_kv))
    up_line = add(up_first).astype(BF)
    up_second = leave(up_line, "z", 0, at_z, at_x)
    g_away, _ = after(up_line, g_kv[n_mine:].astype(BF))
    g_kv_sum = g_kv[:n_mine] + other_core(g_away).astype(F32)
    g_kv_b = g_kv_sum.astype(BF)
    g_kv_b, gw_down = lax.optimization_barrier((g_kv_b, gw_down))
    down_first = leave(gw_down.reshape(4, 4, 56, 1152), "z", 1, at_z, at_x)
    g_parts = [shift(g_kv_b[320 * k : 320 * (k + 1)], "y", 4 - k) for k in (1, 2, 3)]
    g_scores, gb_down, _ = after(g_kv_b, g_scores, gb_down)
    g_pair = add([g_kv_sum[:320]] + list(g_parts))
    away = other_half(g_pair[160:].astype(BF))
    gate_second, up_second, _ = after(g_pair, gate_second, up_second)
    g_q_rows = dot(g_scores, keys) * score_scale
    g_q = [
        jnp.concatenate(
            [turn_back(g_q_rows[TOKENS * h : TOKENS * (h + 1)], cos, sin) for h in (2 * i, 2 * i + 1)],
            axis=1,
        ).astype(BF)
        for i in (0, 1)
    ]
    gate_sum, up_sum = add(gate_second).astype(BF), add(up_second).astype(BF)
    ga_part = jnp.concatenate(
        [dot_tr(gate_sum[:72], b_gate), dot_tr(up_sum[:72], b_up), jnp.zeros((72, 384), F32)], axis=1
    ).astype(BF)
    back_row = jnp.arange(256, dtype=jnp.int32)
    group, line = back_row // 32, back_row % 32
    take = jnp.where(
        line < 9,
        9 * group + line,
        jnp.where(
            line < 18,
            88 + 9 * group + line - 9,
            jnp.where(
                line < 22,
                72 + 88 * ((line - 18) // 2) + 2 * group + line % 2,
                jnp.where(line < 31, 176 + 9 * group + line - 22, -1),
            ),
        ),
    )
    leaving = dot(
        table(take, jnp.arange(248, dtype=jnp.int32)), jnp.concatenate([gate_sum, up_sum, ga_part], axis=0)
    ).astype(BF)
    slab = exchange(leaving.reshape(8, 32, 896), ("y", "c"))
    def of_chip(own, away):
        return (own.astype(F32) + other_core(away.astype(BF)).astype(F32)).astype(BF).reshape(64, 24, -1)

    def both_halves(owned):
        mine, away = pick(is_first, owned[:12], owned[12:])
        return pick(is_first, mine, other_core(away.astype(BF)).astype(F32))

    loss_high, loss_rest = split_in_two(loss_here)
    loss_mid, loss_low = split_in_two(loss_rest)
    lines = jnp.arange(16, dtype=jnp.int32)
    loss_rows = jnp.where(
        lines == 0,
        loss_high.astype(F32),
        jnp.where(lines == 1, loss_mid.astype(F32), jnp.where(lines == 2, loss_low, 0.0)),
    )
    more_side = (loss_rows[:, None] * (j == 11)[None, :]).astype(BF)
    more_grad = table(jnp.where(lines < 3, lines + 3 * core, -1), jnp.arange(512, dtype=jnp.int32))
    chip_q = of_chip(
        *[(dot_tl(sides[0], g_q[i]) + dot_tl(more_side, more_grad)).astype(BF) for i in (0, 1)]
    )
    side_out, _ = after(g_pair, side_out)
    left, right = pick(is_first, gb_down[:, :640], gb_down[:, 512:])
    chip_out = of_chip(
        dot_tl(side_out, g_half[0]) + dot_tl(put_inner_down, left),
        dot_tl(side_out, g_half[1]) + dot_tl(put_inner_down, right),
    )
    g_kv_own = g_pair[:160] + after(chip_q, away)[0].astype(F32)
    g_kv_own, down_first = lax.optimization_barrier((g_kv_own, down_first))
    down_second = leave(add(down_first).astype(BF), "x", 0, at_z, at_x)
    g_k = turn_back(g_kv_own[:, :256], cos, sin).astype(BF)
    g_v = g_kv_own[:, 256:].astype(BF)
    g_k = pick(is_first, g_k[:, :128], g_k[:, 128:])
    g_v = pick(is_first, g_v[:, :128], g_v[:, 128:])
    chip_kv = of_chip(
        *[
            jnp.concatenate([dot_tl(sides[1], g_k[i]).astype(BF), dot_tl(sides[2], g_v[i]).astype(BF)], axis=1)
            for i in (0, 1)
        ]
    )
    chip_sums = jnp.concatenate([chip_q, chip_kv, chip_out], axis=2)
    chip_sums, slab, g_q, g_k, g_v = lax.optimization_barrier((chip_sums, slab, g_q, g_k, g_v))
    parts = exchange(chip_sums, CHIPS)
    g_q, down_second = lax.optimization_barrier((g_q, down_second))

    d_one = None
    for i, (g, first, last) in enumerate(((g_q, 0, 512), (g_k, 512, 640), (g_v, 640, 768))):
        d = dot_tr(g[0], raw[0][:, first:last]) + dot_tr(g[1], raw[1][:, first:last])
        gi = dot_tr(d.astype(BF), put_inner).astype(BF)
        inner_at = 768 + 128 * i
        d = d + dot_tr(gi[:, :128], raw[0][:, inner_at : inner_at + 128])
        d = d + dot_tr(gi[:, 128:], raw[1][:, inner_at : inner_at + 128])
        d_one = d if d_one is None else d_one + d
    g_u_one = select_back(d_one, put_rows)
    grad_hidden = (g_after + norm_back(scale_one, n_one, gain_one_full, g_u_one)).astype(BF)

    narrow = dot_tr(slab.reshape(256, 896), wider).astype(BF).reshape(8, 32, 864)
    wide = jnp.concatenate([narrow[t, :22] for t in range(8)], axis=1)
    ga = jnp.sum(slab[:, 22:31, :512].astype(F32), axis=0)
    gw_down_own = lax.ppermute(
        add(down_second).astype(BF), EVERY, [(b, a) for a, b in down_route()]
    )[:54]
    ga_down_own = dot_tr(gw_down_own, b_down)

    def over_columns(pairs):
        return sum(jnp.sum(a.astype(F32) * b.astype(F32), axis=1) for a, b in pairs)

    gain_two_own = over_columns(
        ((wg, wide[:9]), (wu, wide[9:18]), (ag, ga[:, :256]), (au, ga[:, 256:]))
    ) / (1.0 + gain_two.astype(F32))

    owned = jnp.sum(parts.astype(F32), axis=0)
    loss_value = jnp.sum(owned[11, :6]) / (1152.0 * valid_count)
    left, right = both_halves(owned)
    own_out = jnp.concatenate([left[:, 768:], right[:, 896:]], axis=1)
    ga_out_own = dot_tr(own_out[:8].astype(BF), b_out)
    left_b, right_b = left[:9].astype(BF), right[:9].astype(BF)
    ga_own = [
        dot_tr(left_b[:, first:last], b_left[:, first:last])
        + dot_tr(right_b[:, first:last], b_right[:, first:last])
        for first, last in ((0, 512), (512, 640), (640, 768))
    ]

    def columns(first, last, rows):
        return jnp.concatenate([left[rows, first:last], right[rows, first:last]], axis=1)

    top_rows, low_rows = slice(0, 9), slice(9, 11)
    gw_own = [columns(0, 512, top_rows), columns(512, 640, top_rows), columns(640, 768, top_rows)]
    gain_one_own = over_columns(
        list(zip((wq, wk, wv), gw_own)) + list(zip((aq, ak, av), ga_own))
    ) / (1.0 + gain_one.astype(F32))

    return (
        result.astype(BF)[None],
        loss_value,
        grad_hidden[None],
        gain_one_own,
        *gw_own,
        own_out[:8],
        ga_own[0],
        columns(0, 512, low_rows),
        ga_own[1],
        columns(512, 640, low_rows),
        ga_own[2],
        columns(640, 768, low_rows),
        ga_out_own,
        own_out[8:10],
        gain_two_own,
        wide[:9].astype(F32),
        wide[9:18].astype(F32),
        gw_down_own.astype(F32),
        ga[:, :256],
        wide[18:20].astype(F32),
        ga[:, 256:],
        wide[20:22].astype(F32),
        ga_down_own,
        own_out[10:],
    )


def solution(mesh):
    mesh = Mesh(mesh.devices.reshape([SIZES[a] for a in EVERY]), EVERY)
    tree, seq = ("z", "xl"), ("xh", "y", "c")
    rows = P(EVERY, None)
    vector = P(EVERY)
    return jax.shard_map(
        on_device,
        mesh=mesh,
        in_specs=(
            P(tree, seq, None),
            P(tree, None),
            P(tree, None),
            P(tree, seq),
            P(tree, seq, None),
            vector,
        )
        + (rows,) * 12
        + (vector,)
        + (rows,) * 9,
        out_specs=(P(tree, seq, None), P(), P(tree, seq, None), vector)
        + (rows,) * 12
        + (vector,)
        + (rows,) * 9,
        check_vma=False,
    )
```
